32 devices in a mesh: group: 2 (over y), frame: 4 (over z), space: 2 (over x), head: 2 (over core).
Axes of the slice: x: 2, y: 2, z: 4, core: 2. Of those that a mesh axis runs over, the one named last changes fastest.
Arguments:
- queries: bfloat16 [8, 8, 48, 3072], P(('group', 'frame'), 'space', None, 'head'), parts along dimension 0, may hold values from -8 to 8
- keys: bfloat16 [8, 8, 48, 3072], P(('group', 'frame'), 'space', None, 'head'), parts along dimension 0, may hold values from -8 to 8
- values: bfloat16 [8, 8, 48, 3072], P(('group', 'frame'), 'space', None, 'head'), parts along dimension 0, may hold values from -6 to 6
- flags: int32 [4, 4], replicated, may hold values from 0 to 1, as said below
- widths: int32 [4], replicated, may hold values from 0 to 8, as said below
Outputs:
- attended: bfloat16 [8, 8, 48, 3072], P(('group', 'frame'), 'space', None, 'head'), parts along dimension 0
The draws below stay inside these ranges and needn't reach their ends.
There are 2 independent parts, one for each index of `group`. The reference program is written for one: setup_inputs(seed, part) draws one part's arguments, and reference() takes and returns one part's arrays. A program takes and returns all parts, laid end to end along the dimension named above; an argument that names none is the same for every part. Nothing has to cross between parts.
Inputs may be any that keep to these rules, and one draw needn't show every extreme that they name: flags[f, g] = 1 wherever |f - g| <= 1, and flags[0, 3] = flags[3, 0] = 0. widths[0] = 8, and widths never rise with the frame distance.
All inputs are finite; a program needn't handle non-finite values.
Results may differ from the reference program's by a relative error of at most 0.006.
Values may be sent and summed in bfloat16 or wider, within the bound.
No kernel may reach another device: no remote copies, remote signals or barrier semaphores. Data moves between devices by JAX's collectives and lax.ppermute only.
A program may use at most 128 MiB of HBM per device.

```python
import jax
import jax.numpy as jnp
from jax import lax

HEADS = 24
HEAD_DIM = 128
PC = 48
FRAMES = 4
ROWS = 8


def draw_queries(key, part):
    shape = (FRAMES, ROWS, PC, HEADS, HEAD_DIM)
    base = jax.random.normal(jax.random.fold_in(key, 11), shape, jnp.float32)
    result = jnp.clip(1.5 * base, -8.0, 8.0)
    return result.reshape(FRAMES, ROWS, PC, HEADS * HEAD_DIM).astype(jnp.bfloat16)


def draw_keys(key, part):
    shape = (FRAMES, ROWS, PC, HEADS, HEAD_DIM)
    base = jax.random.normal(jax.random.fold_in(key, 21), shape, jnp.float32)
    result = jnp.clip(base, -6.0, 6.0)
    return result.reshape(FRAMES, ROWS, PC, HEADS * HEAD_DIM).astype(jnp.bfloat16)


def draw_flags(key, part):
    levels = jax.random.randint(jax.random.fold_in(key, 31), (FRAMES, FRAMES), 0, 16)
    frame_ids = jnp.arange(FRAMES, dtype=jnp.int32)
    distance = jnp.abs(frame_ids[:, None] - frame_ids[None, :])
    base_flags = (levels * distance < 24).astype(jnp.int32)
    return jnp.where(distance == FRAMES - 1, 0, base_flags).astype(jnp.int32)


def draw_widths(key, part):
    distance = jnp.arange(FRAMES, dtype=jnp.int32)
    first_band = jax.random.randint(jax.random.fold_in(key, 41), (), 1, 3)
    band_count = jnp.zeros((FRAMES,), jnp.int32)
    for level in range(8):
        band_count = band_count + (distance >= first_band * 2 ** level).astype(jnp.int32)
    extra_drop = jax.random.randint(jax.random.fold_in(key, 42), (FRAMES,), 0, 2)
    extra_drop = jnp.where(distance == 0, 0, extra_drop)
    shifts = jnp.minimum(band_count + extra_drop, 30)
    raw_widths = jnp.right_shift(jnp.full((FRAMES,), ROWS, jnp.int32), shifts)
    return lax.cummin(raw_widths, axis=0).astype(jnp.int32)


def block_scale(stream_key, extent, pieces, least, largest):
    def one(dim, parts):
        heights = jax.random.uniform(jax.random.fold_in(jax.random.fold_in(stream_key, 6), dim), (parts,), jnp.float32, least / len(pieces), largest / len(pieces))
        return jnp.repeat(jnp.exp(heights), extent[dim] // parts).reshape((-1,) + (1,) * (len(extent) - dim - 1))

    factor_of = one(*pieces[0])
    for cut in pieces[1:]:
        factor_of = factor_of * one(*cut)
    return factor_of


def bell_draw(stream_key, dims, spread, reach, split=(), kind=jnp.bfloat16):
    values = jax.random.normal(stream_key, dims, jnp.float32) * spread
    if len(split) > 0:
        values = block_scale(stream_key, dims, split, -0.22, 0.18) * values
    return jnp.clip(values, min=-reach, max=reach).astype(kind)


def setup_inputs(seed: int = 0, part: int = 0) -> dict:
    arg_keys = jax.random.split(jax.random.key(seed), 6)
    part_keys = jax.random.split(jax.random.fold_in(arg_keys[5], part), 6)
    return {
        "queries": draw_queries(jax.random.fold_in(jax.random.fold_in(arg_keys[5], part), 71), part),
        "keys": draw_keys(jax.random.fold_in(jax.random.fold_in(arg_keys[5], part), 71), part),
        "values": bell_draw(part_keys[2], (FRAMES, ROWS, PC, HEADS * HEAD_DIM), 1.0, 6.0, ((0, 4), (1, 2), (3, 2))),
        "flags": draw_flags(jax.random.fold_in(arg_keys[5], 71), part),
        "widths": draw_widths(jax.random.fold_in(arg_keys[5], 71), part),
    }


def reference(queries, keys, values, flags, widths):
    frame_count, row_count, column_count, features = queries.shape
    head_count = features // HEAD_DIM
    per_frame = row_count * column_count
    scale = 1.0 / (HEAD_DIM ** 0.5)
    query_tok = queries.reshape(frame_count, per_frame, head_count, HEAD_DIM)
    key_tok = keys.reshape(frame_count * per_frame, head_count, HEAD_DIM)
    value_tok = values.reshape(frame_count * per_frame, head_count, HEAD_DIM)
    token_ids = jnp.arange(frame_count * per_frame, dtype=jnp.int32)
    key_frame = token_ids // per_frame
    key_row = (token_ids // column_count) % row_count
    query_row = jnp.arange(per_frame, dtype=jnp.int32) // column_count

    def frame_out(query_frame):
        frame_query = lax.dynamic_index_in_dim(query_tok, query_frame, 0, False)
        flag_row = lax.dynamic_index_in_dim(flags, query_frame, 0, False)
        reach_rows = widths[jnp.abs(query_frame - key_frame)]
        allowed = (flag_row[key_frame] > 0)[None, :] & (
            jnp.abs(query_row[:, None] - key_row[None, :]) <= reach_rows[None, :])

        def head_out(head):
            head_query = lax.dynamic_index_in_dim(frame_query, head, 1, False)
            head_key = lax.dynamic_index_in_dim(key_tok, head, 1, False)
            head_value = lax.dynamic_index_in_dim(value_tok, head, 1, False)
            scores = jnp.dot(head_query, head_key.T, preferred_element_type=jnp.float32) * scale
            scores = jnp.where(allowed, scores, -jnp.inf)
            top = jnp.max(scores, axis=1, keepdims=True)
            weights = jnp.where(allowed, jnp.exp(scores - top), 0.0)
            total = jnp.sum(weights, axis=1, keepdims=True)
            blended = jnp.dot(weights.astype(jnp.bfloat16), head_value, preferred_element_type=jnp.float32)
            return blended / total

        outputs = lax.map(head_out, jnp.arange(head_count, dtype=jnp.int32))
        return jnp.transpose(outputs, (1, 0, 2)).reshape(per_frame, features)

    result = lax.map(frame_out, jnp.arange(frame_count, dtype=jnp.int32))
    return result.reshape(queries.shape).astype(jnp.bfloat16)
```

```python
import functools
import math

import jax
import jax.numpy as jnp
from jax import lax
from jax.experimental import pallas as pl
from jax.experimental.pallas import tpu as pltpu
from jax.sharding import PartitionSpec as P

HEAD_DIM = 128
NEG_FILL = -1e30
VMEM_LIMIT = 40 * 1024 * 1024


def pack_kernel(spaces, place_ref, q_ref, k_ref, v_ref, *rest):
    outs, sems = rest[:-1], rest[-1]
    width = outs[0].shape[-1]
    here = place_ref[1]
    copies = []
    for offset in range(spaces):
        column = pl.multiple_of(lax.rem(here + offset, spaces) * width, HEAD_DIM)
        sources = [k_ref, v_ref]
        targets = [outs[offset].at[0], outs[offset].at[1]]
        if offset > 0:
            sources.append(q_ref)
            targets.append(outs[spaces + offset - 1])
        for source, target in zip(sources, targets):
            copy = pltpu.make_async_copy(
                source.at[:, pl.ds(column, width)], target, sems.at[len(copies)]
            )
            copy.start()
            copies.append(copy)
    for copy in copies:
        copy.wait()


def pack(place, q, k, v, spaces):
    tokens, features = q.shape
    width = features // spaces
    shapes = [jax.ShapeDtypeStruct((2, tokens, width), q.dtype)] * spaces
    shapes += [jax.ShapeDtypeStruct((tokens, width), q.dtype)] * (spaces - 1)
    return pl.pallas_call(
        functools.partial(pack_kernel, spaces),
        grid_spec=pltpu.PrefetchScalarGridSpec(
            num_scalar_prefetch=1,
            grid=(1,),
            in_specs=[pl.BlockSpec(memory_space=pl.ANY)] * 3,
            out_specs=[pl.BlockSpec(memory_space=pl.ANY)] * len(shapes),
            scratch_shapes=[pltpu.SemaphoreType.DMA((3 * spaces - 1,))],
        ),
        out_shape=shapes,
        name="pack",
    )(place, q, k, v)


def attend_kernel(
    spaces, frames, columns, row_band, pieces, fresh, final,
    place_ref, flags_ref, widths_ref, *refs,
):
    refs = list(refs)
    queries = [refs.pop(0) for unused in range(spaces)]
    keyvals = [refs.pop(0) for unused in pieces]
    state_in = None if fresh else (refs.pop(0), refs.pop(0))
    outs = [refs.pop(0) for unused in range(spaces if final else 2)]
    top_ref, total_ref, acc_ref = refs
    tokens = queries[0].shape[0]
    frame_now, space_now = place_ref[0], place_ref[1]
    scale = math.log2(math.e) / math.sqrt(HEAD_DIM)

    def band(offset):
        return lax.rem(space_now - offset + spaces, spaces)

    query = jnp.concatenate([ref[...] for ref in queries], axis=0)
    count = spaces * tokens

    def scores_of(ref):
        return scale * lax.dot_general(
            query, ref[0], (((1,), (1,)), ((), ())), preferred_element_type=jnp.float32
        )

    def weighted(weights, ref):
        return jnp.dot(
            weights.astype(jnp.bfloat16), ref[1], preferred_element_type=jnp.float32
        )

    own = [n for n, (distance, offset) in enumerate(pieces) if distance == 0]
    if fresh:
        parts = [scores_of(keyvals[n]) for n in own]
        top = functools.reduce(
            jnp.maximum, [jnp.max(part, axis=1, keepdims=True) for part in parts]
        )
        weights = [jnp.exp2(part - top) for part in parts]
        top_ref[...] = top
        total_ref[...] = sum(jnp.sum(w, axis=1, keepdims=True) for w in weights)
        acc_ref[...] = sum(weighted(w, keyvals[n]) for w, n in zip(weights, own))
    else:
        acc_ref[...] = state_in[0][0]
        top_ref[...] = state_in[1][0, :, 0:1]
        total_ref[...] = state_in[1][0, :, 64:65]

    local = lax.broadcasted_iota(jnp.int32, (count, 1), 0)
    query_row = jnp.zeros((count, 1), jnp.int32)
    for offset in range(spaces):
        inside = (local >= offset * tokens) & (local < (offset + 1) * tokens)
        row = (local - offset * tokens) // columns + band(offset) * row_band
        query_row = jnp.where(inside, row, query_row)
    key_local = lax.broadcasted_iota(jnp.int32, (1, tokens), 1) // columns

    for n, (distance, offset) in enumerate(pieces):
        if distance == 0:
            continue
        key_frame = frame_now + distance
        known = (key_frame >= 0) & (key_frame < frames)
        safe = jnp.clip(key_frame, 0, frames - 1)
        reach = widths_ref[abs(distance)]
        asked = known & (flags_ref[frame_now, safe] > 0)

        @pl.when(asked)
        def _(n=n, offset=offset, reach=reach):
            key_row = key_local + band(offset) * row_band
            scores = scores_of(keyvals[n])
            scores = jnp.where(jnp.abs(query_row - key_row) <= reach, scores, NEG_FILL)
            old = top_ref[...]
            new = jnp.maximum(old, jnp.max(scores, axis=1, keepdims=True))
            weights = jnp.exp2(scores - new)
            fade = jnp.exp2(old - new)
            top_ref[...] = new
            total_ref[...] = total_ref[...] * fade + jnp.sum(weights, axis=1, keepdims=True)
            acc_ref[...] = acc_ref[...] * fade + weighted(weights, keyvals[n])

    if final:
        for offset in range(spaces):
            rows = pl.ds(offset * tokens, tokens)
            outs[offset][...] = (acc_ref[rows, :] / total_ref[rows, :]).astype(outs[offset].dtype)
    else:
        outs[0][0] = acc_ref[...]
        lane = lax.broadcasted_iota(jnp.int32, (count, HEAD_DIM), 1)
        outs[1][0] = jnp.where(lane < 64, top_ref[...], total_ref[...])


def attend(scalars, queries, keyvals, pieces, state, final, sizes):
    spaces, frames, columns, row_band, features = sizes
    tokens = queries[0].shape[0]
    width = features // spaces
    heads = width // HEAD_DIM
    count = spaces * tokens
    own_block = pl.BlockSpec((tokens, HEAD_DIM), lambda h, place, *_: (0, place[1] * heads + h))
    block = pl.BlockSpec((tokens, HEAD_DIM), lambda h, *_: (0, h))
    pair = pl.BlockSpec((2, tokens, HEAD_DIM), lambda h, *_: (0, 0, h))
    kept = pl.BlockSpec((1, count, HEAD_DIM), lambda h, *_: (h, 0, 0))
    in_specs = [own_block] + [block] * (spaces - 1) + [pair] * len(pieces)
    operands = list(queries) + list(keyvals)
    if state is not None:
        in_specs += [kept, kept]
        operands += list(state)
    if final:
        out_specs = [own_block] + [block] * (spaces - 1)
        out_shape = [jax.ShapeDtypeStruct((tokens, features), jnp.bfloat16)]
        out_shape += [jax.ShapeDtypeStruct((tokens, width), jnp.bfloat16)] * (spaces - 1)
    else:
        out_specs = [kept, kept]
        out_shape = [jax.ShapeDtypeStruct((heads, count, HEAD_DIM), jnp.float32)] * 2
    pairs = heads * count * tokens * len(pieces)
    return pl.pallas_call(
        functools.partial(
            attend_kernel, spaces, frames, columns, row_band, tuple(pieces), state is None, final
        ),
        grid_spec=pltpu.PrefetchScalarGridSpec(
            num_scalar_prefetch=3,
            grid=(heads,),
            in_specs=in_specs,
            out_specs=out_specs,
            scratch_shapes=[
                pltpu.VMEM((count, 1), jnp.float32),
                pltpu.VMEM((count, 1), jnp.float32),
                pltpu.VMEM((count, HEAD_DIM), jnp.float32),
            ],
        ),
        out_shape=out_shape,
        compiler_params=pltpu.CompilerParams(vmem_limit_bytes=VMEM_LIMIT),
        cost_estimate=pl.CostEstimate(
            flops=4 * pairs * HEAD_DIM,
            bytes_accessed=len(pieces) * 4 * tokens * width,
            transcendentals=pairs,
        ),
        name="attend_final" if final else "attend",
    )(*scalars, *operands)


def put_kernel(place_ref, piece_ref, whole_ref, out_ref):
    out_ref[...] = piece_ref[...]


def put(place, piece, whole, offset, spaces):
    tokens, width = piece.shape
    return pl.pallas_call(
        put_kernel,
        grid_spec=pltpu.PrefetchScalarGridSpec(
            num_scalar_prefetch=1,
            grid=(1,),
            in_specs=[
                pl.BlockSpec((tokens, width), lambda i, place: (0, 0)),
                pl.BlockSpec(memory_space=pl.ANY),
            ],
            out_specs=pl.BlockSpec(
                (tokens, width), lambda i, place: (0, lax.rem(place[1] + offset, spaces))
            ),
        ),
        out_shape=jax.ShapeDtypeStruct(whole.shape, whole.dtype),
        input_output_aliases={2: 0},
        name="put",
    )(place, piece, whole)


def shards(spaces, frames, queries, keys, values, flags, widths):
    unused, row_band, columns, features = queries.shape
    tokens = row_band * columns
    place = jnp.stack([lax.axis_index("frame"), lax.axis_index("space")]).astype(jnp.int32)
    scalars = (place, flags, widths)
    sizes = (spaces, frames, columns, row_band, features)
    q, k, v = (x.reshape(tokens, features) for x in (queries, keys, values))
    packed = pack(place, q, k, v, spaces)

    def along_space(x, offset):
        return lax.ppermute(x, "space", [(s, (s + offset) % spaces) for s in range(spaces)])

    def along_frame(x, step):
        return lax.ppermute(
            x, "frame", [(f, f + step) for f in range(frames) if 0 <= f + step < frames]
        )

    offsets = range(1, spaces)
    own = [packed[0]] + [along_space(packed[offset], offset) for offset in offsets]
    query_parts = [q] + [along_space(packed[spaces + offset - 1], offset) for offset in offsets]

    waves = [[(0, offset, x) for offset, x in enumerate(own)]]
    from_left, from_right = own, own
    for distance in range(1, frames - 1):
        from_left = [along_frame(x, 1) for x in from_left]
        from_right = [along_frame(x, -1) for x in from_right]
        wave = []
        for offset in range(spaces):
            wave.append((-distance, offset, from_left[offset]))
            wave.append((distance, offset, from_right[offset]))
        waves.append(wave)
    if len(waves) > 1:
        waves = [waves[0] + waves[1]] + waves[2:]

    state = None
    for n, wave in enumerate(waves):
        state = attend(
            scalars, query_parts, [x for d, o, x in wave], [(d, o) for d, o, x in wave],
            state, n == len(waves) - 1, sizes,
        )

    result = state[0]
    for offset in offsets:
        back = along_space(state[offset], -offset)
        result = put(place, back, result, offset, spaces)
    return result.reshape(queries.shape)


def solution(mesh):
    placed = P(("group", "frame"), "space", None, "head")
    return jax.shard_map(
        functools.partial(shards, mesh.shape["space"], mesh.shape["frame"]),
        mesh=mesh,
        in_specs=(placed, placed, placed, P(), P()),
        out_specs=placed,
        check_vma=False,
    )
```

```python
import functools
import math

import jax
import jax.numpy as jnp
from jax import lax
from jax.experimental import pallas as pl
from jax.experimental.pallas import tpu as pltpu
from jax.sharding import PartitionSpec as P

HEAD_DIM = 128
NEG_FILL = -1e30
VMEM_LIMIT = 40 * 1024 * 1024
NT = (((1,), (1,)), ((), ()))
TN = (((0,), (0,)), ((), ()))


def pack_kernel(spaces, place_ref, q_ref, k_ref, v_ref, *outs):
    width = outs[0].shape[-1]
    here = place_ref[1]
    for offset in range(spaces):
        column = pl.multiple_of(lax.rem(here + offset, spaces) * width, HEAD_DIM)
        outs[offset][0] = k_ref[:, pl.ds(column, width)]
        outs[offset][1] = v_ref[:, pl.ds(column, width)]
        if offset > 0:
            outs[spaces + offset - 1][...] = q_ref[:, pl.ds(column, width)]


def pack(place, q, k, v, spaces):
    tokens, features = q.shape
    width = features // spaces
    shapes = [jax.ShapeDtypeStruct((2, tokens, width), q.dtype)] * spaces
    shapes += [jax.ShapeDtypeStruct((tokens, width), q.dtype)] * (spaces - 1)
    return pl.pallas_call(
        functools.partial(pack_kernel, spaces),
        in_specs=[pl.BlockSpec(memory_space=pltpu.SMEM)]
        + [pl.BlockSpec(memory_space=pltpu.VMEM)] * 3,
        out_specs=[pl.BlockSpec(memory_space=pltpu.VMEM)] * len(shapes),
        out_shape=shapes,
        compiler_params=pltpu.CompilerParams(vmem_limit_bytes=VMEM_LIMIT),
        name="pack",
    )(place, q, k, v)


def attend_kernel(
    spaces, frames, columns, row_band, groups, fresh, final,
    place_ref, flags_ref, widths_ref, *refs,
):
    refs = list(refs)
    queries = [refs.pop(0) for unused in range(spaces)]
    keyvals = [[refs.pop(0) for unused in range(spaces)] for unused in groups]
    state_in = None if fresh else (refs.pop(0), refs.pop(0))
    outs = [refs.pop(0) for unused in range(spaces if final else 2)]
    query_ref, key_ref, acc_ref, stat_ref = refs
    tokens = queries[0].shape[0]
    frame_now, space_now = place_ref[0], place_ref[1]
    scale = math.log2(math.e) / math.sqrt(HEAD_DIM)

    def first_row(offset):
        return lax.rem(space_now - offset + spaces, spaces) * row_band

    def asked_of(group):
        slot, hops = group
        side = 1 - 2 * lax.rem(frame_now + slot, 2)
        key_frame = frame_now + side * hops
        safe = jnp.clip(key_frame, 0, frames - 1)
        known = (key_frame >= 0) & (key_frame < frames)
        return known & (flags_ref[frame_now, safe] > 0)

    @pl.when(pl.program_id(0) == 0)
    def _():
        token = lax.broadcasted_iota(jnp.int32, (tokens, HEAD_DIM), 0)
        row = lax.broadcasted_iota(jnp.int32, (tokens, HEAD_DIM), 1)
        for offset in range(spaces):
            rows = pl.ds(offset * tokens, tokens)
            start = (row - first_row(offset)) * columns
            hit = (token >= start) & (token < start + columns)
            query_ref[rows, HEAD_DIM:] = jnp.where(hit, 1.0, 0.0).astype(query_ref.dtype)
            for n, group in enumerate(groups):
                if group[1] > 0:
                    reach = widths_ref[group[1]] * columns
                    near = (token >= start - reach) & (token < start + columns + reach)
                    key_ref[n, rows, HEAD_DIM:] = jnp.where(near, 0.0, NEG_FILL).astype(
                        key_ref.dtype
                    )

    for offset in range(spaces):
        query_ref[pl.ds(offset * tokens, tokens), :HEAD_DIM] = queries[offset][...]

    def step(scores, values, old):
        top = jnp.max(scores, axis=0, keepdims=True) * scale
        if old is not None:
            top = jnp.maximum(top, old[0])
        weights = jnp.exp2(scores * scale - top)
        total = jnp.sum(weights, axis=0, keepdims=True)
        acc = lax.dot_general(
            values, weights.astype(jnp.bfloat16), TN, preferred_element_type=jnp.float32
        )
        if old is not None:
            fade = jnp.exp2(old[0] - top)
            total = total + old[1] * fade
            acc = acc + acc_ref[...] * fade
        stat_ref[0:1, :] = top
        stat_ref[1:2, :] = total
        acc_ref[...] = acc

    if not fresh:
        acc_ref[...] = state_in[0][0]
        stat_ref[...] = state_in[1][0]

    for n, group in enumerate(groups):
        values = lambda n=n: jnp.concatenate([ref[1] for ref in keyvals[n]], axis=0)
        if group[1] == 0:
            keys = jnp.concatenate([ref[0] for ref in keyvals[n]], axis=0)
            scores = lax.dot_general(
                keys, query_ref[:, :HEAD_DIM], NT, preferred_element_type=jnp.float32
            )
            step(scores, values(), None)
            continue

        @pl.when(asked_of(group))
        def _(n=n, values=values):
            for offset in range(spaces):
                key_ref[n, pl.ds(offset * tokens, tokens), :HEAD_DIM] = keyvals[n][offset][0]
            scores = lax.dot_general(
                key_ref[n], query_ref[...], NT, preferred_element_type=jnp.float32
            )
            step(scores, values(), (stat_ref[0:1, :], stat_ref[1:2, :]))

    if final:
        result = jnp.transpose(acc_ref[...] / stat_ref[1:2, :])
        for offset in range(spaces):
            part = result[offset * tokens : (offset + 1) * tokens]
            outs[offset][...] = part.astype(outs[offset].dtype)
    else:
        outs[0][0] = acc_ref[...]
        outs[1][0] = stat_ref[...]


def attend(scalars, queries, groups, state, final, sizes):
    spaces, frames, columns, row_band, features = sizes
    tokens = queries[0].shape[0]
    width = features // spaces
    heads = width // HEAD_DIM
    count = spaces * tokens
    own_block = pl.BlockSpec((tokens, HEAD_DIM), lambda h, place, *_: (0, place[1] * heads + h))
    block = pl.BlockSpec((tokens, HEAD_DIM), lambda h, *_: (0, h))
    pair = pl.BlockSpec((2, tokens, HEAD_DIM), lambda h, *_: (0, 0, h))
    kept = [
        pl.BlockSpec((1, HEAD_DIM, count), lambda h, *_: (h, 0, 0)),
        pl.BlockSpec((1, 8, count), lambda h, *_: (h, 0, 0)),
    ]
    in_specs = [own_block] + [block] * (spaces - 1) + [pair] * (spaces * len(groups))
    operands = list(queries) + [x for slot, hops, pieces in groups for x in pieces]
    if state is not None:
        in_specs += kept
        operands += list(state)
    if final:
        out_specs = [own_block] + [block] * (spaces - 1)
        out_shape = [jax.ShapeDtypeStruct((tokens, features), jnp.bfloat16)]
        out_shape += [jax.ShapeDtypeStruct((tokens, width), jnp.bfloat16)] * (spaces - 1)
    else:
        out_specs = kept
        out_shape = [
            jax.ShapeDtypeStruct((heads, HEAD_DIM, count), jnp.float32),
            jax.ShapeDtypeStruct((heads, 8, count), jnp.float32),
        ]
    pairs = heads * count * count * len(groups)
    return pl.pallas_call(
        functools.partial(
            attend_kernel, spaces, frames, columns, row_band,
            tuple((slot, hops) for slot, hops, pieces in groups), state is None, final,
        ),
        grid_spec=pltpu.PrefetchScalarGridSpec(
            num_scalar_prefetch=3,
            grid=(heads,),
            in_specs=in_specs,
            out_specs=out_specs,
            scratch_shapes=[
                pltpu.VMEM((count, 2 * HEAD_DIM), jnp.bfloat16),
                pltpu.VMEM((len(groups), count, 2 * HEAD_DIM), jnp.bfloat16),
                pltpu.VMEM((HEAD_DIM, count), jnp.float32),
                pltpu.VMEM((8, count), jnp.float32),
            ],
        ),
        out_shape=out_shape,
        compiler_params=pltpu.CompilerParams(vmem_limit_bytes=VMEM_LIMIT),
        cost_estimate=pl.CostEstimate(
            flops=4 * pairs * HEAD_DIM,
            bytes_accessed=len(groups) * 4 * count * width,
            transcendentals=pairs,
        ),
        name="attend_final" if final else "attend",
    )(*scalars, *operands)


def put_kernel(spaces, offset, place_ref, piece_ref, whole_ref, out_ref, sem):
    width = piece_ref.shape[-1]
    column = pl.multiple_of(lax.rem(place_ref[1] + offset, spaces) * width, HEAD_DIM)
    copy = pltpu.make_async_copy(piece_ref, out_ref.at[:, pl.ds(column, width)], sem)
    copy.start()
    copy.wait()


def put(place, piece, whole, offset, spaces):
    return pl.pallas_call(
        functools.partial(put_kernel, spaces, offset),
        in_specs=[
            pl.BlockSpec(memory_space=pltpu.SMEM),
            pl.BlockSpec(memory_space=pltpu.VMEM),
            pl.BlockSpec(memory_space=pl.ANY),
        ],
        out_specs=pl.BlockSpec(memory_space=pl.ANY),
        out_shape=jax.ShapeDtypeStruct(whole.shape, whole.dtype),
        scratch_shapes=[pltpu.SemaphoreType.DMA],
        input_output_aliases={2: 0},
        name="put",
    )(place, piece, whole)


def shards(spaces, frames, queries, keys, values, flags, widths):
    unused, row_band, columns, features = queries.shape
    tokens = row_band * columns
    place = jnp.stack([lax.axis_index("frame"), lax.axis_index("space")]).astype(jnp.int32)
    scalars = (place, flags, widths)
    sizes = (spaces, frames, columns, row_band, features)
    q, k, v = (x.reshape(tokens, features) for x in (queries, keys, values))
    packed = pack(place, q, k, v, spaces)

    def along_space(x, offset):
        return lax.ppermute(x, "space", [(s, (s + offset) % spaces) for s in range(spaces)])

    def swap(x, slot, hops):
        pairs = []
        for f in range(frames):
            side = 1 if (f + slot) % 2 == 0 else -1
            source = f - side * (hops - 1)
            if 0 <= f + side < frames and 0 <= source < frames:
                pairs.append((f, f + side))
        return lax.ppermute(x, "frame", pairs)

    offsets = range(1, spaces)
    own = [packed[0]] + [along_space(packed[offset], offset) for offset in offsets]
    query_parts = [q] + [along_space(packed[spaces + offset - 1], offset) for offset in offsets]

    waves = [[(0, 0, own)]]
    carried = [own, own]
    for hops in range(1, frames - 1):
        carried = [
            [swap(x, 0, hops) for x in carried[1]],
            [swap(x, 1, hops) for x in carried[0]],
        ]
        waves.append([(0, hops, carried[0]), (1, hops, carried[1])])

    state = None
    for n, wave in enumerate(waves):
        state = attend(scalars, query_parts, wave, state, n == len(waves) - 1, sizes)

    result = state[0]
    for offset in offsets:
        back = along_space(state[offset], -offset)
        result = put(place, back, result, offset, spaces)
    return result.reshape(queries.shape)


def solution(mesh):
    placed = P(("group", "frame"), "space", None, "head")
    return jax.shard_map(
        functools.partial(shards, mesh.shape["space"], mesh.shape["frame"]),
        mesh=mesh,
        in_specs=(placed, placed, placed, P(), P()),
        out_specs=placed,
        check_vma=False,
    )
```

```python
import functools
import math

import jax
import jax.numpy as jnp
from jax import lax
from jax.experimental import pallas as pl
from jax.experimental.pallas import tpu as pltpu
from jax.sharding import PartitionSpec as P

HEAD_DIM = 128
NEG_FILL = -1e30
VMEM_LIMIT = 40 * 1024 * 1024
NT = (((1,), (1,)), ((), ()))
TN = (((0,), (0,)), ((), ()))


def pack_kernel(spaces, jobs, place_ref, *refs):
    sems = refs[-1]
    here = place_ref[1]
    copies = []
    for n, (source, offset, first, width, target, row) in enumerate(jobs):
        share = refs[source].shape[-1] // spaces
        column = pl.multiple_of(lax.rem(here + offset, spaces) * share + first, HEAD_DIM)
        out = refs[target] if row is None else refs[target].at[row]
        copy = pltpu.make_async_copy(refs[source].at[:, pl.ds(column, width)], out, sems.at[n])
        copy.start()
        copies.append(copy)
    for copy in copies:
        copy.wait()


def pack(place, sources, blocks, after, spaces):
    tokens = sources[0].shape[0]
    several = len(sources) > 1
    jobs, shapes = [], []
    first_out = len(sources) + len(after)
    for n, (offset, first, width) in enumerate(blocks):
        lead = (len(sources),) if several else ()
        shapes.append(jax.ShapeDtypeStruct(lead + (tokens, width), sources[0].dtype))
        for row in range(len(sources)):
            jobs.append((row, offset, first, width, first_out + n, row if several else None))
    return pl.pallas_call(
        functools.partial(pack_kernel, spaces, tuple(jobs)),
        in_specs=[pl.BlockSpec(memory_space=pltpu.SMEM)]
        + [pl.BlockSpec(memory_space=pltpu.HBM)] * len(sources)
        + [pl.BlockSpec(memory_space=pl.ANY)] * len(after),
        out_specs=[pl.BlockSpec(memory_space=pltpu.VMEM)] * len(shapes),
        out_shape=shapes,
        scratch_shapes=[pltpu.SemaphoreType.DMA((len(jobs),))],
        compiler_params=pltpu.CompilerParams(vmem_limit_bytes=VMEM_LIMIT),
        name="pack",
    )(place, *sources, *after)


def tie(array, after):
    return pl.pallas_call(
        lambda array_ref, after_ref, out_ref: None,
        in_specs=[pl.BlockSpec(memory_space=pl.ANY)] * 2,
        out_specs=pl.BlockSpec(memory_space=pl.ANY),
        out_shape=jax.ShapeDtypeStruct(array.shape, array.dtype),
        input_output_aliases={0: 0},
        name="tie",
    )(array, after)


def attend_kernel(
    spaces, frames, columns, row_band, together, groups, fresh, final, kept_whole,
    place_ref, flags_ref, widths_ref, *refs,
):
    refs = list(refs)
    queries = [refs.pop(0) for unused in range(spaces)]
    keyvals = [[refs.pop(0) for unused in range(spaces)] for unused in groups]
    state_in = None if fresh else (refs.pop(0), refs.pop(0))
    if kept_whole:
        refs.pop(0)
    outs = [refs.pop(0) for unused in range(spaces if final else 2)]
    query_ref, key_ref, acc_ref, stat_ref = refs
    tokens = queries[0].shape[0]
    frame_now, space_now = place_ref[0], place_ref[1]
    scale = math.log2(math.e) / math.sqrt(HEAD_DIM)

    def first_row(offset):
        return lax.rem(space_now - offset + spaces, spaces) * row_band

    def asked_of(group):
        slot, hops = group
        side = 1 - 2 * lax.rem(frame_now + slot, 2)
        key_frame = frame_now + side * hops
        safe = jnp.clip(key_frame, 0, frames - 1)
        known = (key_frame >= 0) & (key_frame < frames)
        return known & (flags_ref[frame_now, safe] > 0)

    @pl.when(pl.program_id(0) == 0)
    def _():
        token = lax.broadcasted_iota(jnp.int32, (tokens, HEAD_DIM), 0)
        row = lax.broadcasted_iota(jnp.int32, (tokens, HEAD_DIM), 1)
        for offset in range(spaces):
            rows = pl.ds(offset * tokens, tokens)
            start = (row - first_row(offset)) * columns
            hit = (token >= start) & (token < start + columns)
            mark = jnp.where(hit, 1.0, 0.0).astype(query_ref.dtype)
            for h in range(together):
                query_ref[h, rows, HEAD_DIM:] = mark
            for n, group in enumerate(groups):
                if group[1] > 0:
                    reach = widths_ref[group[1]] * columns
                    near = (token >= start - reach) & (token < start + columns + reach)
                    fill = jnp.where(near, 0.0, NEG_FILL).astype(key_ref.dtype)
                    for h in range(together):
                        key_ref[n, h, rows, HEAD_DIM:] = fill

    def lanes(h):
        return pl.ds(h * HEAD_DIM, HEAD_DIM)

    for h in range(together):
        for offset in range(spaces):
            rows = pl.ds(offset * tokens, tokens)
            query_ref[h, rows, :HEAD_DIM] = queries[offset][:, lanes(h)]

    def step(h, scores, refs, old):
        top = jnp.max(scores, axis=0, keepdims=True) * scale
        if old:
            before = stat_ref[h, 0:1, :]
            top = jnp.maximum(top, before)
        weights = jnp.exp2(scores * scale - top)
        total = jnp.sum(weights, axis=0, keepdims=True)
        values = jnp.concatenate([ref[1, :, lanes(h)] for ref in refs], axis=0)
        acc = lax.dot_general(
            values, weights.astype(jnp.bfloat16), TN, preferred_element_type=jnp.float32
        )
        if old:
            fade = jnp.exp2(before - top)
            total = total + stat_ref[h, 1:2, :] * fade
            acc = acc + acc_ref[h] * fade
        stat_ref[h, 0:1, :] = top
        stat_ref[h, 1:2, :] = total
        acc_ref[h] = acc

    if not fresh:
        acc_ref[...] = state_in[0][...]
        stat_ref[...] = state_in[1][...]

    for n, group in enumerate(groups):
        if group[1] == 0:
            scores = []
            for h in range(together):
                keys = jnp.concatenate([ref[0, :, lanes(h)] for ref in keyvals[n]], axis=0)
                scores.append(
                    lax.dot_general(
                        keys, query_ref[h, :, :HEAD_DIM], NT, preferred_element_type=jnp.float32
                    )
                )
            for h in range(together):
                step(h, scores[h], keyvals[n], False)
            continue

        @pl.when(asked_of(group))
        def _(n=n):
            for h in range(together):
                for offset in range(spaces):
                    rows = pl.ds(offset * tokens, tokens)
                    key_ref[n, h, rows, :HEAD_DIM] = keyvals[n][offset][0, :, lanes(h)]
            scores = [
                lax.dot_general(
                    key_ref[n, h], query_ref[h], NT, preferred_element_type=jnp.float32
                )
                for h in range(together)
            ]
            for h in range(together):
                step(h, scores[h], keyvals[n], True)

    if final:
        for h in range(together):
            result = jnp.transpose(acc_ref[h] * (1.0 / stat_ref[h, 1:2, :]))
            for offset in range(spaces):
                part = result[offset * tokens : (offset + 1) * tokens]
                outs[offset][:, lanes(h)] = part.astype(outs[offset].dtype)
    else:
        outs[0][...] = acc_ref[...]
        outs[1][...] = stat_ref[...]


def attend(scalars, queries, groups, state, final, whole, chunk, sizes):
    spaces, frames, columns, row_band, features = sizes
    first, heads = chunk
    tokens = queries[0].shape[0]
    width = features // spaces
    all_heads = width // HEAD_DIM
    count = spaces * tokens
    together = 2 if all(x % 2 == 0 for x in (all_heads, first, heads)) else 1
    lanes = together * HEAD_DIM
    own_block = pl.BlockSpec(
        (tokens, lanes), lambda h, place, *_: (0, (place[1] * all_heads + first) // together + h)
    )

    def block(x):
        skip = first // together if x.shape[-1] == width else 0
        if len(x.shape) == 2:
            return pl.BlockSpec((tokens, lanes), lambda h, *_: (0, skip + h))
        return pl.BlockSpec((2, tokens, lanes), lambda h, *_: (0, 0, skip + h))

    kept = [
        pl.BlockSpec((together, HEAD_DIM, count), lambda h, *_: (h, 0, 0)),
        pl.BlockSpec((together, 8, count), lambda h, *_: (h, 0, 0)),
    ]
    operands = list(queries) + [x for slot, hops, pieces in groups for x in pieces]
    in_specs = [own_block] + [block(x) for x in operands[1:]]
    if state is not None:
        in_specs += kept
        operands += list(state)
    aliases = {}
    if final:
        mine = jax.ShapeDtypeStruct((tokens, features), jnp.bfloat16)
        theirs = jax.ShapeDtypeStruct((tokens, heads * HEAD_DIM), jnp.bfloat16)
        out_shape = [mine] + [theirs] * (spaces - 1)
        out_specs = [own_block] + [block(theirs)] * (spaces - 1)
        if heads == all_heads:
            out_specs = [own_block] + [pl.BlockSpec((tokens, lanes), lambda h, *_: (0, h))] * (
                spaces - 1
            )
        if whole is not None:
            aliases = {3 + len(operands): 0}
            in_specs.append(pl.BlockSpec(memory_space=pl.ANY))
            operands.append(whole)
    else:
        out_specs = kept
        out_shape = [
            jax.ShapeDtypeStruct((heads, HEAD_DIM, count), jnp.float32),
            jax.ShapeDtypeStruct((heads, 8, count), jnp.float32),
        ]
    pairs = heads * count * count * len(groups)
    return pl.pallas_call(
        functools.partial(
            attend_kernel, spaces, frames, columns, row_band, together,
            tuple((slot, hops) for slot, hops, pieces in groups),
            state is None, final, bool(aliases),
        ),
        grid_spec=pltpu.PrefetchScalarGridSpec(
            num_scalar_prefetch=3,
            grid=(heads // together,),
            in_specs=in_specs,
            out_specs=out_specs,
            scratch_shapes=[
                pltpu.VMEM((together, count, 2 * HEAD_DIM), jnp.bfloat16),
                pltpu.VMEM((len(groups), together, count, 2 * HEAD_DIM), jnp.bfloat16),
                pltpu.VMEM((together, HEAD_DIM, count), jnp.float32),
                pltpu.VMEM((together, 8, count), jnp.float32),
            ],
        ),
        out_shape=out_shape,
        input_output_aliases=aliases,
        compiler_params=pltpu.CompilerParams(vmem_limit_bytes=VMEM_LIMIT),
        cost_estimate=pl.CostEstimate(
            flops=4 * pairs * HEAD_DIM,
            bytes_accessed=len(groups) * 4 * count * heads * HEAD_DIM,
            transcendentals=pairs,
        ),
        name="attend_final" if final else "attend",
    )(*scalars, *operands)


def put_kernel(spaces, offset, first, place_ref, piece_ref, whole_ref, out_ref, sem):
    width = piece_ref.shape[-1]
    share = out_ref.shape[-1] // spaces
    column = pl.multiple_of(lax.rem(place_ref[1] + offset, spaces) * share + first, HEAD_DIM)
    copy = pltpu.make_async_copy(piece_ref, out_ref.at[:, pl.ds(column, width)], sem)
    copy.start()
    copy.wait()


def put(place, piece, whole, offset, first, spaces):
    return pl.pallas_call(
        functools.partial(put_kernel, spaces, offset, first),
        in_specs=[
            pl.BlockSpec(memory_space=pltpu.SMEM),
            pl.BlockSpec(memory_space=pltpu.VMEM),
            pl.BlockSpec(memory_space=pl.ANY),
        ],
        out_specs=pl.BlockSpec(memory_space=pl.ANY),
        out_shape=jax.ShapeDtypeStruct(whole.shape, whole.dtype),
        scratch_shapes=[pltpu.SemaphoreType.DMA],
        input_output_aliases={2: 0},
        name="put",
    )(place, piece, whole)


def shards(spaces, frames, queries, keys, values, flags, widths):
    unused, row_band, columns, features = queries.shape
    tokens = row_band * columns
    width = features // spaces
    heads = width // HEAD_DIM
    place = jnp.stack([lax.axis_index("frame"), lax.axis_index("space")]).astype(jnp.int32)
    scalars = (place, flags, widths)
    sizes = (spaces, frames, columns, row_band, features)
    q, k, v = (x.reshape(tokens, features) for x in (queries, keys, values))
    tail = max(heads // 3, 1)
    chunks = [(0, heads - tail), (heads - tail, tail)]
    offsets = range(1, spaces)

    def along_space(x, offset):
        return lax.ppermute(x, "space", [(s, (s + offset) % spaces) for s in range(spaces)])

    def swap(x, slot, hops):
        pairs = []
        for f in range(frames):
            side = 1 if (f + slot) % 2 == 0 else -1
            source = f - side * (hops - 1)
            if 0 <= f + side < frames and 0 <= source < frames:
                pairs.append((f, f + side))
        return lax.ppermute(x, "frame", pairs)

    mine = None
    partners = []
    arrived = []
    for first, number in chunks:
        blocks = [(offset, first * HEAD_DIM, number * HEAD_DIM) for offset in offsets]
        if mine is None:
            mine, *sends = pack(place, (k, v), [(0, 0, width)] + blocks, arrived, spaces)
        else:
            sends = pack(place, (k, v), blocks, arrived, spaces)
        arrived = [along_space(x, offset) for x, offset in zip(sends, offsets)]
        partners.append(arrived)
    sends = pack(place, (q,), [(offset, 0, width) for offset in offsets], arrived, spaces)
    query_parts = [q] + [along_space(x, offset) for x, offset in zip(sends, offsets)]

    carried = [[mine, mine]] + [[x, x] for x in partners]
    states = [None] * len(chunks)
    groups = [[(0, 0, [mine] + partners[c])] for c in range(len(chunks))]
    for hops in range(1, frames - 1):
        sent = []
        for c, (first_slot, second_slot) in enumerate(carried):
            over = [second_slot, first_slot]
            if c == 0:
                sent.append([swap(over[slot], slot, hops) for slot in range(2)])
                continue
            if c == len(chunks) and states[0] is not None:
                over = [[tie(x, states[0][1]) for x in xs] for xs in over]
            sent.append([[swap(x, slot, hops) for x in over[slot]] for slot in range(2)])
        carried = sent
        for c, chunk in enumerate(chunks):
            groups[c] += [
                (slot, hops, [carried[0][slot]] + carried[1 + c][slot]) for slot in range(2)
            ]
            if hops < frames - 2:
                states[c] = attend(
                    scalars, query_parts, groups[c], states[c], False, None, chunk, sizes
                )
                groups[c] = []

    result, returned = None, []
    for c, chunk in enumerate(chunks):
        result, *parts = attend(
            scalars, query_parts, groups[c], states[c], True, result, chunk, sizes
        )
        returned.append([along_space(x, -offset) for x, offset in zip(parts, offsets)])
    for (first, unused), parts in zip(chunks, returned):
        for offset, x in zip(offsets, parts):
            result = put(place, x, result, offset, first * HEAD_DIM, spaces)
    return result.reshape(queries.shape)


def solution(mesh):
    placed = P(("group", "frame"), "space", None, "head")
    return jax.shard_map(
        functools.partial(shards, mesh.shape["space"], mesh.shape["frame"]),
        mesh=mesh,
        in_specs=(placed, placed, placed, P(), P()),
        out_specs=placed,
        check_vma=False,
    )
```

```python
import functools
import math

import jax
import jax.numpy as jnp
from jax import lax
from jax.experimental import pallas as pl
from jax.experimental.pallas import tpu as pltpu
from jax.sharding import PartitionSpec as P

HEAD_DIM = 128
NEG_FILL = -1e30
VMEM_LIMIT = 16 * 1024 * 1024
SMALL_LIMIT = 2 * 1024 * 1024
STAGED_LIMIT = 60 * 1024 * 1024
NT = (((1,), (1,)), ((), ()))
TN = (((0,), (0,)), ((), ()))


def pack_kernel(spaces, jobs, staged, place_ref, *refs):
    refs = list(refs)
    halfway = refs[len(refs) - len(jobs) - 1 : -1] if staged else []
    sems = refs[-1]
    here = place_ref[1]

    def target_of(job):
        return refs[job[4]] if job[5] is None else refs[job[4]].at[job[5]]

    copies = []
    for n, job in enumerate(jobs):
        source, offset, first, width = job[:4]
        share = refs[source].shape[-1] // spaces
        column = pl.multiple_of(lax.rem(here + offset, spaces) * share + first, HEAD_DIM)
        out = halfway[n] if staged else target_of(job)
        copy = pltpu.make_async_copy(refs[source].at[:, pl.ds(column, width)], out, sems.at[n])
        copy.start()
        copies.append(copy)
    if staged:
        seconds = []
        for n, job in enumerate(jobs):
            copies[n].wait()
            copy = pltpu.make_async_copy(halfway[n], target_of(job), sems.at[len(jobs) + n])
            copy.start()
            seconds.append(copy)
        copies = seconds
    for copy in copies:
        copy.wait()


def pack(place, sources, blocks, after, spaces, staged):
    tokens = sources[0].shape[0]
    several = len(sources) > 1
    jobs, shapes = [], []
    first_out = len(sources) + len(after)
    for n, (offset, first, width) in enumerate(blocks):
        lead = (len(sources),) if several else ()
        shapes.append(jax.ShapeDtypeStruct(lead + (tokens, width), sources[0].dtype))
        for row in range(len(sources)):
            jobs.append((row, offset, first, width, first_out + n, row if several else None))
    halfway = [pltpu.VMEM((tokens, job[3]), sources[0].dtype) for job in jobs]
    space = pl.ANY if staged else pltpu.VMEM
    return pl.pallas_call(
        functools.partial(pack_kernel, spaces, tuple(jobs), staged),
        in_specs=[pl.BlockSpec(memory_space=pltpu.SMEM)]
        + [pl.BlockSpec(memory_space=pl.ANY)] * first_out,
        out_specs=[pl.BlockSpec(memory_space=space)] * len(shapes),
        out_shape=shapes,
        scratch_shapes=(halfway if staged else []) + [pltpu.SemaphoreType.DMA((2 * len(jobs),))],
        compiler_params=pltpu.CompilerParams(
            vmem_limit_bytes=STAGED_LIMIT if staged else SMALL_LIMIT
        ),
        name="pack",
    )(place, *sources, *after)


def tie(array, after):
    return pl.pallas_call(
        lambda *refs: None,
        in_specs=[pl.BlockSpec(memory_space=pl.ANY)] * (1 + len(after)),
        out_specs=pl.BlockSpec(memory_space=pl.ANY),
        out_shape=jax.ShapeDtypeStruct(array.shape, array.dtype),
        input_output_aliases={0: 0},
        compiler_params=pltpu.CompilerParams(vmem_limit_bytes=SMALL_LIMIT),
        name="tie",
    )(array, *after)


def attend_kernel(
    spaces, frames, columns, row_band, heads, together, groups, skips, fresh, final,
    place_ref, flags_ref, widths_ref, *refs,
):
    refs = list(refs)
    queries = [refs.pop(0) for unused in range(spaces)]
    keyvals = [[refs.pop(0) for unused in range(spaces)] for unused in groups]
    state_in = None if fresh else (refs.pop(0), refs.pop(0))
    outs = [refs.pop(0) for unused in range(spaces if final else 2)]
    query_ref, key_ref = refs[:2]
    acc_ref, stat_ref = refs[2:] if final else outs
    query_skips, piece_skips = skips
    tokens = queries[0].shape[0]
    frame_now, space_now = place_ref[0], place_ref[1]
    scale = math.log2(math.e) / math.sqrt(HEAD_DIM)
    own_column = space_now * (queries[0].shape[-1] // spaces)

    def first_row(offset):
        return lax.rem(space_now - offset + spaces, spaces) * row_band

    def asked_of(group):
        slot, hops = group
        side = 1 - 2 * lax.rem(frame_now + slot, 2)
        key_frame = frame_now + side * hops
        safe = jnp.clip(key_frame, 0, frames - 1)
        known = (key_frame >= 0) & (key_frame < frames)
        return known & (flags_ref[frame_now, safe] > 0)

    token = lax.broadcasted_iota(jnp.int32, (tokens, HEAD_DIM), 0)
    row = lax.broadcasted_iota(jnp.int32, (tokens, HEAD_DIM), 1)
    for offset in range(spaces):
        rows = pl.ds(offset * tokens, tokens)
        start = (row - first_row(offset)) * columns
        hit = (token >= start) & (token < start + columns)
        mark = jnp.where(hit, 1.0, 0.0).astype(query_ref.dtype)
        for t in range(together):
            query_ref[t, rows, HEAD_DIM:] = mark
        for n, group in enumerate(groups):
            if group[1] > 0:

                @pl.when(asked_of(group))
                def _(n=n, group=group, start=start, rows=rows):
                    reach = widths_ref[group[1]] * columns
                    near = (token >= start - reach) & (token < start + columns + reach)
                    fill = jnp.where(near, 0.0, NEG_FILL).astype(key_ref.dtype)
                    for t in range(together):
                        key_ref[n, t, rows, HEAD_DIM:] = fill

    def attend_heads(turn, carry):
        head = turn * together
        slot_of = (lambda t: t) if final else (lambda t: head + t)

        def lanes(t, skip):
            return pl.ds(pl.multiple_of((head + t) * HEAD_DIM + skip, HEAD_DIM), HEAD_DIM)

        def step(t, scores, n, old):
            h = slot_of(t)
            top = jnp.max(scores, axis=0, keepdims=True) * scale
            if old:
                before = stat_ref[h, 0:1, :]
                top = jnp.maximum(top, before)
            weights = jnp.exp2(scores * scale - top)
            total = jnp.sum(weights, axis=0, keepdims=True)
            values = jnp.concatenate(
                [ref[1, :, lanes(t, skip)] for ref, skip in zip(keyvals[n], piece_skips[n])],
                axis=0,
            )
            acc = lax.dot_general(
                values, weights.astype(jnp.bfloat16), TN, preferred_element_type=jnp.float32
            )
            if old:
                fade = jnp.exp2(before - top)
                total = total + stat_ref[h, 1:2, :] * fade
                acc = acc + acc_ref[h] * fade
            stat_ref[h, 0:1, :] = top
            stat_ref[h, 1:2, :] = total
            acc_ref[h] = acc

        for t in range(together):
            for offset in range(spaces):
                skip = query_skips[offset] + (own_column if offset == 0 else 0)
                query_ref[t, pl.ds(offset * tokens, tokens), :HEAD_DIM] = queries[offset][
                    :, lanes(t, skip)
                ]
            if not fresh:
                acc_ref[slot_of(t)] = state_in[0][head + t]
                stat_ref[slot_of(t)] = state_in[1][head + t]

        for n, group in enumerate(groups):
            if group[1] == 0:
                scores = []
                for t in range(together):
                    keys = jnp.concatenate(
                        [
                            ref[0, :, lanes(t, skip)]
                            for ref, skip in zip(keyvals[n], piece_skips[n])
                        ],
                        axis=0,
                    )
                    scores.append(
                        lax.dot_general(
                            keys, query_ref[t, :, :HEAD_DIM], NT,
                            preferred_element_type=jnp.float32,
                        )
                    )
                for t in range(together):
                    step(t, scores[t], n, False)
                continue

            @pl.when(asked_of(group))
            def _(n=n):
                for t in range(together):
                    for offset in range(spaces):
                        rows = pl.ds(offset * tokens, tokens)
                        key_ref[n, t, rows, :HEAD_DIM] = keyvals[n][offset][
                            0, :, lanes(t, piece_skips[n][offset])
                        ]
                scores = [
                    lax.dot_general(
                        key_ref[n, t], query_ref[t], NT, preferred_element_type=jnp.float32
                    )
                    for t in range(together)
                ]
                for t in range(together):
                    step(t, scores[t], n, True)

        if final:
            for t in range(together):
                result = jnp.transpose(acc_ref[t] * (1.0 / stat_ref[t, 1:2, :]))
                for offset in range(spaces):
                    part = result[offset * tokens : (offset + 1) * tokens]
                    outs[offset][:, lanes(t, 0)] = part.astype(outs[offset].dtype)
        return carry

    lax.fori_loop(0, heads // together, attend_heads, 0)


def attend(scalars, queries, groups, state, final, chunk, sizes):
    spaces, frames, columns, row_band, features = sizes
    first, heads = chunk
    tokens = queries[0].shape[0]
    width = features // spaces
    count = spaces * tokens
    together = 2 if heads % 2 == 0 else 1

    def skip_of(x):
        return first * HEAD_DIM if x.shape[-1] != heads * HEAD_DIM else 0

    skips = (
        tuple(skip_of(x) for x in queries),
        tuple(tuple(skip_of(x) for x in pieces) for slot, hops, pieces in groups),
    )
    operands = list(queries) + [x for slot, hops, pieces in groups for x in pieces]
    if state is not None:
        operands += list(state)
    state_shape = [(heads, HEAD_DIM, count), (heads, 8, count)]
    if final:
        out_shape = [jax.ShapeDtypeStruct((tokens, heads * HEAD_DIM), jnp.bfloat16)] * spaces
    else:
        out_shape = [jax.ShapeDtypeStruct(shape, jnp.float32) for shape in state_shape]
    scratch = [
        pltpu.VMEM((together, count, 2 * HEAD_DIM), jnp.bfloat16),
        pltpu.VMEM((len(groups), together, count, 2 * HEAD_DIM), jnp.bfloat16),
    ]
    if final:
        scratch += [pltpu.VMEM((together,) + shape[1:], jnp.float32) for shape in state_shape]
    pairs = heads * count * count * len(groups)
    return pl.pallas_call(
        functools.partial(
            attend_kernel, spaces, frames, columns, row_band, heads, together,
            tuple((slot, hops) for slot, hops, pieces in groups), skips, state is None, final,
        ),
        in_specs=[pl.BlockSpec(memory_space=pltpu.SMEM)] * 3
        + [pl.BlockSpec(memory_space=pltpu.VMEM)] * len(operands),
        out_specs=[pl.BlockSpec(memory_space=pltpu.VMEM)] * len(out_shape),
        out_shape=out_shape,
        scratch_shapes=scratch,
        compiler_params=pltpu.CompilerParams(vmem_limit_bytes=VMEM_LIMIT),
        cost_estimate=pl.CostEstimate(
            flops=4 * pairs * HEAD_DIM,
            bytes_accessed=len(groups) * 4 * count * heads * HEAD_DIM,
            transcendentals=pairs,
        ),
        name="attend_final" if final else "attend",
    )(*scalars, *operands)


def put_kernel(spaces, places, kept, place_ref, *refs):
    pieces, out_ref, sems = refs[: len(places)], refs[-2], refs[-1]
    share = out_ref.shape[-1] // spaces
    copies = []
    for n, (offset, first) in enumerate(places):
        column = pl.multiple_of(lax.rem(place_ref[1] + offset, spaces) * share + first, HEAD_DIM)
        width = pieces[n].shape[-1]
        copy = pltpu.make_async_copy(pieces[n], out_ref.at[:, pl.ds(column, width)], sems.at[n])
        copy.start()
        copies.append(copy)
    for copy in copies:
        copy.wait()


def put(place, pieces, places, whole, shape, spaces):
    kept = [] if whole is None else [whole]
    return pl.pallas_call(
        functools.partial(put_kernel, spaces, tuple(places), len(kept)),
        in_specs=[pl.BlockSpec(memory_space=pltpu.SMEM)]
        + [pl.BlockSpec(memory_space=pltpu.VMEM)] * len(pieces)
        + [pl.BlockSpec(memory_space=pl.ANY)] * len(kept),
        out_specs=pl.BlockSpec(memory_space=pl.ANY),
        out_shape=jax.ShapeDtypeStruct(shape, pieces[0].dtype),
        scratch_shapes=[pltpu.SemaphoreType.DMA((len(pieces),))],
        input_output_aliases={1 + len(pieces): 0} if kept else {},
        compiler_params=pltpu.CompilerParams(vmem_limit_bytes=SMALL_LIMIT),
        name="put",
    )(place, *pieces, *kept)


def shards(spaces, frames, queries, keys, values, flags, widths):
    unused, row_band, columns, features = queries.shape
    tokens = row_band * columns
    width = features // spaces
    heads = width // HEAD_DIM
    place = jnp.stack([lax.axis_index("frame"), lax.axis_index("space")]).astype(jnp.int32)
    scalars = (place, flags, widths)
    sizes = (spaces, frames, columns, row_band, features)
    q, k, v = (x.reshape(tokens, features) for x in (queries, keys, values))
    tail = max(heads // 3, 1)
    chunks = [(0, heads - tail), (heads - tail, tail)]
    offsets = range(1, spaces)

    def along_space(x, offset):
        return lax.ppermute(x, "space", [(s, (s + offset) % spaces) for s in range(spaces)])

    def swap(x, slot, hops):
        pairs = []
        for f in range(frames):
            side = 1 if (f + slot) % 2 == 0 else -1
            source = f - side * (hops - 1)
            if 0 <= f + side < frames and 0 <= source < frames:
                pairs.append((f, f + side))
        return lax.ppermute(x, "frame", pairs)

    mine, queries_back, partners, arrived = None, None, [], []
    for first, number in chunks:
        blocks = [(offset, first * HEAD_DIM, number * HEAD_DIM) for offset in offsets]
        if mine is None:
            mine, *sends = pack(place, (k, v), [(0, 0, width)] + blocks, (), spaces, True)
        else:
            sends = pack(place, (k, v), blocks, arrived, spaces, False)
        arrived = [along_space(x, offset) for x, offset in zip(sends, offsets)]
        partners.append(arrived)
        if queries_back is None:
            sends = pack(place, (q,), [(o, 0, width) for o in offsets], arrived, spaces, False)
            arrived = [along_space(x, offset) for x, offset in zip(sends, offsets)]
            queries_back = arrived
    query_parts = [q] + queries_back

    carried = [[mine, mine]] + [[x, x] for x in partners]
    states = [None] * len(chunks)
    groups = [[(0, 0, [mine] + partners[c])] for c in range(len(chunks))]
    for hops in range(1, frames - 1):
        sent = []
        for c, (first_slot, second_slot) in enumerate(carried):
            over = [second_slot, first_slot]
            if c == 0:
                sent.append([swap(over[slot], slot, hops) for slot in range(2)])
                continue
            if c == len(chunks) and states[0] is not None:
                over = [[tie(x, [state[1] for state in states]) for x in xs] for xs in over]
            sent.append([[swap(x, slot, hops) for x in over[slot]] for slot in range(2)])
        carried = sent
        for c, chunk in enumerate(chunks):
            groups[c] += [
                (slot, hops, [carried[0][slot]] + carried[1 + c][slot]) for slot in range(2)
            ]
            if hops < frames - 2:
                states[c] = attend(
                    scalars, query_parts, groups[c], states[c], False, chunk, sizes
                )
                groups[c] = []

    own, returned = [], []
    for c, chunk in enumerate(chunks):
        kept, *parts = attend(scalars, query_parts, groups[c], states[c], True, chunk, sizes)
        own.append((kept, (0, chunk[0] * HEAD_DIM)))
        for offset, x in zip(offsets, parts):
            returned.append((along_space(x, -offset), (offset, chunk[0] * HEAD_DIM)))
    late = len(returned) - len(offsets)
    result = None
    for batch in (own + returned[:late], returned[late:]):
        pieces, places = zip(*batch)
        result = put(place, pieces, places, result, q.shape, spaces)
    return result.reshape(queries.shape)


def solution(mesh):
    placed = P(("group", "frame"), "space", None, "head")
    return jax.shard_map(
        functools.partial(shards, mesh.shape["space"], mesh.shape["frame"]),
        mesh=mesh,
        in_specs=(placed, placed, placed, P(), P()),
        out_specs=placed,
        check_vma=False,
    )
```

```python
import functools
import math

import jax
import jax.numpy as jnp
from jax import lax
from jax.experimental import pallas as pl
from jax.experimental.pallas import tpu as pltpu
from jax.sharding import PartitionSpec as P

HEAD_DIM = 128
NEG_FILL = -1e30
VMEM_LIMIT = 16 * 1024 * 1024
SMALL_LIMIT = 2 * 1024 * 1024
STAGED_LIMIT = 60 * 1024 * 1024
ROW_GROUPS = 4
NT = (((1,), (1,)), ((), ()))
TN = (((0,), (0,)), ((), ()))


def pack_kernel(spaces, jobs, staged, *refs):
    refs = list(refs)
    halfway = refs[len(refs) - len(jobs) - 1 : -1] if staged else []
    sems = refs[-1]
    here = lax.axis_index("space")
    tokens = refs[0].shape[0]
    groups = ROW_GROUPS if staged else 1
    first_copies, second_copies = [], []
    for n, (source, offset, first, width, target, row) in enumerate(jobs):
        share = refs[source].shape[-1] // spaces
        column = pl.multiple_of(lax.rem(here + offset, spaces) * share + first, HEAD_DIM)
        out = refs[target] if row is None else refs[target].at[row]
        for g in range(groups):
            rows = pl.ds(g * (tokens // groups), tokens // groups)
            origin = refs[source].at[rows, pl.ds(column, width)]
            stop = halfway[n].at[rows] if staged else out.at[rows]
            copy = pltpu.make_async_copy(origin, stop, sems.at[0, n * groups + g])
            copy.start()
            first_copies.append(copy)
            if staged:
                second_copies.append(
                    pltpu.make_async_copy(stop, out.at[rows], sems.at[1, n * groups + g])
                )
    for n, copy in enumerate(first_copies):
        copy.wait()
        if staged:
            second_copies[n].start()
    for copy in second_copies:
        copy.wait()


def pack(sources, blocks, after, spaces, staged):
    tokens = sources[0].shape[0]
    several = len(sources) > 1
    jobs, shapes = [], []
    first_out = len(sources) + len(after)
    for n, (offset, first, width) in enumerate(blocks):
        lead = (len(sources),) if several else ()
        shapes.append(jax.ShapeDtypeStruct(lead + (tokens, width), sources[0].dtype))
        for row in range(len(sources)):
            jobs.append((row, offset, first, width, first_out + n, row if several else None))
    halfway = [pltpu.VMEM((tokens, job[3]), sources[0].dtype) for job in jobs]
    space = pl.ANY if staged else pltpu.VMEM
    return pl.pallas_call(
        functools.partial(pack_kernel, spaces, tuple(jobs), staged),
        in_specs=[pl.BlockSpec(memory_space=pl.ANY)] * first_out,
        out_specs=[pl.BlockSpec(memory_space=space)] * len(shapes),
        out_shape=shapes,
        scratch_shapes=(halfway if staged else [])
        + [pltpu.SemaphoreType.DMA((2, ROW_GROUPS * len(jobs)))],
        compiler_params=pltpu.CompilerParams(
            vmem_limit_bytes=STAGED_LIMIT if staged else SMALL_LIMIT
        ),
        name="pack",
    )(*sources, *after)


def tie(arrays, after):
    return pl.pallas_call(
        lambda *refs: None,
        in_specs=[pl.BlockSpec(memory_space=pl.ANY)] * (len(arrays) + len(after)),
        out_specs=[pl.BlockSpec(memory_space=pl.ANY)] * len(arrays),
        out_shape=[jax.ShapeDtypeStruct(x.shape, x.dtype) for x in arrays],
        input_output_aliases={n: n for n in range(len(arrays))},
        compiler_params=pltpu.CompilerParams(vmem_limit_bytes=SMALL_LIMIT),
        name="tie",
    )(*arrays, *after)


def attend_kernel(
    spaces, frames, columns, row_band, heads, together, groups, skips, fresh, final,
    place_ref, flags_ref, widths_ref, *refs,
):
    refs = list(refs)
    queries = [refs.pop(0) for unused in range(spaces)]
    keyvals = [[refs.pop(0) for unused in range(spaces)] for unused in groups]
    state_in = None if fresh else (refs.pop(0), refs.pop(0))
    outs = [refs.pop(0) for unused in range(spaces if final else 2)]
    query_ref, key_ref = refs[:2]
    acc_ref, stat_ref = refs[2:] if final else outs
    query_skips, piece_skips = skips
    tokens = queries[0].shape[0]
    frame_now, space_now = place_ref[0], place_ref[1]
    scale = math.log2(math.e) / math.sqrt(HEAD_DIM)
    own_column = space_now * (queries[0].shape[-1] // spaces)

    def first_row(offset):
        return lax.rem(space_now - offset + spaces, spaces) * row_band

    def asked_of(group):
        slot, hops = group
        side = 1 - 2 * lax.rem(frame_now + slot, 2)
        key_frame = frame_now + side * hops
        safe = jnp.clip(key_frame, 0, frames - 1)
        known = (key_frame >= 0) & (key_frame < frames)
        return known & (flags_ref[frame_now, safe] > 0)

    token = lax.broadcasted_iota(jnp.int32, (tokens, HEAD_DIM), 0)
    row = lax.broadcasted_iota(jnp.int32, (tokens, HEAD_DIM), 1)
    for offset in range(spaces):
        rows = pl.ds(offset * tokens, tokens)
        start = (row - first_row(offset)) * columns
        hit = (token >= start) & (token < start + columns)
        mark = jnp.where(hit, 1.0, 0.0).astype(query_ref.dtype)
        for t in range(together):
            query_ref[t, rows, HEAD_DIM:] = mark
        for n, group in enumerate(groups):
            if group[1] > 0:

                @pl.when(asked_of(group))
                def _(n=n, group=group, start=start, rows=rows):
                    reach = widths_ref[group[1]] * columns
                    near = (token >= start - reach) & (token < start + columns + reach)
                    fill = jnp.where(near, 0.0, NEG_FILL).astype(key_ref.dtype)
                    for t in range(together):
                        key_ref[n, t, rows, HEAD_DIM:] = fill

    def attend_heads(turn, carry):
        head = turn * together
        slot_of = (lambda t: t) if final else (lambda t: head + t)

        def lanes(t, skip):
            return pl.ds(pl.multiple_of((head + t) * HEAD_DIM + skip, HEAD_DIM), HEAD_DIM)

        def step(t, scores, n, old):
            h = slot_of(t)
            top = jnp.max(scores, axis=0, keepdims=True) * scale
            if old:
                before = stat_ref[h, 0:1, :]
                top = jnp.maximum(top, before)
            weights = jnp.exp2(scores * scale - top)
            total = jnp.sum(weights, axis=0, keepdims=True)
            values = jnp.concatenate(
                [ref[1, :, lanes(t, skip)] for ref, skip in zip(keyvals[n], piece_skips[n])],
                axis=0,
            )
            acc = lax.dot_general(
                values, weights.astype(jnp.bfloat16), TN, preferred_element_type=jnp.float32
            )
            if old:
                fade = jnp.exp2(before - top)
                total = total + stat_ref[h, 1:2, :] * fade
                acc = acc + acc_ref[h] * fade
            stat_ref[h, 0:1, :] = top
            stat_ref[h, 1:2, :] = total
            acc_ref[h] = acc

        for t in range(together):
            for offset in range(spaces):
                skip = query_skips[offset] + (own_column if offset == 0 else 0)
                query_ref[t, pl.ds(offset * tokens, tokens), :HEAD_DIM] = queries[offset][
                    :, lanes(t, skip)
                ]
            if not fresh:
                acc_ref[slot_of(t)] = state_in[0][head + t]
                stat_ref[slot_of(t)] = state_in[1][head + t]

        for n, group in enumerate(groups):
            if group[1] == 0:
                scores = []
                for t in range(together):
                    keys = jnp.concatenate(
                        [
                            ref[0, :, lanes(t, skip)]
                            for ref, skip in zip(keyvals[n], piece_skips[n])
                        ],
                        axis=0,
                    )
                    scores.append(
                        lax.dot_general(
                            keys, query_ref[t, :, :HEAD_DIM], NT,
                            preferred_element_type=jnp.float32,
                        )
                    )
                for t in range(together):
                    step(t, scores[t], n, False)
                continue

            @pl.when(asked_of(group))
            def _(n=n):
                for t in range(together):
                    for offset in range(spaces):
                        rows = pl.ds(offset * tokens, tokens)
                        key_ref[n, t, rows, :HEAD_DIM] = keyvals[n][offset][
                            0, :, lanes(t, piece_skips[n][offset])
                        ]
                scores = [
                    lax.dot_general(
                        key_ref[n, t], query_ref[t], NT, preferred_element_type=jnp.float32
                    )
                    for t in range(together)
                ]
                for t in range(together):
                    step(t, scores[t], n, True)

        if final:
            for t in range(together):
                result = jnp.transpose(acc_ref[t] * (1.0 / stat_ref[t, 1:2, :]))
                for offset in range(spaces):
                    part = result[offset * tokens : (offset + 1) * tokens]
                    outs[offset][:, lanes(t, 0)] = part.astype(outs[offset].dtype)
        return carry

    lax.fori_loop(0, heads // together, attend_heads, 0)


def attend(scalars, queries, groups, state, final, chunk, sizes):
    spaces, frames, columns, row_band, features = sizes
    first, heads = chunk
    tokens = queries[0].shape[0]
    width = features // spaces
    count = spaces * tokens
    together = next(n for n in (3, 2, 1) if heads % n == 0)

    def skip_of(x):
        return first * HEAD_DIM if x.shape[-1] != heads * HEAD_DIM else 0

    skips = (
        tuple(skip_of(x) for x in queries),
        tuple(tuple(skip_of(x) for x in pieces) for slot, hops, pieces in groups),
    )
    operands = list(queries) + [x for slot, hops, pieces in groups for x in pieces]
    if state is not None:
        operands += list(state)
    state_shape = [(heads, HEAD_DIM, count), (heads, 8, count)]
    if final:
        out_shape = [jax.ShapeDtypeStruct((tokens, heads * HEAD_DIM), jnp.bfloat16)] * spaces
    else:
        out_shape = [jax.ShapeDtypeStruct(shape, jnp.float32) for shape in state_shape]
    scratch = [
        pltpu.VMEM((together, count, 2 * HEAD_DIM), jnp.bfloat16),
        pltpu.VMEM((len(groups), together, count, 2 * HEAD_DIM), jnp.bfloat16),
    ]
    if final:
        scratch += [pltpu.VMEM((together,) + shape[1:], jnp.float32) for shape in state_shape]
    pairs = heads * count * count * len(groups)
    return pl.pallas_call(
        functools.partial(
            attend_kernel, spaces, frames, columns, row_band, heads, together,
            tuple((slot, hops) for slot, hops, pieces in groups), skips, state is None, final,
        ),
        in_specs=[pl.BlockSpec(memory_space=pltpu.SMEM)] * 3
        + [pl.BlockSpec(memory_space=pltpu.VMEM)] * len(operands),
        out_specs=[pl.BlockSpec(memory_space=pltpu.VMEM)] * len(out_shape),
        out_shape=out_shape,
        scratch_shapes=scratch,
        compiler_params=pltpu.CompilerParams(vmem_limit_bytes=VMEM_LIMIT),
        cost_estimate=pl.CostEstimate(
            flops=4 * pairs * HEAD_DIM,
            bytes_accessed=len(groups) * 4 * count * heads * HEAD_DIM,
            transcendentals=pairs,
        ),
        name="attend_final" if final else "attend",
    )(*scalars, *operands)


def put_kernel(spaces, places, kept, place_ref, *refs):
    pieces, out_ref, sems = refs[: len(places)], refs[-2], refs[-1]
    share = out_ref.shape[-1] // spaces
    copies = []
    for n, (offset, first) in enumerate(places):
        column = pl.multiple_of(lax.rem(place_ref[1] + offset, spaces) * share + first, HEAD_DIM)
        width = pieces[n].shape[-1]
        copy = pltpu.make_async_copy(pieces[n], out_ref.at[:, pl.ds(column, width)], sems.at[n])
        copy.start()
        copies.append(copy)
    for copy in copies:
        copy.wait()


def put(place, pieces, places, whole, shape, spaces):
    kept = [] if whole is None else [whole]
    return pl.pallas_call(
        functools.partial(put_kernel, spaces, tuple(places), len(kept)),
        in_specs=[pl.BlockSpec(memory_space=pltpu.SMEM)]
        + [pl.BlockSpec(memory_space=pltpu.VMEM)] * len(pieces)
        + [pl.BlockSpec(memory_space=pl.ANY)] * len(kept),
        out_specs=pl.BlockSpec(memory_space=pl.ANY),
        out_shape=jax.ShapeDtypeStruct(shape, pieces[0].dtype),
        scratch_shapes=[pltpu.SemaphoreType.DMA((len(pieces),))],
        input_output_aliases={1 + len(pieces): 0} if kept else {},
        compiler_params=pltpu.CompilerParams(vmem_limit_bytes=SMALL_LIMIT),
        name="put",
    )(place, *pieces, *kept)


def shards(spaces, frames, queries, keys, values, flags, widths):
    unused, row_band, columns, features = queries.shape
    tokens = row_band * columns
    width = features // spaces
    heads = width // HEAD_DIM
    place = jnp.stack([lax.axis_index("frame"), lax.axis_index("space")]).astype(jnp.int32)
    scalars = (place, flags, widths)
    sizes = (spaces, frames, columns, row_band, features)
    q, k, v = (x.reshape(tokens, features) for x in (queries, keys, values))
    half = heads - heads // 2
    chunks = [(0, half), (half, heads - half)]
    offsets = range(1, spaces)

    def along_space(x, offset):
        return lax.ppermute(x, "space", [(s, (s + offset) % spaces) for s in range(spaces)])

    def swap(x, slot, hops):
        pairs = []
        for f in range(frames):
            side = 1 if (f + slot) % 2 == 0 else -1
            source = f - side * (hops - 1)
            if 0 <= f + side < frames and 0 <= source < frames:
                pairs.append((f, f + side))
        return lax.ppermute(x, "frame", pairs)

    partners, arrived = [], []
    for c, (first, number) in enumerate(chunks):
        blocks = [(offset, first * HEAD_DIM, number * HEAD_DIM) for offset in offsets]
        if c == 0:
            mine, *sends = pack((k, v), [(0, 0, width)] + blocks, (), spaces, True)
        else:
            sends = pack((k, v), blocks, arrived, spaces, False)
        arrived = [along_space(x, offset) for x, offset in zip(sends, offsets)]
        partners.append(arrived)
    sends = pack((q,), [(offset, 0, width) for offset in offsets], arrived, spaces, False)
    query_parts = [q] + [along_space(x, offset) for x, offset in zip(sends, offsets)]

    def tied(lists, after):
        flat = list(tie([x for xs in lists for x in xs], after))
        return [[flat.pop(0) for unused in xs] for xs in lists]

    states = [None] * len(chunks)
    own_now = [[mine], [mine]]
    own_next = [[swap(x, slot, 1) for x in own_now[slot]] for slot in range(2)]
    first_next = [[swap(x, slot, 1) for x in partners[0]] for slot in range(2)]
    *first_next, partners[1] = tied(first_next + [partners[1]], sends)
    second_next = [[swap(x, slot, 1) for x in partners[1]] for slot in range(2)]
    groups = [[(0, 0, [mine] + xs)] for xs in partners]
    for hops in range(1, frames - 1):
        if hops > 1:
            own_now, first_now, second_now = own_next, first_next, second_next
            own_next = early
            lists = tied(first_now + second_now, [states[0][1]])
            first_now, second_now = lists[:2], lists[2:]
            first_next = [[swap(x, slot, hops) for x in first_now[1 - slot]] for slot in range(2)]
            groups[1] = [
                (slot, hops - 1, own_now[slot] + second_now[slot]) for slot in range(2)
            ]
            if hops == 2:
                groups[1].insert(0, (0, 0, [mine] + partners[1]))
            states[1] = attend(
                scalars, query_parts, groups[1], states[1], False, chunks[1], sizes
            )
            lists = tied(second_now + own_next, [states[1][1]])
            second_now, own_next = lists[:2], lists[2:]
            second_next = [
                [swap(x, slot, hops) for x in second_now[1 - slot]] for slot in range(2)
            ]
        if hops < frames - 2:
            early = [[swap(x, slot, hops + 1) for x in own_next[1 - slot]] for slot in range(2)]
            if hops > 1:
                groups[0] = []
            groups[0] += [(slot, hops, own_next[slot] + first_next[slot]) for slot in range(2)]
            states[0] = attend(
                scalars, query_parts, groups[0], states[0], False, chunks[0], sizes
            )
    last = frames - 2
    finals = [
        [(slot, last, own_next[slot] + xs[slot]) for slot in range(2)]
        for xs in (first_next, second_next)
    ]
    if last == 1:
        finals = [own + final for own, final in zip(groups, finals)]

    own, returned = [], []
    for c, chunk in enumerate(chunks):
        kept, *parts = attend(scalars, query_parts, finals[c], states[c], True, chunk, sizes)
        own.append((kept, (0, chunk[0] * HEAD_DIM)))
        for offset, x in zip(offsets, parts):
            returned.append((along_space(x, -offset), (offset, chunk[0] * HEAD_DIM)))
    late = len(returned) - len(offsets)
    result = None
    for batch in (own + returned[:late], returned[late:]):
        pieces, places = zip(*batch)
        result = put(place, pieces, places, result, q.shape, spaces)
    return result.reshape(queries.shape)


def solution(mesh):
    placed = P(("group", "frame"), "space", None, "head")
    return jax.shard_map(
        functools.partial(shards, mesh.shape["space"], mesh.shape["frame"]),
        mesh=mesh,
        in_specs=(placed, placed, placed, P(), P()),
        out_specs=placed,
        check_vma=False,
    )
```

```python
import functools
import math

import jax
import jax.numpy as jnp
from jax import lax
from jax.experimental import pallas as pl
from jax.experimental.pallas import tpu as pltpu
from jax.sharding import PartitionSpec as P

HEAD_DIM = 128
NEG_FILL = -1e30
VMEM_LIMIT = 16 * 1024 * 1024
SMALL_LIMIT = 2 * 1024 * 1024
STAGED_LIMIT = 60 * 1024 * 1024
ROW_GROUPS = 4
NT = (((1,), (1,)), ((), ()))
TN = (((0,), (0,)), ((), ()))


def pack_kernel(spaces, jobs, staged, *refs):
    refs = list(refs)
    halfway = refs[len(refs) - len(jobs) - 1 : -1] if staged else []
    sems = refs[-1]
    here = lax.axis_index("space")
    tokens = refs[0].shape[0]
    groups = ROW_GROUPS if staged else 1
    first_copies, second_copies = [], []
    for n, (source, offset, first, width, target, row) in enumerate(jobs):
        share = refs[source].shape[-1] // spaces
        column = pl.multiple_of(lax.rem(here + offset, spaces) * share + first, HEAD_DIM)
        out = refs[target] if row is None else refs[target].at[row]
        for g in range(groups):
            rows = pl.ds(g * (tokens // groups), tokens // groups)
            origin = refs[source].at[rows, pl.ds(column, width)]
            stop = halfway[n].at[rows] if staged else out.at[rows]
            copy = pltpu.make_async_copy(origin, stop, sems.at[0, n * groups + g])
            copy.start()
            first_copies.append(copy)
            if staged:
                second_copies.append(
                    pltpu.make_async_copy(stop, out.at[rows], sems.at[1, n * groups + g])
                )
    for n, copy in enumerate(first_copies):
        copy.wait()
        if staged:
            second_copies[n].start()
    for copy in second_copies:
        copy.wait()


def pack(sources, blocks, after, spaces, staged):
    tokens = sources[0].shape[0]
    several = len(sources) > 1
    jobs, shapes = [], []
    first_out = len(sources) + len(after)
    for n, (offset, first, width) in enumerate(blocks):
        lead = (len(sources),) if several else ()
        shapes.append(jax.ShapeDtypeStruct(lead + (tokens, width), sources[0].dtype))
        for row in range(len(sources)):
            jobs.append((row, offset, first, width, first_out + n, row if several else None))
    halfway = [pltpu.VMEM((tokens, job[3]), sources[0].dtype) for job in jobs]
    space = pl.ANY if staged else pltpu.VMEM
    return pl.pallas_call(
        functools.partial(pack_kernel, spaces, tuple(jobs), staged),
        in_specs=[pl.BlockSpec(memory_space=pl.ANY)] * first_out,
        out_specs=[pl.BlockSpec(memory_space=space)] * len(shapes),
        out_shape=shapes,
        scratch_shapes=(halfway if staged else [])
        + [pltpu.SemaphoreType.DMA((2, ROW_GROUPS * len(jobs)))],
        compiler_params=pltpu.CompilerParams(
            vmem_limit_bytes=STAGED_LIMIT if staged else SMALL_LIMIT
        ),
        name="pack",
    )(*sources, *after)


def tie(arrays, after):
    return pl.pallas_call(
        lambda *refs: None,
        in_specs=[pl.BlockSpec(memory_space=pl.ANY)] * (len(arrays) + len(after)),
        out_specs=[pl.BlockSpec(memory_space=pl.ANY)] * len(arrays),
        out_shape=[jax.ShapeDtypeStruct(x.shape, x.dtype) for x in arrays],
        input_output_aliases={n: n for n in range(len(arrays))},
        compiler_params=pltpu.CompilerParams(vmem_limit_bytes=SMALL_LIMIT),
        name="tie",
    )(*arrays, *after)


def attend_kernel(
    spaces, frames, columns, row_band, heads, together, groups, skips, fresh, final,
    place_ref, flags_ref, widths_ref, *refs,
):
    refs = list(refs)
    queries = [refs.pop(0) for unused in range(spaces)]
    arrays = 1 + max(piece[0] for group in groups for piece in group[2])
    keyvals = [refs.pop(0) for unused in range(arrays)]
    state_in = None if fresh else (refs.pop(0), refs.pop(0))
    outs = [refs.pop(0) for unused in range(spaces if final else 2)]
    query_ref, key_ref = refs[:2]
    acc_ref, stat_ref = refs[2:] if final else outs
    tokens = queries[0].shape[0]
    frame_now, space_now = place_ref[0], place_ref[1]
    scale = math.log2(math.e) / math.sqrt(HEAD_DIM)
    own_column = space_now * (queries[0].shape[-1] // spaces)

    def first_row(offset):
        return lax.rem(space_now - offset + spaces, spaces) * row_band

    def asked_of(group):
        slot, hops = group[:2]
        side = 1 - 2 * lax.rem(frame_now + slot, 2)
        key_frame = frame_now + side * hops
        safe = jnp.clip(key_frame, 0, frames - 1)
        known = (key_frame >= 0) & (key_frame < frames)
        return known & (flags_ref[frame_now, safe] > 0)

    token = lax.broadcasted_iota(jnp.int32, (tokens, HEAD_DIM), 0)
    row = lax.broadcasted_iota(jnp.int32, (tokens, HEAD_DIM), 1)
    starts = [(row - first_row(offset)) * columns for offset in range(spaces)]
    for offset, start in enumerate(starts):
        hit = (token >= start) & (token < start + columns)
        mark = jnp.where(hit, 1.0, 0.0).astype(query_ref.dtype)
        for t in range(together):
            query_ref[t, pl.ds(offset * tokens, tokens), HEAD_DIM:] = mark
    for n, group in enumerate(groups):
        if group[1] > 0:

            @pl.when(asked_of(group))
            def _(n=n, group=group):
                reach = widths_ref[group[1]] * columns
                for m, (unused, unused, offset) in enumerate(group[2]):
                    start = starts[offset]
                    near = (token >= start - reach) & (token < start + columns + reach)
                    fill = jnp.where(near, 0.0, NEG_FILL).astype(key_ref.dtype)
                    for t in range(together):
                        key_ref[n, t, pl.ds(m * tokens, tokens), HEAD_DIM:] = fill

    def attend_heads(turn, carry):
        head = turn * together
        slot_of = (lambda t: t) if final else (lambda t: head + t)

        def lanes(t, skip=0):
            return pl.ds(pl.multiple_of((head + t) * HEAD_DIM + skip, HEAD_DIM), HEAD_DIM)

        def step(t, scores, pieces, old):
            h = slot_of(t)
            top = jnp.max(scores, axis=0, keepdims=True) * scale
            if old:
                before = stat_ref[h, 0:1, :]
                top = jnp.maximum(top, before)
            weights = jnp.exp2(scores * scale - top)
            total = jnp.sum(weights, axis=0, keepdims=True)
            values = jnp.concatenate([keyvals[i][r + 1, :, lanes(t)] for i, r, o in pieces], axis=0)
            acc = lax.dot_general(
                values, weights.astype(jnp.bfloat16), TN, preferred_element_type=jnp.float32
            )
            if old:
                fade = jnp.exp2(before - top)
                total = total + stat_ref[h, 1:2, :] * fade
                acc = acc + acc_ref[h] * fade
            stat_ref[h, 0:1, :] = top
            stat_ref[h, 1:2, :] = total
            acc_ref[h] = acc

        for t in range(together):
            for offset in range(spaces):
                skip = skips[offset] + (own_column if offset == 0 else 0)
                query_ref[t, pl.ds(offset * tokens, tokens), :HEAD_DIM] = queries[offset][
                    :, lanes(t, skip)
                ]
            if not fresh:
                acc_ref[slot_of(t)] = state_in[0][head + t]
                stat_ref[slot_of(t)] = state_in[1][head + t]

        for n, (slot, hops, pieces) in enumerate(groups):
            if hops == 0:
                scores = []
                for t in range(together):
                    keys = jnp.concatenate(
                        [keyvals[i][r, :, lanes(t)] for i, r, o in pieces], axis=0
                    )
                    scores.append(
                        lax.dot_general(
                            keys, query_ref[t, :, :HEAD_DIM], NT,
                            preferred_element_type=jnp.float32,
                        )
                    )
                for t in range(together):
                    step(t, scores[t], pieces, False)
                continue

            @pl.when(asked_of(groups[n]))
            def _(n=n, pieces=pieces):
                many = pl.ds(0, len(pieces) * tokens)
                for t in range(together):
                    for m, (i, r, unused) in enumerate(pieces):
                        key_ref[n, t, pl.ds(m * tokens, tokens), :HEAD_DIM] = keyvals[i][
                            r, :, lanes(t)
                        ]
                scores = [
                    lax.dot_general(
                        key_ref[n, t, many], query_ref[t], NT, preferred_element_type=jnp.float32
                    )
                    for t in range(together)
                ]
                for t in range(together):
                    step(t, scores[t], pieces, True)

        if final:
            for t in range(together):
                result = jnp.transpose(acc_ref[t] * (1.0 / stat_ref[t, 1:2, :]))
                for offset in range(spaces):
                    part = result[offset * tokens : (offset + 1) * tokens]
                    outs[offset][:, lanes(t)] = part.astype(outs[offset].dtype)
        return carry

    lax.fori_loop(0, heads // together, attend_heads, 0)


def attend(scalars, queries, groups, state, final, chunk, sizes):
    spaces, frames, columns, row_band, features = sizes
    first, heads = chunk
    tokens = queries[0].shape[0]
    count = spaces * tokens
    together = next(n for n in (3, 2, 1) if heads % n == 0)
    arrays, numbered = [], []
    for slot, hops, pieces in groups:
        listed = []
        for array, row, offset in pieces:
            known = [n for n, x in enumerate(arrays) if x is array]
            if not known:
                known = [len(arrays)]
                arrays.append(array)
            listed.append((known[0], row, offset))
        numbered.append((slot, hops, tuple(listed)))
    operands = list(queries) + arrays + (list(state) if state is not None else [])
    state_shape = [(heads, HEAD_DIM, count), (heads, 8, count)]
    if final:
        out_shape = [jax.ShapeDtypeStruct((tokens, heads * HEAD_DIM), jnp.bfloat16)] * spaces
    else:
        out_shape = [jax.ShapeDtypeStruct(shape, jnp.float32) for shape in state_shape]
    scratch = [
        pltpu.VMEM((together, count, 2 * HEAD_DIM), jnp.bfloat16),
        pltpu.VMEM((len(groups), together, count, 2 * HEAD_DIM), jnp.bfloat16),
    ]
    if final:
        scratch += [pltpu.VMEM((together,) + shape[1:], jnp.float32) for shape in state_shape]
    pairs = heads * count * tokens * sum(len(pieces) for slot, hops, pieces in groups)
    return pl.pallas_call(
        functools.partial(
            attend_kernel, spaces, frames, columns, row_band, heads, together,
            tuple(numbered), (first * HEAD_DIM,) * spaces, state is None, final,
        ),
        in_specs=[pl.BlockSpec(memory_space=pltpu.SMEM)] * 3
        + [pl.BlockSpec(memory_space=pltpu.VMEM)] * len(operands),
        out_specs=[pl.BlockSpec(memory_space=pltpu.VMEM)] * len(out_shape),
        out_shape=out_shape,
        scratch_shapes=scratch,
        compiler_params=pltpu.CompilerParams(vmem_limit_bytes=VMEM_LIMIT),
        cost_estimate=pl.CostEstimate(
            flops=4 * pairs * HEAD_DIM,
            bytes_accessed=8 * count * heads * HEAD_DIM,
            transcendentals=pairs,
        ),
        name="attend_final" if final else "attend",
    )(*scalars, *operands)


def join_kernel(parts, *refs):
    for n, rows in enumerate(parts):
        refs[-1][pl.ds(sum(parts[:n]), rows)] = refs[n][...]


def join(arrays):
    parts = tuple(x.shape[0] for x in arrays)
    shape = (sum(parts),) + arrays[0].shape[1:]
    return pl.pallas_call(
        functools.partial(join_kernel, parts),
        in_specs=[pl.BlockSpec(memory_space=pltpu.VMEM)] * len(arrays),
        out_specs=pl.BlockSpec(memory_space=pltpu.VMEM),
        out_shape=jax.ShapeDtypeStruct(shape, arrays[0].dtype),
        compiler_params=pltpu.CompilerParams(vmem_limit_bytes=SMALL_LIMIT),
        name="join",
    )(*arrays)


def put_kernel(spaces, places, kept, place_ref, *refs):
    pieces, out_ref, sems = refs[: len(places)], refs[-2], refs[-1]
    share = out_ref.shape[-1] // spaces
    copies = []
    for n, (offset, first) in enumerate(places):
        column = pl.multiple_of(lax.rem(place_ref[1] + offset, spaces) * share + first, HEAD_DIM)
        width = pieces[n].shape[-1]
        copy = pltpu.make_async_copy(pieces[n], out_ref.at[:, pl.ds(column, width)], sems.at[n])
        copy.start()
        copies.append(copy)
    for copy in copies:
        copy.wait()


def put(place, pieces, places, whole, shape, spaces):
    kept = [] if whole is None else [whole]
    return pl.pallas_call(
        functools.partial(put_kernel, spaces, tuple(places), len(kept)),
        in_specs=[pl.BlockSpec(memory_space=pltpu.SMEM)]
        + [pl.BlockSpec(memory_space=pltpu.VMEM)] * len(pieces)
        + [pl.BlockSpec(memory_space=pl.ANY)] * len(kept),
        out_specs=pl.BlockSpec(memory_space=pl.ANY),
        out_shape=jax.ShapeDtypeStruct(shape, pieces[0].dtype),
        scratch_shapes=[pltpu.SemaphoreType.DMA((len(pieces),))],
        input_output_aliases={1 + len(pieces): 0} if kept else {},
        compiler_params=pltpu.CompilerParams(vmem_limit_bytes=SMALL_LIMIT),
        name="put",
    )(place, *pieces, *kept)


def shards(spaces, frames, queries, keys, values, flags, widths):
    unused, row_band, columns, features = queries.shape
    tokens = row_band * columns
    width = features // spaces
    heads = width // HEAD_DIM
    place = jnp.stack([lax.axis_index("frame"), lax.axis_index("space")]).astype(jnp.int32)
    scalars = (place, flags, widths)
    sizes = (spaces, frames, columns, row_band, features)
    q, k, v = (x.reshape(tokens, features) for x in (queries, keys, values))
    half = heads - heads // 2
    chunks = [(0, half), (half, heads - half)]
    offsets = range(1, spaces)

    def along_space(x, offset):
        return lax.ppermute(x, "space", [(s, (s + offset) % spaces) for s in range(spaces)])

    def swap(x, slot):
        pairs = []
        for f in range(frames):
            side = 1 if (f + slot) % 2 == 0 else -1
            if 0 <= f + side < frames:
                pairs.append((f, f + side))
        return lax.ppermute(x, "frame", pairs)

    def swap_both(xs):
        second = swap(xs[1], 1)
        return [swap(xs[0], 0), second]

    own, partners, arrived = [], [], []
    for c, (first, number) in enumerate(chunks):
        blocks = [(offset, first * HEAD_DIM, number * HEAD_DIM) for offset in offsets]
        if c == 0:
            mine = [(0, f * HEAD_DIM, n * HEAD_DIM) for f, n in chunks]
            packed = pack((k, v), blocks + mine, (), spaces, True)
            sends, own = packed[: len(blocks)], packed[len(blocks) :]
        else:
            sends = pack((k, v), blocks, arrived, spaces, False)
        arrived = [along_space(x, offset) for x, offset in zip(sends, offsets)]
        partners.append(arrived)
    sends = pack((q,), [(offset, 0, width) for offset in offsets], arrived, spaces, False)
    query_parts = [q] + [along_space(x, offset) for x, offset in zip(sends, offsets)]

    last = frames - 2
    behind = 2 * len(offsets)

    def own_band(message, hops):
        return [(slot, hops, [(x, x.shape[0] - 2, 0)]) for slot, x in enumerate(message)]

    def partner_bands(message, hops):
        return [
            (slot, hops, [(x, 2 * (o - 1), o) for o in offsets]) for slot, x in enumerate(message)
        ]

    firsts = [swap_both([x, x]) for x in own]
    seconds = []
    for c in range(len(chunks)):
        ready = [join(partners[c] + [firsts[c][1 - slot]]) for slot in range(2)]
        seconds.append(swap_both(ready))
    messages, states, ends = seconds, [None] * len(chunks), [None] * len(chunks)
    for hops in range(2, frames):
        following = []
        for c, chunk in enumerate(chunks):
            came = messages[c]
            if c > 0:
                came = list(tie(came, [states[c - 1][1]]))
            if hops == last:
                sent = [came[1 - slot][:behind] for slot in range(2)]
            else:
                sent = [came[1 - slot] for slot in range(2)]
            if hops <= last:
                following.append(swap_both(sent))
                groups = [
                    (slot, hops - 1, a + b)
                    for (slot, unused, a), (unused, unused, b) in zip(
                        own_band(firsts[c], 1), partner_bands(came, 1)
                    )
                ]
                if hops == 2:
                    own_frame = [(own[c], 0, 0)]
                    own_frame += [(x, 0, o) for x, o in zip(partners[c], offsets)]
                    groups.insert(0, (0, 0, own_frame))
                else:
                    groups = partner_bands(came, hops - 1)
                groups += own_band(came, hops)
                states[c] = attend(
                    scalars, query_parts, groups, states[c], False, chunk, sizes
                )
            else:
                ends[c] = partner_bands(came, last)
        messages = following

    own, returned = [], []
    for c, chunk in enumerate(chunks):
        kept, *parts = attend(scalars, query_parts, ends[c], states[c], True, chunk, sizes)
        own.append((kept, (0, chunk[0] * HEAD_DIM)))
        for offset, x in zip(offsets, parts):
            returned.append((along_space(x, -offset), (offset, chunk[0] * HEAD_DIM)))
    late = len(returned) - len(offsets)
    result = None
    for batch in (own + returned[:late], returned[late:]):
        pieces, places = zip(*batch)
        result = put(place, pieces, places, result, q.shape, spaces)
    return result.reshape(queries.shape)


def solution(mesh):
    placed = P(("group", "frame"), "space", None, "head")
    return jax.shard_map(
        functools.partial(shards, mesh.shape["space"], mesh.shape["frame"]),
        mesh=mesh,
        in_specs=(placed, placed, placed, P(), P()),
        out_specs=placed,
        check_vma=False,
    )
```

```python
import functools
import math

import jax
import jax.numpy as jnp
from jax import lax
from jax.experimental import pallas as pl
from jax.experimental.pallas import tpu as pltpu
from jax.sharding import PartitionSpec as P

HEAD_DIM = 128
NEG_FILL = -1e30
VMEM_LIMIT = 16 * 1024 * 1024
SMALL_LIMIT = 2 * 1024 * 1024
STAGED_LIMIT = 60 * 1024 * 1024
ROW_GROUPS = 4
NT = (((1,), (1,)), ((), ()))
TN = (((0,), (0,)), ((), ()))


def pack_kernel(spaces, jobs, staged, *refs):
    refs = list(refs)
    halfway = refs[len(refs) - len(jobs) - 1 : -1] if staged else []
    sems = refs[-1]
    here = lax.axis_index("space")
    tokens = refs[0].shape[0]
    groups = ROW_GROUPS if staged else 1
    first_copies, second_copies = [], []
    for n, (source, offset, first, width, target, row) in enumerate(jobs):
        share = refs[source].shape[-1] // spaces
        column = pl.multiple_of(lax.rem(here + offset, spaces) * share + first, HEAD_DIM)
        out = refs[target] if row is None else refs[target].at[row]
        for g in range(groups):
            rows = pl.ds(g * (tokens // groups), tokens // groups)
            origin = refs[source].at[rows, pl.ds(column, width)]
            stop = halfway[n].at[rows] if staged else out.at[rows]
            copy = pltpu.make_async_copy(origin, stop, sems.at[0, n * groups + g])
            copy.start()
            first_copies.append(copy)
            if staged:
                second_copies.append(
                    pltpu.make_async_copy(stop, out.at[rows], sems.at[1, n * groups + g])
                )
    for n, copy in enumerate(first_copies):
        copy.wait()
        if staged:
            second_copies[n].start()
    for copy in second_copies:
        copy.wait()


def pack(sources, blocks, after, spaces, staged):
    tokens = sources[0].shape[0]
    several = len(sources) > 1
    jobs, shapes = [], []
    first_out = len(sources) + len(after)
    for n, (offset, first, width) in enumerate(blocks):
        lead = (len(sources),) if several else ()
        shapes.append(jax.ShapeDtypeStruct(lead + (tokens, width), sources[0].dtype))
        for row in range(len(sources)):
            jobs.append((row, offset, first, width, first_out + n, row if several else None))
    halfway = [pltpu.VMEM((tokens, job[3]), sources[0].dtype) for job in jobs]
    space = pl.ANY if staged else pltpu.VMEM
    return pl.pallas_call(
        functools.partial(pack_kernel, spaces, tuple(jobs), staged),
        in_specs=[pl.BlockSpec(memory_space=pl.ANY)] * first_out,
        out_specs=[pl.BlockSpec(memory_space=space)] * len(shapes),
        out_shape=shapes,
        scratch_shapes=(halfway if staged else [])
        + [pltpu.SemaphoreType.DMA((2, ROW_GROUPS * len(jobs)))],
        compiler_params=pltpu.CompilerParams(
            vmem_limit_bytes=STAGED_LIMIT if staged else SMALL_LIMIT
        ),
        name="pack",
    )(*sources, *after)


def tie(arrays, after):
    return pl.pallas_call(
        lambda *refs: None,
        in_specs=[pl.BlockSpec(memory_space=pl.ANY)] * (len(arrays) + len(after)),
        out_specs=[pl.BlockSpec(memory_space=pl.ANY)] * len(arrays),
        out_shape=[jax.ShapeDtypeStruct(x.shape, x.dtype) for x in arrays],
        input_output_aliases={n: n for n in range(len(arrays))},
        compiler_params=pltpu.CompilerParams(vmem_limit_bytes=SMALL_LIMIT),
        name="tie",
    )(*arrays, *after)


def attend_kernel(
    spaces, frames, columns, row_band, heads, together, groups, skips, fresh, final,
    flags_ref, widths_ref, *refs,
):
    refs = list(refs)
    queries = [refs.pop(0) for unused in range(spaces)]
    arrays = 1 + max(piece[0] for group in groups for piece in group[2])
    keyvals = [refs.pop(0) for unused in range(arrays)]
    state_in = None if fresh else (refs.pop(0), refs.pop(0))
    outs = [refs.pop(0) for unused in range(spaces if final else 2)]
    query_ref, key_ref = refs[:2]
    acc_ref, stat_ref = refs[2:] if final else outs
    tokens = queries[0].shape[0]
    frame_now, space_now = lax.axis_index("frame"), lax.axis_index("space")
    scale = math.log2(math.e) / math.sqrt(HEAD_DIM)
    own_column = space_now * (queries[0].shape[-1] // spaces)

    def first_row(offset):
        return lax.rem(space_now - offset + spaces, spaces) * row_band

    def asked_of(group):
        slot, hops = group[:2]
        side = 1 - 2 * lax.rem(frame_now + slot, 2)
        key_frame = frame_now + side * hops
        safe = jnp.clip(key_frame, 0, frames - 1)
        known = (key_frame >= 0) & (key_frame < frames)
        return known & (flags_ref[frame_now, safe] > 0)

    token = lax.broadcasted_iota(jnp.int32, (tokens, HEAD_DIM), 0)
    row = lax.broadcasted_iota(jnp.int32, (tokens, HEAD_DIM), 1)
    starts = [(row - first_row(offset)) * columns for offset in range(spaces)]
    for offset, start in enumerate(starts):
        hit = (token >= start) & (token < start + columns)
        mark = jnp.where(hit, 1.0, 0.0).astype(query_ref.dtype)
        for t in range(together):
            query_ref[t, pl.ds(offset * tokens, tokens), HEAD_DIM:] = mark
    for n, group in enumerate(groups):
        if group[1] > 0:

            @pl.when(asked_of(group))
            def _(n=n, group=group):
                reach = widths_ref[group[1]] * columns
                for m, (unused, unused, offset) in enumerate(group[2]):
                    start = starts[offset]
                    near = (token >= start - reach) & (token < start + columns + reach)
                    fill = jnp.where(near, 0.0, NEG_FILL).astype(key_ref.dtype)
                    for t in range(together):
                        key_ref[n, t, pl.ds(m * tokens, tokens), HEAD_DIM:] = fill

    def attend_heads(turn, carry):
        head = turn * together
        slot_of = (lambda t: t) if final else (lambda t: head + t)

        def lanes(t, skip=0):
            return pl.ds(pl.multiple_of((head + t) * HEAD_DIM + skip, HEAD_DIM), HEAD_DIM)

        def step(t, scores, pieces, old):
            h = slot_of(t)
            top = jnp.max(scores, axis=0, keepdims=True) * scale
            if old:
                before = stat_ref[h, 0:1, :]
                top = jnp.maximum(top, before)
            weights = jnp.exp2(scores * scale - top)
            total = jnp.sum(weights, axis=0, keepdims=True)
            values = jnp.concatenate([keyvals[i][r + 1, :, lanes(t)] for i, r, o in pieces], axis=0)
            acc = lax.dot_general(
                values, weights.astype(jnp.bfloat16), TN, preferred_element_type=jnp.float32
            )
            if old:
                fade = jnp.exp2(before - top)
                total = total + stat_ref[h, 1:2, :] * fade
                acc = acc + acc_ref[h] * fade
            stat_ref[h, 0:1, :] = top
            stat_ref[h, 1:2, :] = total
            acc_ref[h] = acc

        for t in range(together):
            for offset in range(spaces):
                skip = skips[offset] + (own_column if offset == 0 else 0)
                query_ref[t, pl.ds(offset * tokens, tokens), :HEAD_DIM] = queries[offset][
                    :, lanes(t, skip)
                ]
            if not fresh:
                acc_ref[slot_of(t)] = state_in[0][head + t]
                stat_ref[slot_of(t)] = state_in[1][head + t]

        for n, (slot, hops, pieces) in enumerate(groups):
            if hops == 0:
                scores = []
                for t in range(together):
                    keys = jnp.concatenate(
                        [keyvals[i][r, :, lanes(t)] for i, r, o in pieces], axis=0
                    )
                    scores.append(
                        lax.dot_general(
                            keys, query_ref[t, :, :HEAD_DIM], NT,
                            preferred_element_type=jnp.float32,
                        )
                    )
                for t in range(together):
                    step(t, scores[t], pieces, False)
                continue

            @pl.when(asked_of(groups[n]))
            def _(n=n, pieces=pieces):
                many = pl.ds(0, len(pieces) * tokens)
                for t in range(together):
                    for m, (i, r, unused) in enumerate(pieces):
                        key_ref[n, t, pl.ds(m * tokens, tokens), :HEAD_DIM] = keyvals[i][
                            r, :, lanes(t)
                        ]
                scores = [
                    lax.dot_general(
                        key_ref[n, t, many], query_ref[t], NT, preferred_element_type=jnp.float32
                    )
                    for t in range(together)
                ]
                for t in range(together):
                    step(t, scores[t], pieces, True)

        if final:
            for t in range(together):
                result = jnp.transpose(acc_ref[t] * (1.0 / stat_ref[t, 1:2, :]))
                for offset in range(spaces):
                    part = result[offset * tokens : (offset + 1) * tokens]
                    outs[offset][:, lanes(t)] = part.astype(outs[offset].dtype)
        return carry

    lax.fori_loop(0, heads // together, attend_heads, 0)


def attend(scalars, queries, groups, state, final, chunk, sizes):
    spaces, frames, columns, row_band, features = sizes
    first, heads = chunk
    tokens = queries[0].shape[0]
    count = spaces * tokens
    together = next(n for n in (3, 2, 1) if heads % n == 0)
    arrays, numbered = [], []
    for slot, hops, pieces in groups:
        listed = []
        for array, row, offset in pieces:
            known = [n for n, x in enumerate(arrays) if x is array]
            if not known:
                known = [len(arrays)]
                arrays.append(array)
            listed.append((known[0], row, offset))
        numbered.append((slot, hops, tuple(listed)))
    operands = list(queries) + arrays + (list(state) if state is not None else [])
    state_shape = [(heads, HEAD_DIM, count), (heads, 8, count)]
    if final:
        out_shape = [jax.ShapeDtypeStruct((tokens, heads * HEAD_DIM), jnp.bfloat16)] * spaces
    else:
        out_shape = [jax.ShapeDtypeStruct(shape, jnp.float32) for shape in state_shape]
    scratch = [
        pltpu.VMEM((together, count, 2 * HEAD_DIM), jnp.bfloat16),
        pltpu.VMEM((len(groups), together, count, 2 * HEAD_DIM), jnp.bfloat16),
    ]
    if final:
        scratch += [pltpu.VMEM((together,) + shape[1:], jnp.float32) for shape in state_shape]
    pairs = heads * count * tokens * sum(len(pieces) for slot, hops, pieces in groups)
    return pl.pallas_call(
        functools.partial(
            attend_kernel, spaces, frames, columns, row_band, heads, together,
            tuple(numbered), (first * HEAD_DIM,) * spaces, state is None, final,
        ),
        in_specs=[pl.BlockSpec(memory_space=pltpu.SMEM)] * 2
        + [pl.BlockSpec(memory_space=pltpu.VMEM)] * len(operands),
        out_specs=[pl.BlockSpec(memory_space=pltpu.VMEM)] * len(out_shape),
        out_shape=out_shape,
        scratch_shapes=scratch,
        compiler_params=pltpu.CompilerParams(vmem_limit_bytes=VMEM_LIMIT),
        cost_estimate=pl.CostEstimate(
            flops=4 * pairs * HEAD_DIM,
            bytes_accessed=8 * count * heads * HEAD_DIM,
            transcendentals=pairs,
        ),
        name="attend_final" if final else "attend",
    )(*scalars, *operands)


def join_kernel(parts, *refs):
    for n, rows in enumerate(parts):
        refs[-1][pl.ds(sum(parts[:n]), rows)] = refs[n][...]


def join(arrays):
    parts = tuple(x.shape[0] for x in arrays)
    shape = (sum(parts),) + arrays[0].shape[1:]
    return pl.pallas_call(
        functools.partial(join_kernel, parts),
        in_specs=[pl.BlockSpec(memory_space=pltpu.VMEM)] * len(arrays),
        out_specs=pl.BlockSpec(memory_space=pltpu.VMEM),
        out_shape=jax.ShapeDtypeStruct(shape, arrays[0].dtype),
        compiler_params=pltpu.CompilerParams(vmem_limit_bytes=SMALL_LIMIT),
        name="join",
    )(*arrays)


def put_kernel(spaces, places, *refs):
    pieces, out_ref, sems = refs[: len(places)], refs[-2], refs[-1]
    share = out_ref.shape[-1] // spaces
    here = lax.axis_index("space")
    copies = []
    for n, (offset, first) in enumerate(places):
        column = pl.multiple_of(lax.rem(here + offset, spaces) * share + first, HEAD_DIM)
        width = pieces[n].shape[-1]
        copy = pltpu.make_async_copy(pieces[n], out_ref.at[:, pl.ds(column, width)], sems.at[n])
        copy.start()
        copies.append(copy)
    for copy in copies:
        copy.wait()


def put(pieces, places, whole, shape, spaces):
    kept = [] if whole is None else [whole]
    return pl.pallas_call(
        functools.partial(put_kernel, spaces, tuple(places)),
        in_specs=[pl.BlockSpec(memory_space=pltpu.VMEM)] * len(pieces)
        + [pl.BlockSpec(memory_space=pl.ANY)] * len(kept),
        out_specs=pl.BlockSpec(memory_space=pl.ANY),
        out_shape=jax.ShapeDtypeStruct(shape, pieces[0].dtype),
        scratch_shapes=[pltpu.SemaphoreType.DMA((len(pieces),))],
        input_output_aliases={len(pieces): 0} if kept else {},
        compiler_params=pltpu.CompilerParams(vmem_limit_bytes=SMALL_LIMIT),
        name="put",
    )(*pieces, *kept)


def shards(spaces, frames, queries, keys, values, flags, widths):
    unused, row_band, columns, features = queries.shape
    tokens = row_band * columns
    width = features // spaces
    heads = width // HEAD_DIM
    scalars = (flags, widths)
    sizes = (spaces, frames, columns, row_band, features)
    q, k, v = (x.reshape(tokens, features) for x in (queries, keys, values))
    half = heads - heads // 2
    chunks = [(0, half), (half, heads - half)]
    offsets = range(1, spaces)

    def along_space(x, offset):
        return lax.ppermute(x, "space", [(s, (s + offset) % spaces) for s in range(spaces)])

    def swap(x, slot):
        pairs = []
        for f in range(frames):
            side = 1 if (f + slot) % 2 == 0 else -1
            if 0 <= f + side < frames:
                pairs.append((f, f + side))
        return lax.ppermute(x, "frame", pairs)

    def swap_both(xs):
        second = swap(xs[1], 1)
        return [swap(xs[0], 0), second]

    own, partners, arrived = [], [], []
    for c, (first, number) in enumerate(chunks):
        blocks = [(offset, first * HEAD_DIM, number * HEAD_DIM) for offset in offsets]
        if c == 0:
            mine = [(0, f * HEAD_DIM, n * HEAD_DIM) for f, n in chunks]
            packed = pack((k, v), blocks + mine, (), spaces, True)
            sends, own = packed[: len(blocks)], packed[len(blocks) :]
        else:
            sends = pack((k, v), blocks, arrived, spaces, False)
        arrived = [along_space(x, offset) for x, offset in zip(sends, offsets)]
        partners.append(arrived)
    sends = pack((q,), [(offset, 0, width) for offset in offsets], arrived, spaces, False)
    query_parts = [q] + [along_space(x, offset) for x, offset in zip(sends, offsets)]
    partners[1] = list(tie(partners[1], sends))

    last = frames - 2
    behind = 2 * len(offsets)

    def own_band(message, hops):
        return [(slot, hops, [(x, x.shape[0] - 2, 0)]) for slot, x in enumerate(message)]

    def partner_bands(message, hops):
        return [
            (slot, hops, [(x, 2 * (o - 1), o) for o in offsets]) for slot, x in enumerate(message)
        ]

    firsts = [swap_both([x, x]) for x in own]
    seconds = []
    for c in range(len(chunks)):
        ready = [join(partners[c] + [firsts[c][1 - slot]]) for slot in range(2)]
        seconds.append(swap_both(ready))
    states = []
    for c, chunk in enumerate(chunks):
        pieces = [(own[c], 0, 0)] + [(x, 0, o) for x, o in zip(partners[c], offsets)]
        groups = [(0, 0, pieces)] + own_band(firsts[c], 1)
        states.append(attend(scalars, query_parts, groups, None, False, chunk, sizes))

    messages = seconds
    for hops in range(2, frames - 1):
        following = []
        for c, chunk in enumerate(chunks):
            after = [state[1] for state in (states if c == 0 else states[:c])]
            came = list(tie(messages[c], after))
            rows = behind if hops == last else behind + 2
            following.append(swap_both([came[1 - slot][:rows] for slot in range(2)]))
            groups = partner_bands(came, hops - 1) + own_band(came, hops)
            states[c] = attend(scalars, query_parts, groups, states[c], False, chunk, sizes)
        messages = following
    ends = []
    for message in messages:
        came = list(tie(message, [state[1] for state in states]))
        ends.append(partner_bands(came, last))

    own, returned = [], []
    for c, chunk in enumerate(chunks):
        kept, *parts = attend(scalars, query_parts, ends[c], states[c], True, chunk, sizes)
        own.append((kept, (0, chunk[0] * HEAD_DIM)))
        for offset, x in zip(offsets, parts):
            returned.append((along_space(x, -offset), (offset, chunk[0] * HEAD_DIM)))
    late = len(returned) - len(offsets)
    result = None
    for batch in (own + returned[:late], returned[late:]):
        pieces, places = zip(*batch)
        result = put(pieces, places, result, q.shape, spaces)
    return result.reshape(queries.shape)


def solution(mesh):
    placed = P(("group", "frame"), "space", None, "head")
    return jax.shard_map(
        functools.partial(shards, mesh.shape["space"], mesh.shape["frame"]),
        mesh=mesh,
        in_specs=(placed, placed, placed, P(), P()),
        out_specs=placed,
        check_vma=False,
    )
```

```python
import functools
import math

import jax
import jax.numpy as jnp
from jax import lax
from jax.experimental import pallas as pl
from jax.experimental.pallas import tpu as pltpu
from jax.sharding import PartitionSpec as P

HEAD_DIM = 128
NEG_FILL = -1e30
VMEM_LIMIT = 16 * 1024 * 1024
SMALL_LIMIT = 2 * 1024 * 1024
STAGED_LIMIT = 60 * 1024 * 1024
ROW_GROUPS = 4
NT = (((1,), (1,)), ((), ()))
TN = (((0,), (0,)), ((), ()))


def pack_kernel(spaces, jobs, staged, *refs):
    refs = list(refs)
    halfway = refs[len(refs) - len(jobs) - 1 : -1] if staged else []
    sems = refs[-1]
    here = lax.axis_index("space")
    tokens = refs[0].shape[0]
    groups = ROW_GROUPS if staged else 1
    first_copies, second_copies = [], []
    for n, (source, offset, first, width, target, row) in enumerate(jobs):
        share = refs[source].shape[-1] // spaces
        column = pl.multiple_of(lax.rem(here + offset, spaces) * share + first, HEAD_DIM)
        out = refs[target] if row is None else refs[target].at[row]
        for g in range(groups):
            rows = pl.ds(g * (tokens // groups), tokens // groups)
            origin = refs[source].at[rows, pl.ds(column, width)]
            stop = halfway[n].at[rows] if staged else out.at[rows]
            copy = pltpu.make_async_copy(origin, stop, sems.at[0, n * groups + g])
            copy.start()
            first_copies.append(copy)
            if staged:
                second_copies.append(
                    pltpu.make_async_copy(stop, out.at[rows], sems.at[1, n * groups + g])
                )
    for n, copy in enumerate(first_copies):
        copy.wait()
        if staged:
            second_copies[n].start()
    for copy in second_copies:
        copy.wait()


def pack(sources, blocks, after, spaces, staged):
    tokens = sources[0].shape[0]
    several = len(sources) > 1
    jobs, shapes = [], []
    first_out = len(sources) + len(after)
    for n, (offset, first, width) in enumerate(blocks):
        lead = (len(sources),) if several else ()
        shapes.append(jax.ShapeDtypeStruct(lead + (tokens, width), sources[0].dtype))
        for row in range(len(sources)):
            jobs.append((row, offset, first, width, first_out + n, row if several else None))
    halfway = [pltpu.VMEM((tokens, job[3]), sources[0].dtype) for job in jobs]
    space = pl.ANY if staged else pltpu.VMEM
    return pl.pallas_call(
        functools.partial(pack_kernel, spaces, tuple(jobs), staged),
        in_specs=[pl.BlockSpec(memory_space=pl.ANY)] * first_out,
        out_specs=[pl.BlockSpec(memory_space=space)] * len(shapes),
        out_shape=shapes,
        scratch_shapes=(halfway if staged else [])
        + [pltpu.SemaphoreType.DMA((2, ROW_GROUPS * len(jobs)))],
        compiler_params=pltpu.CompilerParams(
            vmem_limit_bytes=STAGED_LIMIT if staged else SMALL_LIMIT
        ),
        name="pack",
    )(*sources, *after)


def tie(arrays, after):
    return pl.pallas_call(
        lambda *refs: None,
        in_specs=[pl.BlockSpec(memory_space=pl.ANY)] * (len(arrays) + len(after)),
        out_specs=[pl.BlockSpec(memory_space=pl.ANY)] * len(arrays),
        out_shape=[jax.ShapeDtypeStruct(x.shape, x.dtype) for x in arrays],
        input_output_aliases={n: n for n in range(len(arrays))},
        compiler_params=pltpu.CompilerParams(vmem_limit_bytes=SMALL_LIMIT),
        name="tie",
    )(*arrays, *after)


def attend_kernel(
    spaces, frames, columns, row_band, heads, together, groups, skips, fresh, final,
    flags_ref, widths_ref, *refs,
):
    refs = list(refs)
    queries = [refs.pop(0) for unused in range(spaces)]
    arrays = 1 + max(piece[0] for group in groups for piece in group[2])
    keyvals = [refs.pop(0) for unused in range(arrays)]
    state_in = None if fresh else (refs.pop(0), refs.pop(0))
    outs = [refs.pop(0) for unused in range(spaces if final else 2)]
    query_skip, array_skips = skips
    query_ref, key_ref = refs[:2]
    acc_ref, stat_ref = refs[2:] if final else outs
    tokens = queries[0].shape[0]
    frame_now, space_now = lax.axis_index("frame"), lax.axis_index("space")
    scale = math.log2(math.e) / math.sqrt(HEAD_DIM)
    own_column = space_now * (queries[0].shape[-1] // spaces)

    def first_row(offset):
        return lax.rem(space_now - offset + spaces, spaces) * row_band

    def asked_of(group):
        slot, hops = group[:2]
        side = 1 - 2 * lax.rem(frame_now + slot, 2)
        key_frame = frame_now + side * hops
        safe = jnp.clip(key_frame, 0, frames - 1)
        known = (key_frame >= 0) & (key_frame < frames)
        return known & (flags_ref[frame_now, safe] > 0)

    token = lax.broadcasted_iota(jnp.int32, (tokens, HEAD_DIM), 0)
    row = lax.broadcasted_iota(jnp.int32, (tokens, HEAD_DIM), 1)
    starts = [(row - first_row(offset)) * columns for offset in range(spaces)]
    for offset, start in enumerate(starts):
        hit = (token >= start) & (token < start + columns)
        mark = jnp.where(hit, 1.0, 0.0).astype(query_ref.dtype)
        for t in range(together):
            query_ref[t, pl.ds(offset * tokens, tokens), HEAD_DIM:] = mark
    for n, group in enumerate(groups):
        if group[1] > 0:

            @pl.when(asked_of(group))
            def _(n=n, group=group):
                reach = widths_ref[group[1]] * columns
                for m, (unused, unused, offset) in enumerate(group[2]):
                    start = starts[offset]
                    near = (token >= start - reach) & (token < start + columns + reach)
                    fill = jnp.where(near, 0.0, NEG_FILL).astype(key_ref.dtype)
                    for t in range(together):
                        key_ref[n, t, pl.ds(m * tokens, tokens), HEAD_DIM:] = fill

    def attend_heads(turn, carry):
        head = turn * together
        slot_of = (lambda t: t) if final else (lambda t: head + t)

        def lanes(t, skip=0):
            return pl.ds(pl.multiple_of((head + t) * HEAD_DIM + skip, HEAD_DIM), HEAD_DIM)

        def step(t, scores, pieces, old):
            h = slot_of(t)
            top = jnp.max(scores, axis=0, keepdims=True) * scale
            if old:
                before = stat_ref[h, 0:1, :]
                top = jnp.maximum(top, before)
            weights = jnp.exp2(scores * scale - top)
            total = jnp.sum(weights, axis=0, keepdims=True)
            values = jnp.concatenate(
                [keyvals[i][r + 1, :, lanes(t, array_skips[i])] for i, r, o in pieces], axis=0
            )
            acc = lax.dot_general(
                values, weights.astype(jnp.bfloat16), TN, preferred_element_type=jnp.float32
            )
            if old:
                fade = jnp.exp2(before - top)
                total = total + stat_ref[h, 1:2, :] * fade
                acc = acc + acc_ref[h] * fade
            stat_ref[h, 0:1, :] = top
            stat_ref[h, 1:2, :] = total
            acc_ref[h] = acc

        for t in range(together):
            for offset in range(spaces):
                skip = query_skip + (own_column if offset == 0 else 0)
                query_ref[t, pl.ds(offset * tokens, tokens), :HEAD_DIM] = queries[offset][
                    :, lanes(t, skip)
                ]
            if not fresh:
                acc_ref[slot_of(t)] = state_in[0][head + t]
                stat_ref[slot_of(t)] = state_in[1][head + t]

        for n, (slot, hops, pieces) in enumerate(groups):
            if hops == 0:
                scores = []
                for t in range(together):
                    keys = jnp.concatenate(
                        [keyvals[i][r, :, lanes(t, array_skips[i])] for i, r, o in pieces], axis=0
                    )
                    scores.append(
                        lax.dot_general(
                            keys, query_ref[t, :, :HEAD_DIM], NT,
                            preferred_element_type=jnp.float32,
                        )
                    )
                for t in range(together):
                    step(t, scores[t], pieces, False)
                continue

            @pl.when(asked_of(groups[n]))
            def _(n=n, pieces=pieces):
                many = pl.ds(0, len(pieces) * tokens)
                for t in range(together):
                    for m, (i, r, unused) in enumerate(pieces):
                        key_ref[n, t, pl.ds(m * tokens, tokens), :HEAD_DIM] = keyvals[i][
                            r, :, lanes(t, array_skips[i])
                        ]
                scores = [
                    lax.dot_general(
                        key_ref[n, t, many], query_ref[t], NT, preferred_element_type=jnp.float32
                    )
                    for t in range(together)
                ]
                for t in range(together):
                    step(t, scores[t], pieces, True)

        if final:
            for t in range(together):
                result = jnp.transpose(acc_ref[t] * (1.0 / stat_ref[t, 1:2, :]))
                for offset in range(spaces):
                    part = result[offset * tokens : (offset + 1) * tokens]
                    outs[offset][:, lanes(t)] = part.astype(outs[offset].dtype)
        return carry

    lax.fori_loop(0, heads // together, attend_heads, 0)


def attend(scalars, queries, groups, state, final, chunk, sizes):
    spaces, frames, columns, row_band, features = sizes
    first, heads = chunk
    tokens = queries[0].shape[0]
    count = spaces * tokens
    together = next(n for n in (3, 2, 1) if heads % n == 0)
    arrays, numbered = [], []
    for slot, hops, pieces in groups:
        listed = []
        for array, row, offset in pieces:
            known = [n for n, x in enumerate(arrays) if x is array]
            if not known:
                known = [len(arrays)]
                arrays.append(array)
            listed.append((known[0], row, offset))
        numbered.append((slot, hops, tuple(listed)))
    skips = (
        first * HEAD_DIM,
        tuple(first * HEAD_DIM if x.shape[-1] != heads * HEAD_DIM else 0 for x in arrays),
    )
    operands = list(queries) + arrays + (list(state) if state is not None else [])
    state_shape = [(heads, HEAD_DIM, count), (heads, 8, count)]
    if final:
        out_shape = [jax.ShapeDtypeStruct((tokens, heads * HEAD_DIM), jnp.bfloat16)] * spaces
    else:
        out_shape = [jax.ShapeDtypeStruct(shape, jnp.float32) for shape in state_shape]
    scratch = [
        pltpu.VMEM((together, count, 2 * HEAD_DIM), jnp.bfloat16),
        pltpu.VMEM((len(groups), together, count, 2 * HEAD_DIM), jnp.bfloat16),
    ]
    if final:
        scratch += [pltpu.VMEM((together,) + shape[1:], jnp.float32) for shape in state_shape]
    pairs = heads * count * tokens * sum(len(pieces) for slot, hops, pieces in groups)
    return pl.pallas_call(
        functools.partial(
            attend_kernel, spaces, frames, columns, row_band, heads, together,
            tuple(numbered), skips, state is None, final,
        ),
        in_specs=[pl.BlockSpec(memory_space=pltpu.SMEM)] * 2
        + [pl.BlockSpec(memory_space=pltpu.VMEM)] * len(operands),
        out_specs=[pl.BlockSpec(memory_space=pltpu.VMEM)] * len(out_shape),
        out_shape=out_shape,
        scratch_shapes=scratch,
        compiler_params=pltpu.CompilerParams(vmem_limit_bytes=VMEM_LIMIT),
        cost_estimate=pl.CostEstimate(
            flops=4 * pairs * HEAD_DIM,
            bytes_accessed=8 * count * heads * HEAD_DIM,
            transcendentals=pairs,
        ),
        name="attend_final" if final else "attend",
    )(*scalars, *operands)


def join_kernel(first, parts, *refs):
    arrays, outs = refs[: -len(parts)], refs[-len(parts) :]
    for out_ref, part in zip(outs, parts):
        row, width = 0, out_ref.shape[-1]
        for n in part:
            rows = arrays[n].shape[0]
            skip = first if arrays[n].shape[-1] != width else 0
            out_ref[pl.ds(row, rows)] = arrays[n][:, :, pl.ds(skip, width)]
            row += rows


def join(arrays, parts, chunk):
    first, heads = chunk
    tokens = arrays[0].shape[1]

    def rows(part):
        return sum(arrays[n].shape[0] for n in part)

    return pl.pallas_call(
        functools.partial(join_kernel, first * HEAD_DIM, parts),
        in_specs=[pl.BlockSpec(memory_space=pltpu.VMEM)] * len(arrays),
        out_specs=[pl.BlockSpec(memory_space=pltpu.VMEM)] * len(parts),
        out_shape=[
            jax.ShapeDtypeStruct((rows(part), tokens, heads * HEAD_DIM), arrays[0].dtype)
            for part in parts
        ],
        compiler_params=pltpu.CompilerParams(vmem_limit_bytes=SMALL_LIMIT),
        name="join",
    )(*arrays)


def put_kernel(spaces, places, *refs):
    pieces, out_ref, sems = refs[: len(places)], refs[-2], refs[-1]
    share = out_ref.shape[-1] // spaces
    here = lax.axis_index("space")
    copies = []
    for n, (offset, first) in enumerate(places):
        column = pl.multiple_of(lax.rem(here + offset, spaces) * share + first, HEAD_DIM)
        width = pieces[n].shape[-1]
        copy = pltpu.make_async_copy(pieces[n], out_ref.at[:, pl.ds(column, width)], sems.at[n])
        copy.start()
        copies.append(copy)
    for copy in copies:
        copy.wait()


def put(pieces, places, whole, shape, spaces):
    kept = [] if whole is None else [whole]
    return pl.pallas_call(
        functools.partial(put_kernel, spaces, tuple(places)),
        in_specs=[pl.BlockSpec(memory_space=pltpu.VMEM)] * len(pieces)
        + [pl.BlockSpec(memory_space=pl.ANY)] * len(kept),
        out_specs=pl.BlockSpec(memory_space=pl.ANY),
        out_shape=jax.ShapeDtypeStruct(shape, pieces[0].dtype),
        scratch_shapes=[pltpu.SemaphoreType.DMA((len(pieces),))],
        input_output_aliases={len(pieces): 0} if kept else {},
        compiler_params=pltpu.CompilerParams(vmem_limit_bytes=SMALL_LIMIT),
        name="put",
    )(*pieces, *kept)


def shards(spaces, frames, queries, keys, values, flags, widths):
    unused, row_band, columns, features = queries.shape
    tokens = row_band * columns
    width = features // spaces
    heads = width // HEAD_DIM
    scalars = (flags, widths)
    sizes = (spaces, frames, columns, row_band, features)
    q, k, v = (x.reshape(tokens, features) for x in (queries, keys, values))
    half = heads - heads // 2
    chunks = [(0, half), (half, heads - half)]
    offsets = range(1, spaces)

    def along_space(x, offset):
        return lax.ppermute(x, "space", [(s, (s + offset) % spaces) for s in range(spaces)])

    def swap(x, slot):
        pairs = []
        for f in range(frames):
            side = 1 if (f + slot) % 2 == 0 else -1
            if 0 <= f + side < frames:
                pairs.append((f, f + side))
        return lax.ppermute(x, "frame", pairs)

    def swap_both(xs):
        second = swap(xs[1], 1)
        return [swap(xs[0], 0), second]

    blocks = [
        [(offset, first * HEAD_DIM, number * HEAD_DIM) for offset in offsets]
        for first, number in chunks
    ]
    *sends, own = pack((k, v), blocks[0] + [(0, 0, width)], (), spaces, True)
    partners = [[along_space(x, offset) for x, offset in zip(sends, offsets)]]
    firsts = swap_both([own, own])
    sends = pack((k, v), blocks[1], partners[0] + firsts, spaces, False)
    partners.append([along_space(x, offset) for x, offset in zip(sends, offsets)])
    sends = pack((q,), [(offset, 0, width) for offset in offsets], partners[1], spaces, False)
    query_parts = [q] + [along_space(x, offset) for x, offset in zip(sends, offsets)]
    partners[1] = list(tie(partners[1], sends))

    last = frames - 2
    behind = 2 * len(offsets)

    def own_band(message, hops):
        return [(slot, hops, [(x, x.shape[0] - 2, 0)]) for slot, x in enumerate(message)]

    def partner_bands(message, hops):
        return [
            (slot, hops, [(x, 2 * (o - 1), o) for o in offsets]) for slot, x in enumerate(message)
        ]

    seconds = []
    for c, chunk in enumerate(chunks):
        shared = tuple(range(len(offsets)))
        parts = tuple(shared + (len(offsets) + 1 - slot,) for slot in range(2))
        seconds.append(swap_both(join(partners[c] + firsts, parts, chunk)))
    states = []
    for c, chunk in enumerate(chunks):
        pieces = [(own, 0, 0)] + [(x, 0, o) for x, o in zip(partners[c], offsets)]
        groups = [(0, 0, pieces)] + own_band(firsts, 1)
        states.append(attend(scalars, query_parts, groups, None, False, chunk, sizes))

    messages = seconds
    for hops in range(2, frames - 1):
        following = []
        for c, chunk in enumerate(chunks):
            after = [state[1] for state in states[: c + 1]]
            came = list(tie(messages[c], after))
            rows = behind if hops == last else behind + 2
            following.append(swap_both([came[1 - slot][:rows] for slot in range(2)]))
            groups = partner_bands(came, hops - 1) + own_band(came, hops)
            states[c] = attend(scalars, query_parts, groups, states[c], False, chunk, sizes)
        messages = following
    ends = []
    for message in messages:
        came = list(tie(message, [state[1] for state in states]))
        ends.append(partner_bands(came, last))

    kept, returned = [], []
    for c, chunk in enumerate(chunks):
        mine, *parts = attend(scalars, query_parts, ends[c], states[c], True, chunk, sizes)
        kept.append((mine, (0, chunk[0] * HEAD_DIM)))
        for offset, x in zip(offsets, parts):
            returned.append((along_space(x, -offset), (offset, chunk[0] * HEAD_DIM)))
    late = len(returned) - len(offsets)
    result = None
    for batch in (kept + returned[:late], returned[late:]):
        pieces, places = zip(*batch)
        result = put(pieces, places, result, q.shape, spaces)
    return result.reshape(queries.shape)


def solution(mesh):
    placed = P(("group", "frame"), "space", None, "head")
    return jax.shard_map(
        functools.partial(shards, mesh.shape["space"], mesh.shape["frame"]),
        mesh=mesh,
        in_specs=(placed, placed, placed, P(), P()),
        out_specs=placed,
        check_vma=False,
    )
```

```python
import functools
import math

import jax
import jax.numpy as jnp
from jax import lax
from jax.experimental import pallas as pl
from jax.experimental.pallas import tpu as pltpu
from jax.sharding import PartitionSpec as P

HEAD_DIM = 128
NEG_FILL = -1e30
VMEM_LIMIT = 16 * 1024 * 1024
SMALL_LIMIT = 2 * 1024 * 1024
STAGED_LIMIT = 60 * 1024 * 1024
ROW_GROUPS = 4
NT = (((1,), (1,)), ((), ()))
TN = (((0,), (0,)), ((), ()))


def pack_kernel(spaces, jobs, staged, *refs):
    refs = list(refs)
    halfway = refs[len(refs) - len(jobs) - 1 : -1] if staged else []
    sems = refs[-1]
    here = lax.axis_index("space")
    tokens = refs[0].shape[0]
    groups = ROW_GROUPS if staged else 1
    first_copies, second_copies = [], []
    for n, (source, offset, first, width, target, row) in enumerate(jobs):
        share = refs[source].shape[-1] // spaces
        column = pl.multiple_of(lax.rem(here + offset, spaces) * share + first, HEAD_DIM)
        out = refs[target] if row is None else refs[target].at[row]
        for g in range(groups):
            rows = pl.ds(g * (tokens // groups), tokens // groups)
            origin = refs[source].at[rows, pl.ds(column, width)]
            stop = halfway[n].at[rows] if staged else out.at[rows]
            copy = pltpu.make_async_copy(origin, stop, sems.at[0, n * groups + g])
            copy.start()
            first_copies.append(copy)
            if staged:
                second_copies.append(
                    pltpu.make_async_copy(stop, out.at[rows], sems.at[1, n * groups + g])
                )
    for n, copy in enumerate(first_copies):
        copy.wait()
        if staged:
            second_copies[n].start()
    for copy in second_copies:
        copy.wait()


def pack(sources, blocks, after, spaces, staged):
    tokens = sources[0].shape[0]
    several = len(sources) > 1
    jobs, shapes = [], []
    first_out = len(sources) + len(after)
    for n, (offset, first, width) in enumerate(blocks):
        lead = (len(sources),) if several else ()
        shapes.append(jax.ShapeDtypeStruct(lead + (tokens, width), sources[0].dtype))
        for row in range(len(sources)):
            jobs.append((row, offset, first, width, first_out + n, row if several else None))
    halfway = [pltpu.VMEM((tokens, job[3]), sources[0].dtype) for job in jobs]
    space = pl.ANY if staged else pltpu.VMEM
    return pl.pallas_call(
        functools.partial(pack_kernel, spaces, tuple(jobs), staged),
        in_specs=[pl.BlockSpec(memory_space=pl.ANY)] * first_out,
        out_specs=[pl.BlockSpec(memory_space=space)] * len(shapes),
        out_shape=shapes,
        scratch_shapes=(halfway if staged else [])
        + [pltpu.SemaphoreType.DMA((2, ROW_GROUPS * len(jobs)))],
        compiler_params=pltpu.CompilerParams(
            vmem_limit_bytes=STAGED_LIMIT if staged else SMALL_LIMIT
        ),
        name="pack",
    )(*sources, *after)


def tie(arrays, after):
    return pl.pallas_call(
        lambda *refs: None,
        in_specs=[pl.BlockSpec(memory_space=pl.ANY)] * (len(arrays) + len(after)),
        out_specs=[pl.BlockSpec(memory_space=pl.ANY)] * len(arrays),
        out_shape=[jax.ShapeDtypeStruct(x.shape, x.dtype) for x in arrays],
        input_output_aliases={n: n for n in range(len(arrays))},
        compiler_params=pltpu.CompilerParams(vmem_limit_bytes=SMALL_LIMIT),
        name="tie",
    )(*arrays, *after)


def attend_kernel(
    spaces, frames, columns, row_band, heads, together, groups, skips, fresh, final,
    flags_ref, widths_ref, *refs,
):
    refs = list(refs)
    queries = [refs.pop(0) for unused in range(spaces)]
    arrays = 1 + max(piece[0] for group in groups for piece in group[2])
    keyvals = [refs.pop(0) for unused in range(arrays)]
    state_in = None if fresh else (refs.pop(0), refs.pop(0))
    outs = [refs.pop(0) for unused in range(spaces if final else 2)]
    query_ref, key_ref = refs[:2]
    acc_ref, stat_ref = refs[2:] if final else outs
    tokens = queries[0].shape[0]
    frame_now, space_now = lax.axis_index("frame"), lax.axis_index("space")
    scale = math.log2(math.e) / math.sqrt(HEAD_DIM)
    own_column = space_now * (queries[0].shape[-1] // spaces)

    def first_row(offset):
        return lax.rem(space_now - offset + spaces, spaces) * row_band

    def asked_of(group):
        slot, hops = group[:2]
        side = 1 - 2 * lax.rem(frame_now + slot, 2)
        key_frame = frame_now + side * hops
        safe = jnp.clip(key_frame, 0, frames - 1)
        known = (key_frame >= 0) & (key_frame < frames)
        return known & (flags_ref[frame_now, safe] > 0)

    token = lax.broadcasted_iota(jnp.int32, (tokens, HEAD_DIM), 0)
    row = lax.broadcasted_iota(jnp.int32, (tokens, HEAD_DIM), 1)
    starts = [(row - first_row(offset)) * columns for offset in range(spaces)]
    for offset, start in enumerate(starts):
        hit = (token >= start) & (token < start + columns)
        mark = jnp.where(hit, 1.0, 0.0).astype(query_ref.dtype)
        for t in range(together):
            query_ref[t, pl.ds(offset * tokens, tokens), HEAD_DIM:] = mark
    for n, group in enumerate(groups):
        if group[1] > 0:

            @pl.when(asked_of(group))
            def _(n=n, group=group):
                reach = widths_ref[group[1]] * columns
                for m, (unused, unused, offset) in enumerate(group[2]):
                    start = starts[offset]
                    near = (token >= start - reach) & (token < start + columns + reach)
                    fill = jnp.where(near, 0.0, NEG_FILL).astype(key_ref.dtype)
                    for t in range(together):
                        key_ref[n, t, pl.ds(m * tokens, tokens), HEAD_DIM:] = fill

    def attend_heads(turn, carry):
        head = turn * together
        slot_of = (lambda t: t) if final else (lambda t: head + t)

        def lanes(t, skip=0):
            return pl.ds(pl.multiple_of((head + t) * HEAD_DIM + skip, HEAD_DIM), HEAD_DIM)

        def step(t, scores, pieces, old):
            h = slot_of(t)
            top = jnp.max(scores, axis=0, keepdims=True) * scale
            if old:
                before = stat_ref[h, 0:1, :]
                top = jnp.maximum(top, before)
            weights = jnp.exp2(scores * scale - top)
            total = jnp.sum(weights, axis=0, keepdims=True)
            values = jnp.concatenate([keyvals[i][r + 1, :, lanes(t)] for i, r, o in pieces], axis=0)
            acc = lax.dot_general(
                values, weights.astype(jnp.bfloat16), TN, preferred_element_type=jnp.float32
            )
            if old:
                fade = jnp.exp2(before - top)
                total = total + stat_ref[h, 1:2, :] * fade
                acc = acc + acc_ref[h] * fade
            stat_ref[h, 0:1, :] = top
            stat_ref[h, 1:2, :] = total
            acc_ref[h] = acc

        for t in range(together):
            for offset in range(spaces):
                skip = skips[offset] + (own_column if offset == 0 else 0)
                query_ref[t, pl.ds(offset * tokens, tokens), :HEAD_DIM] = queries[offset][
                    :, lanes(t, skip)
                ]
            if not fresh:
                acc_ref[slot_of(t)] = state_in[0][head + t]
                stat_ref[slot_of(t)] = state_in[1][head + t]

        for n, (slot, hops, pieces) in enumerate(groups):
            if hops == 0:
                scores = []
                for t in range(together):
                    keys = jnp.concatenate(
                        [keyvals[i][r, :, lanes(t)] for i, r, o in pieces], axis=0
                    )
                    scores.append(
                        lax.dot_general(
                            keys, query_ref[t, :, :HEAD_DIM], NT,
                            preferred_element_type=jnp.float32,
                        )
                    )
                for t in range(together):
                    step(t, scores[t], pieces, False)
                continue

            @pl.when(asked_of(groups[n]))
            def _(n=n, pieces=pieces):
                many = pl.ds(0, len(pieces) * tokens)
                for t in range(together):
                    for m, (i, r, unused) in enumerate(pieces):
                        key_ref[n, t, pl.ds(m * tokens, tokens), :HEAD_DIM] = keyvals[i][
                            r, :, lanes(t)
                        ]
                scores = [
                    lax.dot_general(
                        key_ref[n, t, many], query_ref[t], NT, preferred_element_type=jnp.float32
                    )
                    for t in range(together)
                ]
                for t in range(together):
                    step(t, scores[t], pieces, True)

        if final:
            for t in range(together):
                result = jnp.transpose(acc_ref[t] * (1.0 / stat_ref[t, 1:2, :]))
                for offset in range(spaces):
                    part = result[offset * tokens : (offset + 1) * tokens]
                    outs[offset][:, lanes(t)] = part.astype(outs[offset].dtype)
        return carry

    lax.fori_loop(0, heads // together, attend_heads, 0)


def attend(scalars, queries, groups, state, final, chunk, sizes):
    spaces, frames, columns, row_band, features = sizes
    first, heads = chunk
    tokens = queries[0].shape[0]
    count = spaces * tokens
    together = next(n for n in (3, 2, 1) if heads % n == 0)
    arrays, numbered = [], []
    for slot, hops, pieces in groups:
        listed = []
        for array, row, offset in pieces:
            known = [n for n, x in enumerate(arrays) if x is array]
            if not known:
                known = [len(arrays)]
                arrays.append(array)
            listed.append((known[0], row, offset))
        numbered.append((slot, hops, tuple(listed)))
    operands = list(queries) + arrays + (list(state) if state is not None else [])
    state_shape = [(heads, HEAD_DIM, count), (heads, 8, count)]
    if final:
        out_shape = [jax.ShapeDtypeStruct((tokens, heads * HEAD_DIM), jnp.bfloat16)] * spaces
    else:
        out_shape = [jax.ShapeDtypeStruct(shape, jnp.float32) for shape in state_shape]
    scratch = [
        pltpu.VMEM((together, count, 2 * HEAD_DIM), jnp.bfloat16),
        pltpu.VMEM((len(groups), together, count, 2 * HEAD_DIM), jnp.bfloat16),
    ]
    if final:
        scratch += [pltpu.VMEM((together,) + shape[1:], jnp.float32) for shape in state_shape]
    pairs = heads * count * tokens * sum(len(pieces) for slot, hops, pieces in groups)
    return pl.pallas_call(
        functools.partial(
            attend_kernel, spaces, frames, columns, row_band, heads, together,
            tuple(numbered), (first * HEAD_DIM,) * spaces, state is None, final,
        ),
        in_specs=[pl.BlockSpec(memory_space=pltpu.SMEM)] * 2
        + [pl.BlockSpec(memory_space=pltpu.VMEM)] * len(operands),
        out_specs=[pl.BlockSpec(memory_space=pltpu.VMEM)] * len(out_shape),
        out_shape=out_shape,
        scratch_shapes=scratch,
        compiler_params=pltpu.CompilerParams(vmem_limit_bytes=VMEM_LIMIT),
        cost_estimate=pl.CostEstimate(
            flops=4 * pairs * HEAD_DIM,
            bytes_accessed=8 * count * heads * HEAD_DIM,
            transcendentals=pairs,
        ),
        name="attend_final" if final else "attend",
    )(*scalars, *operands)


def join_kernel(parts, *refs):
    arrays, outs = refs[: -len(parts)], refs[-len(parts) :]
    for out_ref, part in zip(outs, parts):
        row = 0
        for n in part:
            rows = arrays[n].shape[0]
            out_ref[pl.ds(row, rows)] = arrays[n][...]
            row += rows


def join(arrays, parts):
    def rows(part):
        return sum(arrays[n].shape[0] for n in part)

    return pl.pallas_call(
        functools.partial(join_kernel, parts),
        in_specs=[pl.BlockSpec(memory_space=pltpu.VMEM)] * len(arrays),
        out_specs=[pl.BlockSpec(memory_space=pltpu.VMEM)] * len(parts),
        out_shape=[
            jax.ShapeDtypeStruct((rows(part),) + arrays[0].shape[1:], arrays[0].dtype)
            for part in parts
        ],
        compiler_params=pltpu.CompilerParams(vmem_limit_bytes=SMALL_LIMIT),
        name="join",
    )(*arrays)


def put_kernel(spaces, places, *refs):
    pieces, out_ref, sems = refs[: len(places)], refs[-2], refs[-1]
    share = out_ref.shape[-1] // spaces
    here = lax.axis_index("space")
    copies = []
    for n, (offset, first) in enumerate(places):
        column = pl.multiple_of(lax.rem(here + offset, spaces) * share + first, HEAD_DIM)
        width = pieces[n].shape[-1]
        copy = pltpu.make_async_copy(pieces[n], out_ref.at[:, pl.ds(column, width)], sems.at[n])
        copy.start()
        copies.append(copy)
    for copy in copies:
        copy.wait()


def put(pieces, places, whole, shape, spaces):
    kept = [] if whole is None else [whole]
    return pl.pallas_call(
        functools.partial(put_kernel, spaces, tuple(places)),
        in_specs=[pl.BlockSpec(memory_space=pltpu.VMEM)] * len(pieces)
        + [pl.BlockSpec(memory_space=pl.ANY)] * len(kept),
        out_specs=pl.BlockSpec(memory_space=pl.ANY),
        out_shape=jax.ShapeDtypeStruct(shape, pieces[0].dtype),
        scratch_shapes=[pltpu.SemaphoreType.DMA((len(pieces),))],
        input_output_aliases={len(pieces): 0} if kept else {},
        compiler_params=pltpu.CompilerParams(vmem_limit_bytes=SMALL_LIMIT),
        name="put",
    )(*pieces, *kept)


def shards(spaces, frames, queries, keys, values, flags, widths):
    unused, row_band, columns, features = queries.shape
    tokens = row_band * columns
    width = features // spaces
    heads = width // HEAD_DIM
    scalars = (flags, widths)
    sizes = (spaces, frames, columns, row_band, features)
    q, k, v = (x.reshape(tokens, features) for x in (queries, keys, values))
    half = heads - heads // 2
    chunks = [(0, half), (half, heads - half)]
    offsets = range(1, spaces)

    def along_space(x, offset):
        return lax.ppermute(x, "space", [(s, (s + offset) % spaces) for s in range(spaces)])

    def swap(x, slot):
        pairs = []
        for f in range(frames):
            side = 1 if (f + slot) % 2 == 0 else -1
            if 0 <= f + side < frames:
                pairs.append((f, f + side))
        return lax.ppermute(x, "frame", pairs)

    def swap_both(xs):
        second = swap(xs[1], 1)
        return [swap(xs[0], 0), second]

    own, partners, arrived = [], [], []
    for c, (first, number) in enumerate(chunks):
        blocks = [(offset, first * HEAD_DIM, number * HEAD_DIM) for offset in offsets]
        if c == 0:
            mine = [(0, f * HEAD_DIM, n * HEAD_DIM) for f, n in chunks]
            packed = pack((k, v), blocks + mine, (), spaces, True)
            sends, own = packed[: len(blocks)], packed[len(blocks) :]
        else:
            sends = pack((k, v), blocks, arrived, spaces, False)
        arrived = [along_space(x, offset) for x, offset in zip(sends, offsets)]
        partners.append(arrived)
    sends = pack((q,), [(offset, 0, width) for offset in offsets], arrived, spaces, False)
    query_parts = [q] + [along_space(x, offset) for x, offset in zip(sends, offsets)]
    partners[1] = list(tie(partners[1], sends))

    last = frames - 2
    behind = 2 * len(offsets)

    def own_band(message, hops):
        return [(slot, hops, [(x, x.shape[0] - 2, 0)]) for slot, x in enumerate(message)]

    def partner_bands(message, hops):
        return [
            (slot, hops, [(x, 2 * (o - 1), o) for o in offsets]) for slot, x in enumerate(message)
        ]

    firsts = [swap_both([x, x]) for x in own]
    seconds = []
    for c in range(len(chunks)):
        shared = tuple(range(len(offsets)))
        parts = tuple(shared + (len(offsets) + 1 - slot,) for slot in range(2))
        seconds.append(swap_both(join(partners[c] + firsts[c], parts)))
    states = []
    for c, chunk in enumerate(chunks):
        pieces = [(own[c], 0, 0)] + [(x, 0, o) for x, o in zip(partners[c], offsets)]
        groups = [(0, 0, pieces)] + own_band(firsts[c], 1)
        states.append(attend(scalars, query_parts, groups, None, False, chunk, sizes))

    messages = seconds
    for hops in range(2, frames - 1):
        following = []
        for c, chunk in enumerate(chunks):
            after = [state[1] for state in states[: c + 1]]
            came = list(tie(messages[c][::-1], after))[::-1]
            rows = behind if hops == last else behind + 2
            following.append(swap_both([came[1 - slot][:rows] for slot in range(2)]))
            groups = partner_bands(came, hops - 1) + own_band(came, hops)
            states[c] = attend(scalars, query_parts, groups, states[c], False, chunk, sizes)
        messages = following
    ends = []
    for message in messages:
        came = list(tie(message, [state[1] for state in states]))
        ends.append(partner_bands(came, last))

    own, returned = [], []
    for c, chunk in enumerate(chunks):
        kept, *parts = attend(scalars, query_parts, ends[c], states[c], True, chunk, sizes)
        own.append((kept, (0, chunk[0] * HEAD_DIM)))
        for offset, x in zip(offsets, parts):
            returned.append((along_space(x, -offset), (offset, chunk[0] * HEAD_DIM)))
    late = len(returned) - len(offsets)
    result = None
    for batch in (own + returned[:late], returned[late:]):
        pieces, places = zip(*batch)
        result = put(pieces, places, result, q.shape, spaces)
    return result.reshape(queries.shape)


def solution(mesh):
    placed = P(("group", "frame"), "space", None, "head")
    return jax.shard_map(
        functools.partial(shards, mesh.shape["space"], mesh.shape["frame"]),
        mesh=mesh,
        in_specs=(placed, placed, placed, P(), P()),
        out_specs=placed,
        check_vma=False,
    )
```

```python
import functools
import math

import jax
import jax.numpy as jnp
from jax import lax
from jax.experimental import pallas as pl
from jax.experimental.pallas import tpu as pltpu
from jax.sharding import PartitionSpec as P

HEAD_DIM = 128
NEG_FILL = -1e30
VMEM_LIMIT = 16 * 1024 * 1024
SMALL_LIMIT = 2 * 1024 * 1024
STAGED_LIMIT = 60 * 1024 * 1024
ROW_GROUPS = 4
NT = (((1,), (1,)), ((), ()))
TN = (((0,), (0,)), ((), ()))


def pack_kernel(spaces, jobs, staged, *refs):
    refs = list(refs)
    halfway = refs[len(refs) - len(jobs) - 1 : -1] if staged else []
    sems = refs[-1]
    here = lax.axis_index("space")
    tokens = refs[0].shape[0]
    groups = ROW_GROUPS if staged else 1
    first_copies, second_copies = [], []
    for n, (source, offset, first, width, target, row) in enumerate(jobs):
        share = refs[source].shape[-1] // spaces
        column = pl.multiple_of(lax.rem(here + offset, spaces) * share + first, HEAD_DIM)
        out = refs[target] if row is None else refs[target].at[row]
        for g in range(groups):
            rows = pl.ds(g * (tokens // groups), tokens // groups)
            origin = refs[source].at[rows, pl.ds(column, width)]
            stop = halfway[n].at[rows] if staged else out.at[rows]
            copy = pltpu.make_async_copy(origin, stop, sems.at[0, n * groups + g])
            copy.start()
            first_copies.append(copy)
            if staged:
                second_copies.append(
                    pltpu.make_async_copy(stop, out.at[rows], sems.at[1, n * groups + g])
                )
    for n, copy in enumerate(first_copies):
        copy.wait()
        if staged:
            second_copies[n].start()
    for copy in second_copies:
        copy.wait()


def pack(sources, blocks, after, spaces, staged):
    tokens = sources[0].shape[0]
    several = len(sources) > 1
    jobs, shapes = [], []
    first_out = len(sources) + len(after)
    for n, (offset, first, width) in enumerate(blocks):
        lead = (len(sources),) if several else ()
        shapes.append(jax.ShapeDtypeStruct(lead + (tokens, width), sources[0].dtype))
        for row in range(len(sources)):
            jobs.append((row, offset, first, width, first_out + n, row if several else None))
    halfway = [pltpu.VMEM((tokens, job[3]), sources[0].dtype) for job in jobs]
    space = pl.ANY if staged else pltpu.VMEM
    return pl.pallas_call(
        functools.partial(pack_kernel, spaces, tuple(jobs), staged),
        in_specs=[pl.BlockSpec(memory_space=pl.ANY)] * first_out,
        out_specs=[pl.BlockSpec(memory_space=space)] * len(shapes),
        out_shape=shapes,
        scratch_shapes=(halfway if staged else [])
        + [pltpu.SemaphoreType.DMA((2, ROW_GROUPS * len(jobs)))],
        compiler_params=pltpu.CompilerParams(
            vmem_limit_bytes=STAGED_LIMIT if staged else SMALL_LIMIT
        ),
        name="pack",
    )(*sources, *after)


def tie(arrays, after):
    return pl.pallas_call(
        lambda *refs: None,
        in_specs=[pl.BlockSpec(memory_space=pl.ANY)] * (len(arrays) + len(after)),
        out_specs=[pl.BlockSpec(memory_space=pl.ANY)] * len(arrays),
        out_shape=[jax.ShapeDtypeStruct(x.shape, x.dtype) for x in arrays],
        input_output_aliases={n: n for n in range(len(arrays))},
        compiler_params=pltpu.CompilerParams(vmem_limit_bytes=SMALL_LIMIT),
        name="tie",
    )(*arrays, *after)


def attend_kernel(
    spaces, frames, columns, row_band, heads, together, groups, query_skip, fresh, final,
    flags_ref, widths_ref, *refs,
):
    refs = list(refs)
    queries = [refs.pop(0) for unused in range(spaces)]
    arrays = 1 + max(piece[0] for group in groups for piece in group[2])
    keyvals = [refs.pop(0) for unused in range(arrays)]
    state_in = None if fresh else (refs.pop(0), refs.pop(0))
    outs = [refs.pop(0) for unused in range(spaces if final else 2)]
    query_ref, key_ref = refs[:2]
    acc_ref, stat_ref = refs[2:] if final else outs
    tokens = queries[0].shape[0]
    frame_now, space_now = lax.axis_index("frame"), lax.axis_index("space")
    scale = math.log2(math.e) / math.sqrt(HEAD_DIM)
    own_column = space_now * (queries[0].shape[-1] // spaces)

    def first_row(offset):
        return lax.rem(space_now - offset + spaces, spaces) * row_band

    def asked_of(group):
        slot, hops = group[:2]
        side = 1 - 2 * lax.rem(frame_now + slot, 2)
        key_frame = frame_now + side * hops
        safe = jnp.clip(key_frame, 0, frames - 1)
        known = (key_frame >= 0) & (key_frame < frames)
        return known & (flags_ref[frame_now, safe] > 0)

    token = lax.broadcasted_iota(jnp.int32, (tokens, HEAD_DIM), 0)
    row = lax.broadcasted_iota(jnp.int32, (tokens, HEAD_DIM), 1)
    starts = [(row - first_row(offset)) * columns for offset in range(spaces)]
    for offset, start in enumerate(starts):
        hit = (token >= start) & (token < start + columns)
        mark = jnp.where(hit, 1.0, 0.0).astype(query_ref.dtype)
        for t in range(together):
            query_ref[t, pl.ds(offset * tokens, tokens), HEAD_DIM:] = mark
    for n, group in enumerate(groups):
        if group[1] > 0:

            @pl.when(asked_of(group))
            def _(n=n, group=group):
                reach = widths_ref[group[1]] * columns
                for m, (unused, unused, offset) in enumerate(group[2]):
                    start = starts[offset]
                    near = (token >= start - reach) & (token < start + columns + reach)
                    fill = jnp.where(near, 0.0, NEG_FILL).astype(key_ref.dtype)
                    for t in range(together):
                        key_ref[n, t, pl.ds(m * tokens, tokens), HEAD_DIM:] = fill

    def attend_heads(turn, carry):
        head = turn * together
        slot_of = (lambda t: t) if final else (lambda t: head + t)

        def lanes(t, skip=0):
            return pl.ds(pl.multiple_of((head + t) * HEAD_DIM + skip, HEAD_DIM), HEAD_DIM)

        def step(t, scores, pieces, old):
            h = slot_of(t)
            top = jnp.max(scores, axis=0, keepdims=True) * scale
            if old:
                before = stat_ref[h, 0:1, :]
                top = jnp.maximum(top, before)
            weights = jnp.exp2(scores * scale - top)
            total = jnp.sum(weights, axis=0, keepdims=True)
            values = jnp.concatenate(
                [keyvals[i][r + 1, :, lanes(t)] for i, r, o in pieces], axis=0
            )
            acc = lax.dot_general(
                values, weights.astype(jnp.bfloat16), TN, preferred_element_type=jnp.float32
            )
            if old:
                fade = jnp.exp2(before - top)
                total = total + stat_ref[h, 1:2, :] * fade
                acc = acc + acc_ref[h] * fade
            stat_ref[h, 0:1, :] = top
            stat_ref[h, 1:2, :] = total
            acc_ref[h] = acc

        for t in range(together):
            for offset in range(spaces):
                skip = query_skip + (own_column if offset == 0 else 0)
                query_ref[t, pl.ds(offset * tokens, tokens), :HEAD_DIM] = queries[offset][
                    :, lanes(t, skip)
                ]
            if not fresh:
                acc_ref[slot_of(t)] = state_in[0][head + t]
                stat_ref[slot_of(t)] = state_in[1][head + t]

        for n, (slot, hops, pieces) in enumerate(groups):
            if hops == 0:
                scores = []
                for t in range(together):
                    keys = jnp.concatenate(
                        [keyvals[i][r, :, lanes(t)] for i, r, o in pieces], axis=0
                    )
                    scores.append(
                        lax.dot_general(
                            keys, query_ref[t, :, :HEAD_DIM], NT,
                            preferred_element_type=jnp.float32,
                        )
                    )
                for t in range(together):
                    step(t, scores[t], pieces, False)
                continue

            @pl.when(asked_of(groups[n]))
            def _(n=n, pieces=pieces):
                many = pl.ds(0, len(pieces) * tokens)
                for t in range(together):
                    for m, (i, r, unused) in enumerate(pieces):
                        key_ref[n, t, pl.ds(m * tokens, tokens), :HEAD_DIM] = keyvals[i][
                            r, :, lanes(t)
                        ]
                scores = [
                    lax.dot_general(
                        key_ref[n, t, many], query_ref[t], NT, preferred_element_type=jnp.float32
                    )
                    for t in range(together)
                ]
                for t in range(together):
                    step(t, scores[t], pieces, True)

        if final:
            for t in range(together):
                result = jnp.transpose(acc_ref[t] * (1.0 / stat_ref[t, 1:2, :]))
                for offset in range(spaces):
                    part = result[offset * tokens : (offset + 1) * tokens]
                    outs[offset][:, lanes(t)] = part.astype(outs[offset].dtype)
        return carry

    lax.fori_loop(0, heads // together, attend_heads, 0)


def attend(scalars, queries, groups, state, final, chunk, sizes):
    spaces, frames, columns, row_band, features = sizes
    first, heads = chunk
    tokens = queries[0].shape[0]
    count = spaces * tokens
    together = next(n for n in (3, 2, 1) if heads % n == 0)
    arrays, numbered = [], []
    for slot, hops, pieces in groups:
        listed = []
        for array, row, offset in pieces:
            known = [n for n, x in enumerate(arrays) if x is array]
            if not known:
                known = [len(arrays)]
                arrays.append(array)
            listed.append((known[0], row, offset))
        numbered.append((slot, hops, tuple(listed)))
    operands = list(queries) + arrays + (list(state) if state is not None else [])
    state_shape = [(heads, HEAD_DIM, count), (heads, 8, count)]
    if final:
        out_shape = [jax.ShapeDtypeStruct((tokens, heads * HEAD_DIM), jnp.bfloat16)] * spaces
    else:
        out_shape = [jax.ShapeDtypeStruct(shape, jnp.float32) for shape in state_shape]
    scratch = [
        pltpu.VMEM((together, count, 2 * HEAD_DIM), jnp.bfloat16),
        pltpu.VMEM((len(groups), together, count, 2 * HEAD_DIM), jnp.bfloat16),
    ]
    if final:
        scratch += [pltpu.VMEM((together,) + shape[1:], jnp.float32) for shape in state_shape]
    pairs = heads * count * tokens * sum(len(pieces) for slot, hops, pieces in groups)
    return pl.pallas_call(
        functools.partial(
            attend_kernel, spaces, frames, columns, row_band, heads, together,
            tuple(numbered), first * HEAD_DIM, state is None, final,
        ),
        in_specs=[pl.BlockSpec(memory_space=pltpu.SMEM)] * 2
        + [pl.BlockSpec(memory_space=pltpu.VMEM)] * len(operands),
        out_specs=[pl.BlockSpec(memory_space=pltpu.VMEM)] * len(out_shape),
        out_shape=out_shape,
        scratch_shapes=scratch,
        compiler_params=pltpu.CompilerParams(vmem_limit_bytes=VMEM_LIMIT),
        cost_estimate=pl.CostEstimate(
            flops=4 * pairs * HEAD_DIM,
            bytes_accessed=8 * count * heads * HEAD_DIM,
            transcendentals=pairs,
        ),
        name="attend_final" if final else "attend",
    )(*scalars, *operands)


def join_kernel(outs_copies, *refs):
    arrays, outs = refs[: -len(outs_copies)], refs[-len(outs_copies) :]
    for out_ref, copies in zip(outs, outs_copies):
        for n, lane, width, row, column in copies:
            rows = pl.ds(row, arrays[n].shape[0])
            out_ref[rows, :, pl.ds(column, width)] = arrays[n][:, :, pl.ds(lane, width)]


def join(arrays, outs_copies, rows, width):
    shape = jax.ShapeDtypeStruct((rows, arrays[0].shape[1], width), arrays[0].dtype)
    return pl.pallas_call(
        functools.partial(join_kernel, outs_copies),
        in_specs=[pl.BlockSpec(memory_space=pltpu.VMEM)] * len(arrays),
        out_specs=[pl.BlockSpec(memory_space=pltpu.VMEM)] * len(outs_copies),
        out_shape=[shape] * len(outs_copies),
        compiler_params=pltpu.CompilerParams(vmem_limit_bytes=SMALL_LIMIT),
        name="join",
    )(*arrays)


def put_kernel(spaces, places, *refs):
    pieces, out_ref, sems = refs[: len(places)], refs[-2], refs[-1]
    share = out_ref.shape[-1] // spaces
    here = lax.axis_index("space")
    copies = []
    for n, (offset, first) in enumerate(places):
        column = pl.multiple_of(lax.rem(here + offset, spaces) * share + first, HEAD_DIM)
        width = pieces[n].shape[-1]
        copy = pltpu.make_async_copy(pieces[n], out_ref.at[:, pl.ds(column, width)], sems.at[n])
        copy.start()
        copies.append(copy)
    for copy in copies:
        copy.wait()


def put(pieces, places, whole, shape, spaces):
    kept = [] if whole is None else [whole]
    return pl.pallas_call(
        functools.partial(put_kernel, spaces, tuple(places)),
        in_specs=[pl.BlockSpec(memory_space=pltpu.VMEM)] * len(pieces)
        + [pl.BlockSpec(memory_space=pl.ANY)] * len(kept),
        out_specs=pl.BlockSpec(memory_space=pl.ANY),
        out_shape=jax.ShapeDtypeStruct(shape, pieces[0].dtype),
        scratch_shapes=[pltpu.SemaphoreType.DMA((len(pieces),))],
        input_output_aliases={len(pieces): 0} if kept else {},
        compiler_params=pltpu.CompilerParams(vmem_limit_bytes=SMALL_LIMIT),
        name="put",
    )(*pieces, *kept)


def shards(spaces, frames, queries, keys, values, flags, widths):
    unused, row_band, columns, features = queries.shape
    tokens = row_band * columns
    width = features // spaces
    heads = width // HEAD_DIM
    scalars = (flags, widths)
    sizes = (spaces, frames, columns, row_band, features)
    q, k, v = (x.reshape(tokens, features) for x in (queries, keys, values))
    half = heads - heads // 2
    chunks = [(0, half), (half, heads - half)]
    offsets = range(1, spaces)

    def along_space(x, offset):
        return lax.ppermute(x, "space", [(s, (s + offset) % spaces) for s in range(spaces)])

    def swap(x, slot):
        pairs = []
        for f in range(frames):
            side = 1 if (f + slot) % 2 == 0 else -1
            if 0 <= f + side < frames:
                pairs.append((f, f + side))
        return lax.ppermute(x, "frame", pairs)

    def swap_both(xs):
        second = swap(xs[1], 1)
        return [swap(xs[0], 0), second]

    def blocks_of(chunk, which):
        return [(offset, chunk[0] * HEAD_DIM, chunk[1] * HEAD_DIM) for offset in which]

    large = heads - heads // 3
    cuts = [(0, large), (large, heads - large)]
    packed = pack(
        (k, v), blocks_of(chunks[0], offsets) + [blocks_of(cut, (0,))[0] for cut in cuts],
        (), spaces, True,
    )
    sends, sources = packed[: len(offsets)], packed[len(offsets) :]
    partners = [[along_space(x, offset) for x, offset in zip(sends, offsets)]]
    firsts = [swap_both([x, x]) for x in sources]
    *sends, own = pack(
        (k, v), blocks_of(chunks[1], offsets) + blocks_of(chunks[1], (0,)), partners[0], spaces, False
    )
    partners.append([along_space(x, offset) for x, offset in zip(sends, offsets)])
    own = [sources[0], own]
    sends = pack((q,), [(offset, 0, width) for offset in offsets], partners[1], spaces, False)
    query_parts = [q] + [along_space(x, offset) for x, offset in zip(sends, offsets)]
    partners[1] = list(tie(partners[1], sends))

    last = frames - 2
    behind = 2 * len(offsets)

    def own_band(message, hops):
        return [(slot, hops, [(x, x.shape[0] - 2, 0)]) for slot, x in enumerate(message)]

    def partner_bands(message, hops):
        return [
            (slot, hops, [(x, 2 * (o - 1), o) for o in offsets]) for slot, x in enumerate(message)
        ]

    seconds, states = [], []
    for c, chunk in enumerate(chunks):
        begin, end = chunk[0], sum(chunk)
        arrays, here = list(partners[c]), []
        for (first, number), pair in zip(cuts, firsts):
            low, high = max(begin, first), min(end, first + number)
            if low < high:
                here.append((len(arrays), low - first, high - low, low - begin))
                arrays += pair
        outs_copies = []
        for slot in range(2):
            copies = [(n, 0, chunk[1] * HEAD_DIM, 2 * n, 0) for n in range(len(offsets))]
            copies += [
                (n + 1 - slot, lane * HEAD_DIM, number * HEAD_DIM, behind, to * HEAD_DIM)
                for n, lane, number, to in here
            ]
            outs_copies.append(tuple(copies))
        ready = join(arrays, tuple(outs_copies), behind + 2, chunk[1] * HEAD_DIM)
        seconds.append(swap_both(ready))
        pieces = [(own[c], 0, 0)] + [(x, 0, o) for x, o in zip(partners[c], offsets)]
        groups = [(0, 0, pieces)] + own_band(ready[::-1], 1)
        states.append(attend(scalars, query_parts, groups, None, False, chunk, sizes))

    messages = seconds
    for hops in range(2, frames - 1):
        following = []
        for c, chunk in enumerate(chunks):
            after = [state[1] for state in states]
            came = list(tie(messages[c][::-1], after))[::-1]
            rows = behind if hops == last else behind + 2
            following.append(swap_both([came[1 - slot][:rows] for slot in range(2)]))
            groups = partner_bands(came, hops - 1) + own_band(came, hops)
            states[c] = attend(scalars, query_parts, groups, states[c], False, chunk, sizes)
        messages = following
    ends = []
    for message in messages:
        came = list(tie(message, [state[1] for state in states]))
        ends.append(partner_bands(came, last))

    own, returned = [], []
    for c, chunk in enumerate(chunks):
        kept, *parts = attend(scalars, query_parts, ends[c], states[c], True, chunk, sizes)
        own.append((kept, (0, chunk[0] * HEAD_DIM)))
        for offset, x in zip(offsets, parts):
            returned.append((along_space(x, -offset), (offset, chunk[0] * HEAD_DIM)))
    late = len(returned) - len(offsets)
    result = None
    for batch in (own + returned[:late], returned[late:]):
        pieces, places = zip(*batch)
        result = put(pieces, places, result, q.shape, spaces)
    return result.reshape(queries.shape)


def solution(mesh):
    placed = P(("group", "frame"), "space", None, "head")
    return jax.shard_map(
        functools.partial(shards, mesh.shape["space"], mesh.shape["frame"]),
        mesh=mesh,
        in_specs=(placed, placed, placed, P(), P()),
        out_specs=placed,
        check_vma=False,
    )
```

```python
import functools
import math

import jax
import jax.numpy as jnp
from jax import lax
from jax.experimental import pallas as pl
from jax.experimental.pallas import tpu as pltpu
from jax.sharding import PartitionSpec as P

HEAD_DIM = 128
NEG_FILL = -1e30
VMEM_LIMIT = 16 * 1024 * 1024
SMALL_LIMIT = 2 * 1024 * 1024
STAGED_LIMIT = 60 * 1024 * 1024
ROW_GROUPS = 4
NT = (((1,), (1,)), ((), ()))
TN = (((0,), (0,)), ((), ()))


def pack_kernel(spaces, jobs, staged, *refs):
    refs = list(refs)
    halfway = refs[len(refs) - len(jobs) - 1 : -1] if staged else []
    sems = refs[-1]
    here = lax.axis_index("space")
    tokens = refs[0].shape[0]
    groups = ROW_GROUPS if staged else 1
    first_copies, second_copies = [], []
    for n, (source, offset, first, width, target, row) in enumerate(jobs):
        share = refs[source].shape[-1] // spaces
        column = pl.multiple_of(lax.rem(here + offset, spaces) * share + first, HEAD_DIM)
        out = refs[target] if row is None else refs[target].at[row]
        for g in range(groups):
            rows = pl.ds(g * (tokens // groups), tokens // groups)
            origin = refs[source].at[rows, pl.ds(column, width)]
            stop = halfway[n].at[rows] if staged else out.at[rows]
            copy = pltpu.make_async_copy(origin, stop, sems.at[0, n * groups + g])
            copy.start()
            first_copies.append(copy)
            if staged:
                second_copies.append(
                    pltpu.make_async_copy(stop, out.at[rows], sems.at[1, n * groups + g])
                )
    for n, copy in enumerate(first_copies):
        copy.wait()
        if staged:
            second_copies[n].start()
    for copy in second_copies:
        copy.wait()


def pack(sources, blocks, after, spaces, staged):
    tokens = sources[0].shape[0]
    several = len(sources) > 1
    jobs, shapes = [], []
    first_out = len(sources) + len(after)
    for n, (offset, first, width) in enumerate(blocks):
        lead = (len(sources),) if several else ()
        shapes.append(jax.ShapeDtypeStruct(lead + (tokens, width), sources[0].dtype))
        for row in range(len(sources)):
            jobs.append((row, offset, first, width, first_out + n, row if several else None))
    halfway = [pltpu.VMEM((tokens, job[3]), sources[0].dtype) for job in jobs]
    space = pl.ANY if staged else pltpu.VMEM
    return pl.pallas_call(
        functools.partial(pack_kernel, spaces, tuple(jobs), staged),
        in_specs=[pl.BlockSpec(memory_space=pl.ANY)] * first_out,
        out_specs=[pl.BlockSpec(memory_space=space)] * len(shapes),
        out_shape=shapes,
        scratch_shapes=(halfway if staged else [])
        + [pltpu.SemaphoreType.DMA((2, ROW_GROUPS * len(jobs)))],
        compiler_params=pltpu.CompilerParams(
            vmem_limit_bytes=STAGED_LIMIT if staged else SMALL_LIMIT
        ),
        name="pack",
    )(*sources, *after)


def tie(arrays, after):
    return pl.pallas_call(
        lambda *refs: None,
        in_specs=[pl.BlockSpec(memory_space=pl.ANY)] * (len(arrays) + len(after)),
        out_specs=[pl.BlockSpec(memory_space=pl.ANY)] * len(arrays),
        out_shape=[jax.ShapeDtypeStruct(x.shape, x.dtype) for x in arrays],
        input_output_aliases={n: n for n in range(len(arrays))},
        compiler_params=pltpu.CompilerParams(vmem_limit_bytes=SMALL_LIMIT),
        name="tie",
    )(*arrays, *after)


def attend_kernel(
    spaces, frames, columns, row_band, heads, together, groups, query_skip, fresh, final,
    flags_ref, widths_ref, *refs,
):
    refs = list(refs)
    queries = [refs.pop(0) for unused in range(spaces)]
    arrays = 1 + max(piece[0] for group in groups for piece in group[2])
    keyvals = [refs.pop(0) for unused in range(arrays)]
    state_in = None if fresh else (refs.pop(0), refs.pop(0))
    outs = [refs.pop(0) for unused in range(spaces if final else 2)]
    query_ref, key_ref = refs[:2]
    acc_ref, stat_ref = refs[2:] if final else outs
    tokens = queries[0].shape[0]
    frame_now, space_now = lax.axis_index("frame"), lax.axis_index("space")
    scale = math.log2(math.e) / math.sqrt(HEAD_DIM)
    own_column = space_now * (queries[0].shape[-1] // spaces)

    def first_row(offset):
        return lax.rem(space_now - offset + spaces, spaces) * row_band

    def asked_of(group):
        slot, hops = group[:2]
        side = 1 - 2 * lax.rem(frame_now + slot, 2)
        key_frame = frame_now + side * hops
        safe = jnp.clip(key_frame, 0, frames - 1)
        known = (key_frame >= 0) & (key_frame < frames)
        return known & (flags_ref[frame_now, safe] > 0)

    token = lax.broadcasted_iota(jnp.int32, (tokens, HEAD_DIM), 0)
    row = lax.broadcasted_iota(jnp.int32, (tokens, HEAD_DIM), 1)
    starts = [(row - first_row(offset)) * columns for offset in range(spaces)]
    for offset, start in enumerate(starts):
        hit = (token >= start) & (token < start + columns)
        mark = jnp.where(hit, 1.0, 0.0).astype(query_ref.dtype)
        for t in range(together):
            query_ref[t, pl.ds(offset * tokens, tokens), HEAD_DIM:] = mark
    for n, group in enumerate(groups):
        if group[1] > 0:

            @pl.when(asked_of(group))
            def _(n=n, group=group):
                reach = widths_ref[group[1]] * columns
                for m, (unused, unused, offset) in enumerate(group[2]):
                    start = starts[offset]
                    near = (token >= start - reach) & (token < start + columns + reach)
                    fill = jnp.where(near, 0.0, NEG_FILL).astype(key_ref.dtype)
                    for t in range(together):
                        key_ref[n, t, pl.ds(m * tokens, tokens), HEAD_DIM:] = fill

    def attend_heads(turn, carry):
        head = turn * together
        slot_of = (lambda t: t) if final else (lambda t: head + t)

        def lanes(t, skip=0):
            return pl.ds(pl.multiple_of((head + t) * HEAD_DIM + skip, HEAD_DIM), HEAD_DIM)

        def step(t, scores, pieces, old):
            h = slot_of(t)
            top = jnp.max(scores, axis=0, keepdims=True) * scale
            if old:
                before = stat_ref[h, 0:1, :]
                top = jnp.maximum(top, before)
            weights = jnp.exp2(scores * scale - top)
            total = jnp.sum(weights, axis=0, keepdims=True)
            values = jnp.concatenate(
                [keyvals[i][r + 1, :, lanes(t)] for i, r, o in pieces], axis=0
            )
            acc = lax.dot_general(
                values, weights.astype(jnp.bfloat16), TN, preferred_element_type=jnp.float32
            )
            if old:
                fade = jnp.exp2(before - top)
                total = total + stat_ref[h, 1:2, :] * fade
                acc = acc + acc_ref[h] * fade
            stat_ref[h, 0:1, :] = top
            stat_ref[h, 1:2, :] = total
            acc_ref[h] = acc

        for t in range(together):
            for offset in range(spaces):
                skip = query_skip + (own_column if offset == 0 else 0)
                query_ref[t, pl.ds(offset * tokens, tokens), :HEAD_DIM] = queries[offset][
                    :, lanes(t, skip)
                ]
            if not fresh:
                acc_ref[slot_of(t)] = state_in[0][head + t]
                stat_ref[slot_of(t)] = state_in[1][head + t]

        for n, (slot, hops, pieces) in enumerate(groups):
            if hops == 0:
                scores = []
                for t in range(together):
                    keys = jnp.concatenate(
                        [keyvals[i][r, :, lanes(t)] for i, r, o in pieces], axis=0
                    )
                    scores.append(
                        lax.dot_general(
                            keys, query_ref[t, :, :HEAD_DIM], NT,
                            preferred_element_type=jnp.float32,
                        )
                    )
                for t in range(together):
                    step(t, scores[t], pieces, False)
                continue

            @pl.when(asked_of(groups[n]))
            def _(n=n, pieces=pieces):
                many = pl.ds(0, len(pieces) * tokens)
                for t in range(together):
                    for m, (i, r, unused) in enumerate(pieces):
                        key_ref[n, t, pl.ds(m * tokens, tokens), :HEAD_DIM] = keyvals[i][
                            r, :, lanes(t)
                        ]
                scores = [
                    lax.dot_general(
                        key_ref[n, t, many], query_ref[t], NT, preferred_element_type=jnp.float32
                    )
                    for t in range(together)
                ]
                for t in range(together):
                    step(t, scores[t], pieces, True)

        if final:
            for t in range(together):
                result = jnp.transpose(acc_ref[t] * (1.0 / stat_ref[t, 1:2, :]))
                for offset in range(spaces):
                    part = result[offset * tokens : (offset + 1) * tokens]
                    outs[offset][:, lanes(t)] = part.astype(outs[offset].dtype)
        return carry

    lax.fori_loop(0, heads // together, attend_heads, 0)


def attend(scalars, queries, groups, state, final, chunk, sizes):
    spaces, frames, columns, row_band, features = sizes
    first, heads = chunk
    tokens = queries[0].shape[0]
    count = spaces * tokens
    together = next(n for n in (3, 2, 1) if heads % n == 0)
    arrays, numbered = [], []
    for slot, hops, pieces in groups:
        listed = []
        for array, row, offset in pieces:
            known = [n for n, x in enumerate(arrays) if x is array]
            if not known:
                known = [len(arrays)]
                arrays.append(array)
            listed.append((known[0], row, offset))
        numbered.append((slot, hops, tuple(listed)))
    operands = list(queries) + arrays + (list(state) if state is not None else [])
    state_shape = [(heads, HEAD_DIM, count), (heads, 8, count)]
    if final:
        out_shape = [jax.ShapeDtypeStruct((tokens, heads * HEAD_DIM), jnp.bfloat16)] * spaces
    else:
        out_shape = [jax.ShapeDtypeStruct(shape, jnp.float32) for shape in state_shape]
    scratch = [
        pltpu.VMEM((together, count, 2 * HEAD_DIM), jnp.bfloat16),
        pltpu.VMEM((len(groups), together, count, 2 * HEAD_DIM), jnp.bfloat16),
    ]
    if final:
        scratch += [pltpu.VMEM((together,) + shape[1:], jnp.float32) for shape in state_shape]
    pairs = heads * count * tokens * sum(len(pieces) for slot, hops, pieces in groups)
    return pl.pallas_call(
        functools.partial(
            attend_kernel, spaces, frames, columns, row_band, heads, together,
            tuple(numbered), first * HEAD_DIM, state is None, final,
        ),
        in_specs=[pl.BlockSpec(memory_space=pltpu.SMEM)] * 2
        + [pl.BlockSpec(memory_space=pltpu.VMEM)] * len(operands),
        out_specs=[pl.BlockSpec(memory_space=pltpu.VMEM)] * len(out_shape),
        out_shape=out_shape,
        scratch_shapes=scratch,
        compiler_params=pltpu.CompilerParams(vmem_limit_bytes=VMEM_LIMIT),
        cost_estimate=pl.CostEstimate(
            flops=4 * pairs * HEAD_DIM,
            bytes_accessed=8 * count * heads * HEAD_DIM,
            transcendentals=pairs,
        ),
        name="attend_final" if final else "attend",
    )(*scalars, *operands)


def join_kernel(outs_copies, *refs):
    arrays, outs = refs[: -len(outs_copies)], refs[-len(outs_copies) :]
    for out_ref, copies in zip(outs, outs_copies):
        for n, lane, width, row, column in copies:
            rows = pl.ds(row, arrays[n].shape[0])
            out_ref[rows, :, pl.ds(column, width)] = arrays[n][:, :, pl.ds(lane, width)]


def join(arrays, outs_copies, rows, width):
    shape = jax.ShapeDtypeStruct((rows, arrays[0].shape[1], width), arrays[0].dtype)
    return pl.pallas_call(
        functools.partial(join_kernel, outs_copies),
        in_specs=[pl.BlockSpec(memory_space=pltpu.VMEM)] * len(arrays),
        out_specs=[pl.BlockSpec(memory_space=pltpu.VMEM)] * len(outs_copies),
        out_shape=[shape] * len(outs_copies),
        compiler_params=pltpu.CompilerParams(vmem_limit_bytes=SMALL_LIMIT),
        name="join",
    )(*arrays)


def put_kernel(spaces, places, *refs):
    pieces, out_ref, sems = refs[: len(places)], refs[-2], refs[-1]
    share = out_ref.shape[-1] // spaces
    here = lax.axis_index("space")
    copies = []
    for n, (offset, first) in enumerate(places):
        column = pl.multiple_of(lax.rem(here + offset, spaces) * share + first, HEAD_DIM)
        width = pieces[n].shape[-1]
        copy = pltpu.make_async_copy(pieces[n], out_ref.at[:, pl.ds(column, width)], sems.at[n])
        copy.start()
        copies.append(copy)
    for copy in copies:
        copy.wait()


def put(pieces, places, whole, shape, spaces):
    kept = [] if whole is None else [whole]
    return pl.pallas_call(
        functools.partial(put_kernel, spaces, tuple(places)),
        in_specs=[pl.BlockSpec(memory_space=pltpu.VMEM)] * len(pieces)
        + [pl.BlockSpec(memory_space=pl.ANY)] * len(kept),
        out_specs=pl.BlockSpec(memory_space=pl.ANY),
        out_shape=jax.ShapeDtypeStruct(shape, pieces[0].dtype),
        scratch_shapes=[pltpu.SemaphoreType.DMA((len(pieces),))],
        input_output_aliases={len(pieces): 0} if kept else {},
        compiler_params=pltpu.CompilerParams(vmem_limit_bytes=SMALL_LIMIT),
        name="put",
    )(*pieces, *kept)


def shards(spaces, frames, queries, keys, values, flags, widths):
    unused, row_band, columns, features = queries.shape
    tokens = row_band * columns
    width = features // spaces
    heads = width // HEAD_DIM
    scalars = (flags, widths)
    sizes = (spaces, frames, columns, row_band, features)
    q, k, v = (x.reshape(tokens, features) for x in (queries, keys, values))
    half = heads - heads // 2
    chunks = [(0, half), (half, heads - half)]
    offsets = range(1, spaces)

    def along_space(x, offset):
        return lax.ppermute(x, "space", [(s, (s + offset) % spaces) for s in range(spaces)])

    def swap(x, slot):
        pairs = []
        for f in range(frames):
            side = 1 if (f + slot) % 2 == 0 else -1
            if 0 <= f + side < frames:
                pairs.append((f, f + side))
        return lax.ppermute(x, "frame", pairs)

    def swap_both(xs):
        second = swap(xs[1], 1)
        return [swap(xs[0], 0), second]

    def blocks_of(chunk, which):
        return [(offset, chunk[0] * HEAD_DIM, chunk[1] * HEAD_DIM) for offset in which]

    large = heads - heads // 3
    cuts = [(0, large), (large, heads - large)]
    *sends, source = pack(
        (k, v), blocks_of(chunks[0], offsets) + blocks_of(cuts[0], (0,)), (), spaces, True
    )
    partners = [[along_space(x, offset) for x, offset in zip(sends, offsets)]]
    firsts, own = [swap_both([source, source])], [source]
    *sends, source, rest = pack(
        (k, v),
        blocks_of(chunks[1], offsets) + blocks_of(cuts[1], (0,)) + blocks_of(chunks[1], (0,)),
        partners[0], spaces, False,
    )
    partners.append([along_space(x, offset) for x, offset in zip(sends, offsets)])
    firsts.append(swap_both([source, source]))
    own.append(rest)
    sends = pack((q,), [(offset, 0, width) for offset in offsets], partners[1], spaces, False)
    query_parts = [q] + [along_space(x, offset) for x, offset in zip(sends, offsets)]
    partners[1] = list(tie(partners[1], sends))

    last = frames - 2
    behind = 2 * len(offsets)

    def own_band(message, hops):
        return [(slot, hops, [(x, x.shape[0] - 2, 0)]) for slot, x in enumerate(message)]

    def partner_bands(message, hops):
        return [
            (slot, hops, [(x, 2 * (o - 1), o) for o in offsets]) for slot, x in enumerate(message)
        ]

    seconds, states = [], []
    for c, chunk in enumerate(chunks):
        begin, end = chunk[0], sum(chunk)
        arrays, here = list(partners[c]), []
        for (first, number), pair in zip(cuts, firsts):
            low, high = max(begin, first), min(end, first + number)
            if low < high:
                here.append((len(arrays), low - first, high - low, low - begin))
                arrays += pair
        outs_copies = []
        for slot in range(2):
            copies = [(n, 0, chunk[1] * HEAD_DIM, 2 * n, 0) for n in range(len(offsets))]
            copies += [
                (n + 1 - slot, lane * HEAD_DIM, number * HEAD_DIM, behind, to * HEAD_DIM)
                for n, lane, number, to in here
            ]
            outs_copies.append(tuple(copies))
        ready = join(arrays, tuple(outs_copies), behind + 2, chunk[1] * HEAD_DIM)
        seconds.append(swap_both(ready))
        pieces = [(own[c], 0, 0)] + [(x, 0, o) for x, o in zip(partners[c], offsets)]
        groups = [(0, 0, pieces)] + own_band(ready[::-1], 1)
        states.append(attend(scalars, query_parts, groups, None, False, chunk, sizes))

    messages = seconds
    for hops in range(2, frames - 1):
        following = []
        for c, chunk in enumerate(chunks):
            came = messages[c]
            if c == 0:
                groups = partner_bands(came, hops - 1)[::-1] + own_band(came, hops)[::-1]
                states[c] = attend(scalars, query_parts, groups, states[c], False, chunk, sizes)
            came = list(tie(came[::-1], [state[1] for state in states]))[::-1]
            rows = behind if hops == last else behind + 2
            following.append(swap_both([came[1 - slot][:rows] for slot in range(2)]))
            if c > 0:
                groups = partner_bands(came, hops - 1) + own_band(came, hops)
                states[c] = attend(scalars, query_parts, groups, states[c], False, chunk, sizes)
        messages = following
    ends = []
    for message in messages:
        came = list(tie(message, [state[1] for state in states]))
        ends.append(partner_bands(came, last))

    own, returned = [], []
    for c, chunk in enumerate(chunks):
        kept, *parts = attend(scalars, query_parts, ends[c], states[c], True, chunk, sizes)
        own.append((kept, (0, chunk[0] * HEAD_DIM)))
        for offset, x in zip(offsets, parts):
            returned.append((along_space(x, -offset), (offset, chunk[0] * HEAD_DIM)))
    late = len(returned) - len(offsets)
    result = None
    for batch in (own + returned[:late], returned[late:]):
        pieces, places = zip(*batch)
        result = put(pieces, places, result, q.shape, spaces)
    return result.reshape(queries.shape)


def solution(mesh):
    placed = P(("group", "frame"), "space", None, "head")
    return jax.shard_map(
        functools.partial(shards, mesh.shape["space"], mesh.shape["frame"]),
        mesh=mesh,
        in_specs=(placed, placed, placed, P(), P()),
        out_specs=placed,
        check_vma=False,
    )
```

```python
import functools
import math

import jax
import jax.numpy as jnp
from jax import lax
from jax.experimental import pallas as pl
from jax.experimental.pallas import tpu as pltpu
from jax.sharding import PartitionSpec as P

HEAD_DIM = 128
NEG_FILL = -1e30
VMEM_LIMIT = 16 * 1024 * 1024
SMALL_LIMIT = 2 * 1024 * 1024
STAGED_LIMIT = 60 * 1024 * 1024
ROW_GROUPS = 2
NT = (((1,), (1,)), ((), ()))
TN = (((0,), (0,)), ((), ()))


def pack_kernel(spaces, jobs, staged, *refs):
    refs = list(refs)
    halfway = refs[len(refs) - len(jobs) - 1 : -1] if staged else []
    sems = refs[-1]
    here = lax.axis_index("space")
    tokens = refs[0].shape[0]
    groups = ROW_GROUPS if staged else 1
    first_copies, second_copies = [], []
    for n, (source, offset, first, width, target, row) in enumerate(jobs):
        share = refs[source].shape[-1] // spaces
        column = pl.multiple_of(lax.rem(here + offset, spaces) * share + first, HEAD_DIM)
        out = refs[target] if row is None else refs[target].at[row]
        for g in range(groups):
            rows = pl.ds(g * (tokens // groups), tokens // groups)
            origin = refs[source].at[rows, pl.ds(column, width)]
            stop = halfway[n].at[rows] if staged else out.at[rows]
            copy = pltpu.make_async_copy(origin, stop, sems.at[0, n * groups + g])
            copy.start()
            first_copies.append(copy)
            if staged:
                second_copies.append(
                    pltpu.make_async_copy(stop, out.at[rows], sems.at[1, n * groups + g])
                )
    for n, copy in enumerate(first_copies):
        copy.wait()
        if staged:
            second_copies[n].start()
    for copy in second_copies:
        copy.wait()


def pack(sources, blocks, after, spaces, staged):
    tokens = sources[0].shape[0]
    several = len(sources) > 1
    jobs, shapes = [], []
    first_out = len(sources) + len(after)
    for n, (offset, first, width) in enumerate(blocks):
        lead = (len(sources),) if several else ()
        shapes.append(jax.ShapeDtypeStruct(lead + (tokens, width), sources[0].dtype))
        for row in range(len(sources)):
            jobs.append((row, offset, first, width, first_out + n, row if several else None))
    halfway = [pltpu.VMEM((tokens, job[3]), sources[0].dtype) for job in jobs]
    space = pl.ANY if staged else pltpu.VMEM
    return pl.pallas_call(
        functools.partial(pack_kernel, spaces, tuple(jobs), staged),
        in_specs=[pl.BlockSpec(memory_space=pl.ANY)] * first_out,
        out_specs=[pl.BlockSpec(memory_space=space)] * len(shapes),
        out_shape=shapes,
        scratch_shapes=(halfway if staged else [])
        + [pltpu.SemaphoreType.DMA((2, ROW_GROUPS * len(jobs)))],
        compiler_params=pltpu.CompilerParams(
            vmem_limit_bytes=STAGED_LIMIT if staged else SMALL_LIMIT
        ),
        name="pack",
    )(*sources, *after)


def tie(arrays, after):
    return pl.pallas_call(
        lambda *refs: None,
        in_specs=[pl.BlockSpec(memory_space=pl.ANY)] * (len(arrays) + len(after)),
        out_specs=[pl.BlockSpec(memory_space=pl.ANY)] * len(arrays),
        out_shape=[jax.ShapeDtypeStruct(x.shape, x.dtype) for x in arrays],
        input_output_aliases={n: n for n in range(len(arrays))},
        compiler_params=pltpu.CompilerParams(vmem_limit_bytes=SMALL_LIMIT),
        name="tie",
    )(*arrays, *after)


def attend_kernel(
    spaces, frames, columns, row_band, heads, together, groups, query_skip, fresh, final,
    flags_ref, widths_ref, *refs,
):
    refs = list(refs)
    queries = [refs.pop(0) for unused in range(spaces)]
    arrays = 1 + max(piece[0] for group in groups for piece in group[2])
    keyvals = [refs.pop(0) for unused in range(arrays)]
    state_in = None if fresh else (refs.pop(0), refs.pop(0))
    outs = [refs.pop(0) for unused in range(spaces if final else 2)]
    query_ref, key_ref = refs[:2]
    acc_ref, stat_ref = refs[2:] if final else outs
    tokens = queries[0].shape[0]
    frame_now, space_now = lax.axis_index("frame"), lax.axis_index("space")
    scale = math.log2(math.e) / math.sqrt(HEAD_DIM)
    own_column = space_now * (queries[0].shape[-1] // spaces)

    def first_row(offset):
        return lax.rem(space_now - offset + spaces, spaces) * row_band

    def asked_of(group):
        slot, hops = group[:2]
        side = 1 - 2 * lax.rem(frame_now + slot, 2)
        key_frame = frame_now + side * hops
        safe = jnp.clip(key_frame, 0, frames - 1)
        known = (key_frame >= 0) & (key_frame < frames)
        return known & (flags_ref[frame_now, safe] > 0)

    token = lax.broadcasted_iota(jnp.int32, (tokens, HEAD_DIM), 0)
    row = lax.broadcasted_iota(jnp.int32, (tokens, HEAD_DIM), 1)
    starts = [(row - first_row(offset)) * columns for offset in range(spaces)]
    for offset, start in enumerate(starts):
        hit = (token >= start) & (token < start + columns)
        mark = jnp.where(hit, 1.0, 0.0).astype(query_ref.dtype)
        for t in range(together):
            query_ref[t, pl.ds(offset * tokens, tokens), HEAD_DIM:] = mark
    for n, group in enumerate(groups):
        if group[1] > 0:

            @pl.when(asked_of(group))
            def _(n=n, group=group):
                reach = widths_ref[group[1]] * columns
                for m, (unused, unused, offset) in enumerate(group[2]):
                    start = starts[offset]
                    near = (token >= start - reach) & (token < start + columns + reach)
                    fill = jnp.where(near, 0.0, NEG_FILL).astype(key_ref.dtype)
                    for t in range(together):
                        key_ref[n, t, pl.ds(m * tokens, tokens), HEAD_DIM:] = fill

    def attend_heads(turn, carry):
        head = turn * together
        slot_of = (lambda t: t) if final else (lambda t: head + t)

        def lanes(t, skip=0):
            return pl.ds(pl.multiple_of((head + t) * HEAD_DIM + skip, HEAD_DIM), HEAD_DIM)

        def step(t, scores, pieces, old):
            h = slot_of(t)
            top = jnp.max(scores, axis=0, keepdims=True) * scale
            if old:
                before = stat_ref[h, 0:1, :]
                top = jnp.maximum(top, before)
            weights = jnp.exp2(scores * scale - top)
            total = jnp.sum(weights, axis=0, keepdims=True)
            values = jnp.concatenate(
                [keyvals[i][r + 1, :, lanes(t)] for i, r, o in pieces], axis=0
            )
            acc = lax.dot_general(
                values, weights.astype(jnp.bfloat16), TN, preferred_element_type=jnp.float32
            )
            if old:
                fade = jnp.exp2(before - top)
                total = total + stat_ref[h, 1:2, :] * fade
                acc = acc + acc_ref[h] * fade
            stat_ref[h, 0:1, :] = top
            stat_ref[h, 1:2, :] = total
            acc_ref[h] = acc

        for t in range(together):
            for offset in range(spaces):
                skip = query_skip + (own_column if offset == 0 else 0)
                query_ref[t, pl.ds(offset * tokens, tokens), :HEAD_DIM] = queries[offset][
                    :, lanes(t, skip)
                ]
            if not fresh:
                acc_ref[slot_of(t)] = state_in[0][head + t]
                stat_ref[slot_of(t)] = state_in[1][head + t]

        for n, (slot, hops, pieces) in enumerate(groups):
            if hops == 0:
                scores = []
                for t in range(together):
                    keys = jnp.concatenate(
                        [keyvals[i][r, :, lanes(t)] for i, r, o in pieces], axis=0
                    )
                    scores.append(
                        lax.dot_general(
                            keys, query_ref[t, :, :HEAD_DIM], NT,
                            preferred_element_type=jnp.float32,
                        )
                    )
                for t in range(together):
                    step(t, scores[t], pieces, False)
                continue

            @pl.when(asked_of(groups[n]))
            def _(n=n, pieces=pieces):
                many = pl.ds(0, len(pieces) * tokens)
                for t in range(together):
                    for m, (i, r, unused) in enumerate(pieces):
                        key_ref[n, t, pl.ds(m * tokens, tokens), :HEAD_DIM] = keyvals[i][
                            r, :, lanes(t)
                        ]
                scores = [
                    lax.dot_general(
                        key_ref[n, t, many], query_ref[t], NT, preferred_element_type=jnp.float32
                    )
                    for t in range(together)
                ]
                for t in range(together):
                    step(t, scores[t], pieces, True)

        if final:
            for t in range(together):
                result = jnp.transpose(acc_ref[t] * (1.0 / stat_ref[t, 1:2, :]))
                for offset in range(spaces):
                    part = result[offset * tokens : (offset + 1) * tokens]
                    outs[offset][:, lanes(t)] = part.astype(outs[offset].dtype)
        return carry

    lax.fori_loop(0, heads // together, attend_heads, 0)


def attend(scalars, queries, groups, state, final, chunk, sizes):
    spaces, frames, columns, row_band, features = sizes
    first, heads = chunk
    tokens = queries[0].shape[0]
    count = spaces * tokens
    together = next(n for n in (3, 2, 1) if heads % n == 0)
    arrays, numbered = [], []
    for slot, hops, pieces in groups:
        listed = []
        for array, row, offset in pieces:
            known = [n for n, x in enumerate(arrays) if x is array]
            if not known:
                known = [len(arrays)]
                arrays.append(array)
            listed.append((known[0], row, offset))
        numbered.append((slot, hops, tuple(listed)))
    operands = list(queries) + arrays + (list(state) if state is not None else [])
    state_shape = [(heads, HEAD_DIM, count), (heads, 8, count)]
    if final:
        out_shape = [jax.ShapeDtypeStruct((tokens, heads * HEAD_DIM), jnp.bfloat16)] * spaces
    else:
        out_shape = [jax.ShapeDtypeStruct(shape, jnp.float32) for shape in state_shape]
    scratch = [
        pltpu.VMEM((together, count, 2 * HEAD_DIM), jnp.bfloat16),
        pltpu.VMEM((len(groups), together, count, 2 * HEAD_DIM), jnp.bfloat16),
    ]
    if final:
        scratch += [pltpu.VMEM((together,) + shape[1:], jnp.float32) for shape in state_shape]
    pairs = heads * count * tokens * sum(len(pieces) for slot, hops, pieces in groups)
    return pl.pallas_call(
        functools.partial(
            attend_kernel, spaces, frames, columns, row_band, heads, together,
            tuple(numbered), first * HEAD_DIM, state is None, final,
        ),
        in_specs=[pl.BlockSpec(memory_space=pltpu.SMEM)] * 2
        + [pl.BlockSpec(memory_space=pltpu.VMEM)] * len(operands),
        out_specs=[pl.BlockSpec(memory_space=pltpu.VMEM)] * len(out_shape),
        out_shape=out_shape,
        scratch_shapes=scratch,
        compiler_params=pltpu.CompilerParams(vmem_limit_bytes=VMEM_LIMIT),
        cost_estimate=pl.CostEstimate(
            flops=4 * pairs * HEAD_DIM,
            bytes_accessed=8 * count * heads * HEAD_DIM,
            transcendentals=pairs,
        ),
        name="attend_final" if final else "attend",
    )(*scalars, *operands)


def join_kernel(outs_copies, *refs):
    arrays, outs = refs[: -len(outs_copies)], refs[-len(outs_copies) :]
    for out_ref, copies in zip(outs, outs_copies):
        for n, lane, width, row, column in copies:
            rows = pl.ds(row, arrays[n].shape[0])
            out_ref[rows, :, pl.ds(column, width)] = arrays[n][:, :, pl.ds(lane, width)]


def join(arrays, outs_copies, rows, width):
    shape = jax.ShapeDtypeStruct((rows, arrays[0].shape[1], width), arrays[0].dtype)
    return pl.pallas_call(
        functools.partial(join_kernel, outs_copies),
        in_specs=[pl.BlockSpec(memory_space=pltpu.VMEM)] * len(arrays),
        out_specs=[pl.BlockSpec(memory_space=pltpu.VMEM)] * len(outs_copies),
        out_shape=[shape] * len(outs_copies),
        compiler_params=pltpu.CompilerParams(vmem_limit_bytes=SMALL_LIMIT),
        name="join",
    )(*arrays)


def put_kernel(spaces, places, *refs):
    pieces, out_ref, sems = refs[: len(places)], refs[-2], refs[-1]
    share = out_ref.shape[-1] // spaces
    here = lax.axis_index("space")
    copies = []
    for n, (offset, first) in enumerate(places):
        column = pl.multiple_of(lax.rem(here + offset, spaces) * share + first, HEAD_DIM)
        width = pieces[n].shape[-1]
        copy = pltpu.make_async_copy(pieces[n], out_ref.at[:, pl.ds(column, width)], sems.at[n])
        copy.start()
        copies.append(copy)
    for copy in copies:
        copy.wait()


def put(pieces, places, whole, shape, spaces):
    kept = [] if whole is None else [whole]
    return pl.pallas_call(
        functools.partial(put_kernel, spaces, tuple(places)),
        in_specs=[pl.BlockSpec(memory_space=pltpu.VMEM)] * len(pieces)
        + [pl.BlockSpec(memory_space=pl.ANY)] * len(kept),
        out_specs=pl.BlockSpec(memory_space=pl.ANY),
        out_shape=jax.ShapeDtypeStruct(shape, pieces[0].dtype),
        scratch_shapes=[pltpu.SemaphoreType.DMA((len(pieces),))],
        input_output_aliases={len(pieces): 0} if kept else {},
        compiler_params=pltpu.CompilerParams(vmem_limit_bytes=SMALL_LIMIT),
        name="put",
    )(*pieces, *kept)


def shards(spaces, frames, queries, keys, values, flags, widths):
    unused, row_band, columns, features = queries.shape
    tokens = row_band * columns
    width = features // spaces
    heads = width // HEAD_DIM
    scalars = (flags, widths)
    sizes = (spaces, frames, columns, row_band, features)
    q, k, v = (x.reshape(tokens, features) for x in (queries, keys, values))
    half = heads - heads // 2
    chunks = [(0, half), (half, heads - half)]
    offsets = range(1, spaces)

    def along_space(x, offset):
        return lax.ppermute(x, "space", [(s, (s + offset) % spaces) for s in range(spaces)])

    def swap(x, slot, brought=0):
        pairs = []
        for f in range(frames):
            side = 1 if (f + slot) % 2 == 0 else -1
            if 0 <= f + side < frames and 0 <= f - side * brought < frames:
                pairs.append((f, f + side))
        return lax.ppermute(x, "frame", pairs)

    def swap_both(xs, brought=0):
        second = swap(xs[1], 1, brought)
        return [swap(xs[0], 0, brought), second]

    def blocks_of(chunk, which):
        return [(offset, chunk[0] * HEAD_DIM, chunk[1] * HEAD_DIM) for offset in which]

    large = heads - heads // 3
    cuts = [(0, large), (large, heads - large)]
    *sends, source = pack(
        (k, v), blocks_of(chunks[0], offsets) + blocks_of(cuts[0], (0,)), (), spaces, True
    )
    partners = [[along_space(x, offset) for x, offset in zip(sends, offsets)]]
    firsts, own = [swap_both([source, source])], [source]
    *sends, source, rest = pack(
        (k, v),
        blocks_of(chunks[1], offsets) + blocks_of(cuts[1], (0,)) + blocks_of(chunks[1], (0,)),
        partners[0], spaces, False,
    )
    partners.append([along_space(x, offset) for x, offset in zip(sends, offsets)])
    firsts.append(swap_both([source, source]))
    own.append(rest)
    sends = pack((q,), [(offset, 0, width) for offset in offsets], partners[1], spaces, False)
    query_parts = [q] + [along_space(x, offset) for x, offset in zip(sends, offsets)]
    partners[1] = list(tie(partners[1], sends))

    last = frames - 2
    behind = 2 * len(offsets)

    def own_band(message, hops):
        return [(slot, hops, [(x, x.shape[0] - 2, 0)]) for slot, x in enumerate(message)]

    def partner_bands(message, hops):
        return [
            (slot, hops, [(x, 2 * (o - 1), o) for o in offsets]) for slot, x in enumerate(message)
        ]

    seconds, states = [], []
    for c, chunk in enumerate(chunks):
        begin, end = chunk[0], sum(chunk)
        arrays, here = list(partners[c]), []
        for (first, number), pair in zip(cuts, firsts):
            low, high = max(begin, first), min(end, first + number)
            if low < high:
                here.append((len(arrays), low - first, high - low, low - begin))
                arrays += pair
        outs_copies = []
        for slot in range(2):
            copies = [(n, 0, chunk[1] * HEAD_DIM, 2 * n, 0) for n in range(len(offsets))]
            copies += [
                (n + 1 - slot, lane * HEAD_DIM, number * HEAD_DIM, behind, to * HEAD_DIM)
                for n, lane, number, to in here
            ]
            outs_copies.append(tuple(copies))
        ready = join(arrays, tuple(outs_copies), behind + 2, chunk[1] * HEAD_DIM)
        seconds.append(swap_both(ready))
        pieces = [(own[c], 0, 0)] + [(x, 0, o) for x, o in zip(partners[c], offsets)]
        groups = [(0, 0, pieces)] + own_band(ready[::-1], 1)
        states.append(attend(scalars, query_parts, groups, None, False, chunk, sizes))

    messages = seconds
    for hops in range(2, frames - 1):
        following = []
        for c, chunk in enumerate(chunks):
            came = messages[c]
            if c == 0:
                groups = partner_bands(came, hops - 1)[::-1] + own_band(came, hops)[::-1]
                states[c] = attend(scalars, query_parts, groups, states[c], False, chunk, sizes)
            came = list(tie(came[::-1], [state[1] for state in states]))[::-1]
            rows = behind if hops == last else behind + 2
            sent = [came[1 - slot][:rows] for slot in range(2)]
            following.append(swap_both(sent, hops - 1))
            if c > 0:
                groups = partner_bands(came, hops - 1) + own_band(came, hops)
                states[c] = attend(scalars, query_parts, groups, states[c], False, chunk, sizes)
        messages = following
    ends = []
    for message in messages:
        came = list(tie(message, [state[1] for state in states]))
        ends.append(partner_bands(came, last))

    own, returned = [], []
    for c, chunk in enumerate(chunks):
        kept, *parts = attend(scalars, query_parts, ends[c], states[c], True, chunk, sizes)
        own.append((kept, (0, chunk[0] * HEAD_DIM)))
        for offset, x in zip(offsets, parts):
            returned.append((along_space(x, -offset), (offset, chunk[0] * HEAD_DIM)))
    late = len(returned) - len(offsets)
    result = None
    for batch in (own + returned[:late], returned[late:]):
        pieces, places = zip(*batch)
        result = put(pieces, places, result, q.shape, spaces)
    return result.reshape(queries.shape)


def solution(mesh):
    placed = P(("group", "frame"), "space", None, "head")
    return jax.shard_map(
        functools.partial(shards, mesh.shape["space"], mesh.shape["frame"]),
        mesh=mesh,
        in_specs=(placed, placed, placed, P(), P()),
        out_specs=placed,
        check_vma=False,
    )
```

```python
import functools
import math

import jax
import jax.numpy as jnp
from jax import lax
from jax.experimental import pallas as pl
from jax.experimental.pallas import tpu as pltpu
from jax.sharding import PartitionSpec as P

HEAD_DIM = 128
NEG_FILL = -1e30
VMEM_LIMIT = 16 * 1024 * 1024
SMALL_LIMIT = 2 * 1024 * 1024
STAGED_LIMIT = 60 * 1024 * 1024
ROW_GROUPS = 2
NT = (((1,), (1,)), ((), ()))
TN = (((0,), (0,)), ((), ()))


def pack_kernel(spaces, jobs, staged, *refs):
    refs = list(refs)
    halfway = refs[len(refs) - len(jobs) - 1 : -1] if staged else []
    sems = refs[-1]
    here = lax.axis_index("space")
    tokens = refs[0].shape[0]
    groups = ROW_GROUPS if staged else 1
    first_copies, second_copies = [], []
    for n, (source, offset, first, width, target, row) in enumerate(jobs):
        share = refs[source].shape[-1] // spaces
        column = pl.multiple_of(lax.rem(here + offset, spaces) * share + first, HEAD_DIM)
        out = refs[target] if row is None else refs[target].at[row]
        for g in range(groups):
            rows = pl.ds(g * (tokens // groups), tokens // groups)
            origin = refs[source].at[rows, pl.ds(column, width)]
            stop = halfway[n].at[rows] if staged else out.at[rows]
            copy = pltpu.make_async_copy(origin, stop, sems.at[0, n * groups + g])
            copy.start()
            first_copies.append(copy)
            if staged:
                second_copies.append(
                    pltpu.make_async_copy(stop, out.at[rows], sems.at[1, n * groups + g])
                )
    for n, copy in enumerate(first_copies):
        copy.wait()
        if staged:
            second_copies[n].start()
    for copy in second_copies:
        copy.wait()


def pack(sources, blocks, after, spaces, staged):
    tokens = sources[0].shape[0]
    several = len(sources) > 1
    jobs, shapes = [], []
    first_out = len(sources) + len(after)
    for n, (offset, first, width) in enumerate(blocks):
        lead = (len(sources),) if several else ()
        shapes.append(jax.ShapeDtypeStruct(lead + (tokens, width), sources[0].dtype))
        for row in range(len(sources)):
            jobs.append((row, offset, first, width, first_out + n, row if several else None))
    halfway = [pltpu.VMEM((tokens, job[3]), sources[0].dtype) for job in jobs]
    space = pl.ANY if staged else pltpu.VMEM
    return pl.pallas_call(
        functools.partial(pack_kernel, spaces, tuple(jobs), staged),
        in_specs=[pl.BlockSpec(memory_space=pl.ANY)] * first_out,
        out_specs=[pl.BlockSpec(memory_space=space)] * len(shapes),
        out_shape=shapes,
        scratch_shapes=(halfway if staged else [])
        + [pltpu.SemaphoreType.DMA((2, ROW_GROUPS * len(jobs)))],
        compiler_params=pltpu.CompilerParams(
            vmem_limit_bytes=STAGED_LIMIT if staged else SMALL_LIMIT
        ),
        name="pack",
    )(*sources, *after)


def tie(arrays, after):
    return pl.pallas_call(
        lambda *refs: None,
        in_specs=[pl.BlockSpec(memory_space=pl.ANY)] * (len(arrays) + len(after)),
        out_specs=[pl.BlockSpec(memory_space=pl.ANY)] * len(arrays),
        out_shape=[jax.ShapeDtypeStruct(x.shape, x.dtype) for x in arrays],
        input_output_aliases={n: n for n in range(len(arrays))},
        compiler_params=pltpu.CompilerParams(vmem_limit_bytes=SMALL_LIMIT),
        name="tie",
    )(*arrays, *after)


def attend_kernel(
    spaces, frames, columns, row_band, heads, together, groups, query_skip, fresh, final,
    flags_ref, widths_ref, *refs,
):
    refs = list(refs)
    queries = [refs.pop(0) for unused in range(spaces)]
    arrays = 1 + max(piece[0] for group in groups for piece in group[2])
    keyvals = [refs.pop(0) for unused in range(arrays)]
    state_in = None if fresh else (refs.pop(0), refs.pop(0))
    outs = [refs.pop(0) for unused in range(spaces if final else 2)]
    query_ref, key_ref = refs[:2]
    acc_ref, stat_ref = refs[2:] if final else outs
    tokens = queries[0].shape[0]
    frame_now, space_now = lax.axis_index("frame"), lax.axis_index("space")
    scale = math.log2(math.e) / math.sqrt(HEAD_DIM)
    own_column = space_now * (queries[0].shape[-1] // spaces)

    def first_row(offset):
        return lax.rem(space_now - offset + spaces, spaces) * row_band

    def asked_of(group):
        slot, hops = group[:2]
        side = 1 - 2 * lax.rem(frame_now + slot, 2)
        key_frame = frame_now + side * hops
        safe = jnp.clip(key_frame, 0, frames - 1)
        known = (key_frame >= 0) & (key_frame < frames)
        return known & (flags_ref[frame_now, safe] > 0)

    token = lax.broadcasted_iota(jnp.int32, (tokens, HEAD_DIM), 0)
    row = lax.broadcasted_iota(jnp.int32, (tokens, HEAD_DIM), 1)
    starts = [(row - first_row(offset)) * columns for offset in range(spaces)]
    for offset, start in enumerate(starts):
        hit = (token >= start) & (token < start + columns)
        mark = jnp.where(hit, 1.0, 0.0).astype(query_ref.dtype)
        for t in range(together):
            query_ref[t, pl.ds(offset * tokens, tokens), HEAD_DIM:] = mark
    for n, group in enumerate(groups):
        if group[1] > 0:

            @pl.when(asked_of(group))
            def _(n=n, group=group):
                reach = widths_ref[group[1]] * columns
                for m, (unused, unused, offset) in enumerate(group[2]):
                    start = starts[offset]
                    near = (token >= start - reach) & (token < start + columns + reach)
                    fill = jnp.where(near, 0.0, NEG_FILL).astype(key_ref.dtype)
                    for t in range(together):
                        key_ref[n, t, pl.ds(m * tokens, tokens), HEAD_DIM:] = fill

    def attend_heads(turn, carry):
        head = turn * together
        slot_of = (lambda t: t) if final else (lambda t: head + t)

        def lanes(t, skip=0):
            return pl.ds(pl.multiple_of((head + t) * HEAD_DIM + skip, HEAD_DIM), HEAD_DIM)

        def step(t, scores, pieces, old):
            h = slot_of(t)
            top = jnp.max(scores, axis=0, keepdims=True) * scale
            if old:
                before = stat_ref[h, 0:1, :]
                top = jnp.maximum(top, before)
            weights = jnp.exp2(scores * scale - top)
            total = jnp.sum(weights, axis=0, keepdims=True)
            values = jnp.concatenate(
                [keyvals[i][r + 1, :, lanes(t)] for i, r, o in pieces], axis=0
            )
            acc = lax.dot_general(
                values, weights.astype(jnp.bfloat16), TN, preferred_element_type=jnp.float32
            )
            if old:
                fade = jnp.exp2(before - top)
                total = total + stat_ref[h, 1:2, :] * fade
                acc = acc + acc_ref[h] * fade
            stat_ref[h, 0:1, :] = top
            stat_ref[h, 1:2, :] = total
            acc_ref[h] = acc

        for t in range(together):
            for offset in range(spaces):
                skip = query_skip + (own_column if offset == 0 else 0)
                query_ref[t, pl.ds(offset * tokens, tokens), :HEAD_DIM] = queries[offset][
                    :, lanes(t, skip)
                ]
            if not fresh:
                acc_ref[slot_of(t)] = state_in[0][head + t]
                stat_ref[slot_of(t)] = state_in[1][head + t]

        for n, (slot, hops, pieces) in enumerate(groups):
            if hops == 0:
                scores = []
                for t in range(together):
                    keys = jnp.concatenate(
                        [keyvals[i][r, :, lanes(t)] for i, r, o in pieces], axis=0
                    )
                    scores.append(
                        lax.dot_general(
                            keys, query_ref[t, :, :HEAD_DIM], NT,
                            preferred_element_type=jnp.float32,
                        )
                    )
                for t in range(together):
                    step(t, scores[t], pieces, False)
                continue

            @pl.when(asked_of(groups[n]))
            def _(n=n, pieces=pieces):
                many = pl.ds(0, len(pieces) * tokens)
                for t in range(together):
                    for m, (i, r, unused) in enumerate(pieces):
                        key_ref[n, t, pl.ds(m * tokens, tokens), :HEAD_DIM] = keyvals[i][
                            r, :, lanes(t)
                        ]
                scores = [
                    lax.dot_general(
                        key_ref[n, t, many], query_ref[t], NT, preferred_element_type=jnp.float32
                    )
                    for t in range(together)
                ]
                for t in range(together):
                    step(t, scores[t], pieces, True)

        if final:
            for t in range(together):
                result = jnp.transpose(acc_ref[t] * (1.0 / stat_ref[t, 1:2, :]))
                for offset in range(spaces):
                    part = result[offset * tokens : (offset + 1) * tokens]
                    outs[offset][:, lanes(t)] = part.astype(outs[offset].dtype)
        return carry

    lax.fori_loop(0, heads // together, attend_heads, 0)


def attend(scalars, queries, groups, state, final, chunk, sizes):
    spaces, frames, columns, row_band, features = sizes
    first, heads = chunk
    tokens = queries[0].shape[0]
    count = spaces * tokens
    together = next(n for n in (3, 2, 1) if heads % n == 0)
    arrays, numbered = [], []
    for slot, hops, pieces in groups:
        listed = []
        for array, row, offset in pieces:
            known = [n for n, x in enumerate(arrays) if x is array]
            if not known:
                known = [len(arrays)]
                arrays.append(array)
            listed.append((known[0], row, offset))
        numbered.append((slot, hops, tuple(listed)))
    operands = list(queries) + arrays + (list(state) if state is not None else [])
    state_shape = [(heads, HEAD_DIM, count), (heads, 8, count)]
    if final:
        out_shape = [jax.ShapeDtypeStruct((tokens, heads * HEAD_DIM), jnp.bfloat16)] * spaces
    else:
        out_shape = [jax.ShapeDtypeStruct(shape, jnp.float32) for shape in state_shape]
    scratch = [
        pltpu.VMEM((together, count, 2 * HEAD_DIM), jnp.bfloat16),
        pltpu.VMEM((len(groups), together, count, 2 * HEAD_DIM), jnp.bfloat16),
    ]
    if final:
        scratch += [pltpu.VMEM((together,) + shape[1:], jnp.float32) for shape in state_shape]
    pairs = heads * count * tokens * sum(len(pieces) for slot, hops, pieces in groups)
    return pl.pallas_call(
        functools.partial(
            attend_kernel, spaces, frames, columns, row_band, heads, together,
            tuple(numbered), first * HEAD_DIM, state is None, final,
        ),
        in_specs=[pl.BlockSpec(memory_space=pltpu.SMEM)] * 2
        + [pl.BlockSpec(memory_space=pltpu.VMEM)] * len(operands),
        out_specs=[pl.BlockSpec(memory_space=pltpu.VMEM)] * len(out_shape),
        out_shape=out_shape,
        scratch_shapes=scratch,
        compiler_params=pltpu.CompilerParams(vmem_limit_bytes=VMEM_LIMIT),
        cost_estimate=pl.CostEstimate(
            flops=4 * pairs * HEAD_DIM,
            bytes_accessed=8 * count * heads * HEAD_DIM,
            transcendentals=pairs,
        ),
        name="attend_final" if final else "attend",
    )(*scalars, *operands)


def join_kernel(outs_copies, *refs):
    arrays, outs = refs[: -len(outs_copies)], refs[-len(outs_copies) :]
    for out_ref, copies in zip(outs, outs_copies):
        for n, lane, width, row, column in copies:
            rows = pl.ds(row, arrays[n].shape[0])
            out_ref[rows, :, pl.ds(column, width)] = arrays[n][:, :, pl.ds(lane, width)]


def join(arrays, outs_copies, rows, width):
    shape = jax.ShapeDtypeStruct((rows, arrays[0].shape[1], width), arrays[0].dtype)
    return pl.pallas_call(
        functools.partial(join_kernel, outs_copies),
        in_specs=[pl.BlockSpec(memory_space=pltpu.VMEM)] * len(arrays),
        out_specs=[pl.BlockSpec(memory_space=pltpu.VMEM)] * len(outs_copies),
        out_shape=[shape] * len(outs_copies),
        compiler_params=pltpu.CompilerParams(vmem_limit_bytes=SMALL_LIMIT),
        name="join",
    )(*arrays)


def put_kernel(spaces, places, *refs):
    pieces, out_ref, sems = refs[: len(places)], refs[-2], refs[-1]
    share = out_ref.shape[-1] // spaces
    here = lax.axis_index("space")
    copies = []
    for n, (offset, first) in enumerate(places):
        column = pl.multiple_of(lax.rem(here + offset, spaces) * share + first, HEAD_DIM)
        width = pieces[n].shape[-1]
        copy = pltpu.make_async_copy(pieces[n], out_ref.at[:, pl.ds(column, width)], sems.at[n])
        copy.start()
        copies.append(copy)
    for copy in copies:
        copy.wait()


def put(pieces, places, whole, shape, spaces):
    kept = [] if whole is None else [whole]
    return pl.pallas_call(
        functools.partial(put_kernel, spaces, tuple(places)),
        in_specs=[pl.BlockSpec(memory_space=pltpu.VMEM)] * len(pieces)
        + [pl.BlockSpec(memory_space=pl.ANY)] * len(kept),
        out_specs=pl.BlockSpec(memory_space=pl.ANY),
        out_shape=jax.ShapeDtypeStruct(shape, pieces[0].dtype),
        scratch_shapes=[pltpu.SemaphoreType.DMA((len(pieces),))],
        input_output_aliases={len(pieces): 0} if kept else {},
        compiler_params=pltpu.CompilerParams(vmem_limit_bytes=SMALL_LIMIT),
        name="put",
    )(*pieces, *kept)


def shards(spaces, frames, queries, keys, values, flags, widths):
    unused, row_band, columns, features = queries.shape
    tokens = row_band * columns
    width = features // spaces
    heads = width // HEAD_DIM
    scalars = (flags, widths)
    sizes = (spaces, frames, columns, row_band, features)
    q, k, v = (x.reshape(tokens, features) for x in (queries, keys, values))
    half = heads - heads // 2
    chunks = [(0, half), (half, heads - half)]
    offsets = range(1, spaces)

    def along_space(x, offset):
        return lax.ppermute(x, "space", [(s, (s + offset) % spaces) for s in range(spaces)])

    def swap(x, slot, brought=0):
        pairs = []
        for f in range(frames):
            side = 1 if (f + slot) % 2 == 0 else -1
            if 0 <= f + side < frames and 0 <= f - side * brought < frames:
                pairs.append((f, f + side))
        return lax.ppermute(x, "frame", pairs)

    def swap_both(xs, brought=0):
        second = swap(xs[1], 1, brought)
        return [swap(xs[0], 0, brought), second]

    def blocks_of(chunk, which):
        return [(offset, chunk[0] * HEAD_DIM, chunk[1] * HEAD_DIM) for offset in which]

    large = heads - heads // 3
    cuts = [(0, large), (large, heads - large)]
    *sends, source = pack(
        (k, v), blocks_of(chunks[0], offsets) + blocks_of(cuts[0], (0,)), (), spaces, True
    )
    partners = [[along_space(x, offset) for x, offset in zip(sends, offsets)]]
    firsts, own = [swap_both([source, source])], [source]
    *sends, source, rest = pack(
        (k, v),
        blocks_of(chunks[1], offsets) + blocks_of(cuts[1], (0,)) + blocks_of(chunks[1], (0,)),
        partners[0], spaces, False,
    )
    partners.append([along_space(x, offset) for x, offset in zip(sends, offsets)])
    firsts.append(swap_both([source, source]))
    own.append(rest)
    sends = pack((q,), [(offset, 0, width) for offset in offsets], partners[1], spaces, False)
    query_parts = [q] + [along_space(x, offset) for x, offset in zip(sends, offsets)]
    partners[1] = list(tie(partners[1], sends))

    last = frames - 2
    behind = 2 * len(offsets)

    def own_band(message, hops):
        return [(slot, hops, [(x, x.shape[0] - 2, 0)]) for slot, x in enumerate(message)]

    def partner_bands(message, hops):
        return [
            (slot, hops, [(x, 2 * (o - 1), o) for o in offsets]) for slot, x in enumerate(message)
        ]

    seconds, states = [], []
    for c, chunk in enumerate(chunks):
        begin, end = chunk[0], sum(chunk)
        arrays, here = list(partners[c]), []
        for (first, number), pair in zip(cuts, firsts):
            low, high = max(begin, first), min(end, first + number)
            if low < high:
                here.append((len(arrays), low - first, high - low, low - begin))
                arrays += pair
        outs_copies = []
        for slot in range(2):
            copies = [(n, 0, chunk[1] * HEAD_DIM, 2 * n, 0) for n in range(len(offsets))]
            copies += [
                (n + 1 - slot, lane * HEAD_DIM, number * HEAD_DIM, behind, to * HEAD_DIM)
                for n, lane, number, to in here
            ]
            outs_copies.append(tuple(copies))
        ready = join(arrays, tuple(outs_copies), behind + 2, chunk[1] * HEAD_DIM)
        seconds.append(swap_both(ready))
        pieces = [(own[c], 0, 0)] + [(x, 0, o) for x, o in zip(partners[c], offsets)]
        groups = [(0, 0, pieces)] + own_band(ready[::-1], 1)
        states.append(attend(scalars, query_parts, groups, None, False, chunk, sizes))

    messages = seconds
    for hops in range(2, frames - 1):
        following = []
        for c, chunk in enumerate(chunks):
            came = messages[c]
            if c == 0:
                groups = partner_bands(came, hops - 1)[::-1] + own_band(came, hops)[::-1]
                states[c] = attend(scalars, query_parts, groups, states[c], False, chunk, sizes)
            came = list(tie(came[::-1], [state[1] for state in states]))[::-1]
            rows = behind if hops == last else behind + 2
            sent = [came[1 - slot][:rows] for slot in range(2)]
            following.append(swap_both(sent, hops - 1))
            if c > 0:
                groups = partner_bands(came, hops - 1) + own_band(came, hops)
                states[c] = attend(scalars, query_parts, groups, states[c], False, chunk, sizes)
        messages = following
    ends = []
    for message in messages:
        came = [*tie(message[:1], [state[1] for state in states]), message[1]]
        ends.append(partner_bands(came, last))

    own, returned = [], []
    for c, chunk in enumerate(chunks):
        kept, *parts = attend(scalars, query_parts, ends[c], states[c], True, chunk, sizes)
        own.append((kept, (0, chunk[0] * HEAD_DIM)))
        for offset, x in zip(offsets, parts):
            returned.append((along_space(x, -offset), (offset, chunk[0] * HEAD_DIM)))
    late = len(returned) - len(offsets)
    result = None
    for batch in (own + returned[:late], returned[late:]):
        pieces, places = zip(*batch)
        result = put(pieces, places, result, q.shape, spaces)
    return result.reshape(queries.shape)


def solution(mesh):
    placed = P(("group", "frame"), "space", None, "head")
    return jax.shard_map(
        functools.partial(shards, mesh.shape["space"], mesh.shape["frame"]),
        mesh=mesh,
        in_specs=(placed, placed, placed, P(), P()),
        out_specs=placed,
        check_vma=False,
    )
```

```python
import functools
import math

import jax
import jax.numpy as jnp
from jax import lax
from jax.experimental import pallas as pl
from jax.experimental.pallas import tpu as pltpu
from jax.sharding import PartitionSpec as P

HEAD_DIM = 128
NEG_FILL = -1e30
VMEM_LIMIT = 16 * 1024 * 1024
SMALL_LIMIT = 2 * 1024 * 1024
STAGED_LIMIT = 60 * 1024 * 1024
ROW_GROUPS = 2
NT = (((1,), (1,)), ((), ()))
TN = (((0,), (0,)), ((), ()))


def pack_kernel(spaces, jobs, staged, *refs):
    refs = list(refs)
    halfway = refs[len(refs) - len(jobs) - 1 : -1] if staged else []
    sems = refs[-1]
    here = lax.axis_index("space")
    tokens = refs[0].shape[0]
    groups = ROW_GROUPS if staged else 1
    first_copies, second_copies = [], []
    for n, (source, offset, first, width, target, row) in enumerate(jobs):
        share = refs[source].shape[-1] // spaces
        column = pl.multiple_of(lax.rem(here + offset, spaces) * share + first, HEAD_DIM)
        out = refs[target] if row is None else refs[target].at[row]
        for g in range(groups):
            rows = pl.ds(g * (tokens // groups), tokens // groups)
            origin = refs[source].at[rows, pl.ds(column, width)]
            stop = halfway[n].at[rows] if staged else out.at[rows]
            copy = pltpu.make_async_copy(origin, stop, sems.at[0, n * groups + g])
            copy.start()
            first_copies.append(copy)
            if staged:
                second_copies.append(
                    pltpu.make_async_copy(stop, out.at[rows], sems.at[1, n * groups + g])
                )
    for n, copy in enumerate(first_copies):
        copy.wait()
        if staged:
            second_copies[n].start()
    for copy in second_copies:
        copy.wait()


def pack(sources, blocks, after, spaces, staged):
    tokens = sources[0].shape[0]
    several = len(sources) > 1
    jobs, shapes = [], []
    first_out = len(sources) + len(after)
    for n, (offset, first, width) in enumerate(blocks):
        lead = (len(sources),) if several else ()
        shapes.append(jax.ShapeDtypeStruct(lead + (tokens, width), sources[0].dtype))
        for row in range(len(sources)):
            jobs.append((row, offset, first, width, first_out + n, row if several else None))
    halfway = [pltpu.VMEM((tokens, job[3]), sources[0].dtype) for job in jobs]
    space = pl.ANY if staged else pltpu.VMEM
    return pl.pallas_call(
        functools.partial(pack_kernel, spaces, tuple(jobs), staged),
        in_specs=[pl.BlockSpec(memory_space=pl.ANY)] * first_out,
        out_specs=[pl.BlockSpec(memory_space=space)] * len(shapes),
        out_shape=shapes,
        scratch_shapes=(halfway if staged else [])
        + [pltpu.SemaphoreType.DMA((2, ROW_GROUPS * len(jobs)))],
        compiler_params=pltpu.CompilerParams(
            vmem_limit_bytes=STAGED_LIMIT if staged else SMALL_LIMIT
        ),
        name="pack",
    )(*sources, *after)


def tie(arrays, after):
    return pl.pallas_call(
        lambda *refs: None,
        in_specs=[pl.BlockSpec(memory_space=pl.ANY)] * (len(arrays) + len(after)),
        out_specs=[pl.BlockSpec(memory_space=pl.ANY)] * len(arrays),
        out_shape=[jax.ShapeDtypeStruct(x.shape, x.dtype) for x in arrays],
        input_output_aliases={n: n for n in range(len(arrays))},
        compiler_params=pltpu.CompilerParams(vmem_limit_bytes=SMALL_LIMIT),
        name="tie",
    )(*arrays, *after)


def attend_kernel(
    spaces, frames, columns, row_band, heads, together, groups, query_skip, fresh, final,
    flags_ref, widths_ref, *refs,
):
    refs = list(refs)
    queries = [refs.pop(0) for unused in range(spaces)]
    arrays = 1 + max(piece[0] for group in groups for piece in group[2])
    keyvals = [refs.pop(0) for unused in range(arrays)]
    state_in = None if fresh else (refs.pop(0), refs.pop(0))
    outs = [refs.pop(0) for unused in range(spaces if final else 2)]
    query_ref, key_ref = refs[:2]
    acc_ref, stat_ref = refs[2:] if final else outs
    tokens = queries[0].shape[0]
    frame_now, space_now = lax.axis_index("frame"), lax.axis_index("space")
    scale = math.log2(math.e) / math.sqrt(HEAD_DIM)
    own_column = space_now * (queries[0].shape[-1] // spaces)

    def first_row(offset):
        return lax.rem(space_now - offset + spaces, spaces) * row_band

    def asked_of(group):
        slot, hops = group[:2]
        side = 1 - 2 * lax.rem(frame_now + slot, 2)
        key_frame = frame_now + side * hops
        safe = jnp.clip(key_frame, 0, frames - 1)
        known = (key_frame >= 0) & (key_frame < frames)
        return known & (flags_ref[frame_now, safe] > 0)

    token = lax.broadcasted_iota(jnp.int32, (tokens, HEAD_DIM), 0)
    row = lax.broadcasted_iota(jnp.int32, (tokens, HEAD_DIM), 1)
    starts = [(row - first_row(offset)) * columns for offset in range(spaces)]
    for offset, start in enumerate(starts):
        hit = (token >= start) & (token < start + columns)
        mark = jnp.where(hit, 1.0, 0.0).astype(query_ref.dtype)
        for t in range(together):
            query_ref[t, pl.ds(offset * tokens, tokens), HEAD_DIM:] = mark
    for n, group in enumerate(groups):
        if group[1] > 0:

            @pl.when(asked_of(group))
            def _(n=n, group=group):
                reach = widths_ref[group[1]] * columns
                for m, (unused, unused, offset) in enumerate(group[2]):
                    start = starts[offset]
                    near = (token >= start - reach) & (token < start + columns + reach)
                    fill = jnp.where(near, 0.0, NEG_FILL).astype(key_ref.dtype)
                    for t in range(together):
                        key_ref[n, t, pl.ds(m * tokens, tokens), HEAD_DIM:] = fill

    def attend_heads(turn, carry):
        head = turn * together
        slot_of = (lambda t: t) if final else (lambda t: head + t)

        def lanes(t, skip=0):
            return pl.ds(pl.multiple_of((head + t) * HEAD_DIM + skip, HEAD_DIM), HEAD_DIM)

        def step(t, scores, pieces, old):
            h = slot_of(t)
            top = jnp.max(scores, axis=0, keepdims=True) * scale
            if old:
                before = stat_ref[h, 0:1, :]
                top = jnp.maximum(top, before)
            weights = jnp.exp2(scores * scale - top)
            total = jnp.sum(weights, axis=0, keepdims=True)
            values = jnp.concatenate(
                [keyvals[i][r + 1, :, lanes(t)] for i, r, o in pieces], axis=0
            )
            acc = lax.dot_general(
                values, weights.astype(jnp.bfloat16), TN, preferred_element_type=jnp.float32
            )
            if old:
                fade = jnp.exp2(before - top)
                total = total + stat_ref[h, 1:2, :] * fade
                acc = acc + acc_ref[h] * fade
            stat_ref[h, 0:1, :] = top
            stat_ref[h, 1:2, :] = total
            acc_ref[h] = acc

        for t in range(together):
            for offset in range(spaces):
                skip = query_skip + (own_column if offset == 0 else 0)
                query_ref[t, pl.ds(offset * tokens, tokens), :HEAD_DIM] = queries[offset][
                    :, lanes(t, skip)
                ]
            if not fresh:
                acc_ref[slot_of(t)] = state_in[0][head + t]
                stat_ref[slot_of(t)] = state_in[1][head + t]

        for n, (slot, hops, pieces) in enumerate(groups):
            if hops == 0:
                scores = []
                for t in range(together):
                    keys = jnp.concatenate(
                        [keyvals[i][r, :, lanes(t)] for i, r, o in pieces], axis=0
                    )
                    scores.append(
                        lax.dot_general(
                            keys, query_ref[t, :, :HEAD_DIM], NT,
                            preferred_element_type=jnp.float32,
                        )
                    )
                for t in range(together):
                    step(t, scores[t], pieces, False)
                continue

            @pl.when(asked_of(groups[n]))
            def _(n=n, pieces=pieces):
                many = pl.ds(0, len(pieces) * tokens)
                for t in range(together):
                    for m, (i, r, unused) in enumerate(pieces):
                        key_ref[n, t, pl.ds(m * tokens, tokens), :HEAD_DIM] = keyvals[i][
                            r, :, lanes(t)
                        ]
                scores = [
                    lax.dot_general(
                        key_ref[n, t, many], query_ref[t], NT, preferred_element_type=jnp.float32
                    )
                    for t in range(together)
                ]
                for t in range(together):
                    step(t, scores[t], pieces, True)

        if final:
            for t in range(together):
                result = jnp.transpose(acc_ref[t] * (1.0 / stat_ref[t, 1:2, :]))
                for offset in range(spaces):
                    part = result[offset * tokens : (offset + 1) * tokens]
                    outs[offset][:, lanes(t)] = part.astype(outs[offset].dtype)
        return carry

    lax.fori_loop(0, heads // together, attend_heads, 0)


def attend(scalars, queries, groups, state, final, chunk, sizes):
    spaces, frames, columns, row_band, features = sizes
    first, heads = chunk
    tokens = queries[0].shape[0]
    count = spaces * tokens
    together = next(n for n in (3, 2, 1) if heads % n == 0)
    arrays, numbered = [], []
    for slot, hops, pieces in groups:
        listed = []
        for array, row, offset in pieces:
            known = [n for n, x in enumerate(arrays) if x is array]
            if not known:
                known = [len(arrays)]
                arrays.append(array)
            listed.append((known[0], row, offset))
        numbered.append((slot, hops, tuple(listed)))
    operands = list(queries) + arrays + (list(state) if state is not None else [])
    state_shape = [(heads, HEAD_DIM, count), (heads, 8, count)]
    if final:
        out_shape = [jax.ShapeDtypeStruct((tokens, heads * HEAD_DIM), jnp.bfloat16)] * spaces
    else:
        out_shape = [jax.ShapeDtypeStruct(shape, jnp.float32) for shape in state_shape]
    scratch = [
        pltpu.VMEM((together, count, 2 * HEAD_DIM), jnp.bfloat16),
        pltpu.VMEM((len(groups), together, count, 2 * HEAD_DIM), jnp.bfloat16),
    ]
    if final:
        scratch += [pltpu.VMEM((together,) + shape[1:], jnp.float32) for shape in state_shape]
    pairs = heads * count * tokens * sum(len(pieces) for slot, hops, pieces in groups)
    return pl.pallas_call(
        functools.partial(
            attend_kernel, spaces, frames, columns, row_band, heads, together,
            tuple(numbered), first * HEAD_DIM, state is None, final,
        ),
        in_specs=[pl.BlockSpec(memory_space=pltpu.SMEM)] * 2
        + [pl.BlockSpec(memory_space=pltpu.VMEM)] * len(operands),
        out_specs=[pl.BlockSpec(memory_space=pltpu.VMEM)] * len(out_shape),
        out_shape=out_shape,
        scratch_shapes=scratch,
        compiler_params=pltpu.CompilerParams(vmem_limit_bytes=VMEM_LIMIT),
        cost_estimate=pl.CostEstimate(
            flops=4 * pairs * HEAD_DIM,
            bytes_accessed=8 * count * heads * HEAD_DIM,
            transcendentals=pairs,
        ),
        name="attend_final" if final else "attend",
    )(*scalars, *operands)


def join_kernel(outs_copies, *refs):
    arrays, outs = refs[: -len(outs_copies)], refs[-len(outs_copies) :]
    for out_ref, copies in zip(outs, outs_copies):
        for n, lane, width, row, column in copies:
            rows = pl.ds(row, arrays[n].shape[0])
            out_ref[rows, :, pl.ds(column, width)] = arrays[n][:, :, pl.ds(lane, width)]


def join(arrays, outs_copies, rows, width):
    shape = jax.ShapeDtypeStruct((rows, arrays[0].shape[1], width), arrays[0].dtype)
    return pl.pallas_call(
        functools.partial(join_kernel, outs_copies),
        in_specs=[pl.BlockSpec(memory_space=pltpu.VMEM)] * len(arrays),
        out_specs=[pl.BlockSpec(memory_space=pltpu.VMEM)] * len(outs_copies),
        out_shape=[shape] * len(outs_copies),
        compiler_params=pltpu.CompilerParams(vmem_limit_bytes=SMALL_LIMIT),
        name="join",
    )(*arrays)


def put_kernel(spaces, places, *refs):
    pieces, out_ref, sems = refs[: len(places)], refs[-2], refs[-1]
    share = out_ref.shape[-1] // spaces
    here = lax.axis_index("space")
    copies = []
    for n, (offset, first) in enumerate(places):
        column = pl.multiple_of(lax.rem(here + offset, spaces) * share + first, HEAD_DIM)
        width = pieces[n].shape[-1]
        copy = pltpu.make_async_copy(pieces[n], out_ref.at[:, pl.ds(column, width)], sems.at[n])
        copy.start()
        copies.append(copy)
    for copy in copies:
        copy.wait()


def put(pieces, places, whole, shape, spaces):
    kept = [] if whole is None else [whole]
    return pl.pallas_call(
        functools.partial(put_kernel, spaces, tuple(places)),
        in_specs=[pl.BlockSpec(memory_space=pltpu.VMEM)] * len(pieces)
        + [pl.BlockSpec(memory_space=pl.ANY)] * len(kept),
        out_specs=pl.BlockSpec(memory_space=pl.ANY),
        out_shape=jax.ShapeDtypeStruct(shape, pieces[0].dtype),
        scratch_shapes=[pltpu.SemaphoreType.DMA((len(pieces),))],
        input_output_aliases={len(pieces): 0} if kept else {},
        compiler_params=pltpu.CompilerParams(vmem_limit_bytes=SMALL_LIMIT),
        name="put",
    )(*pieces, *kept)


def shards(spaces, frames, queries, keys, values, flags, widths):
    unused, row_band, columns, features = queries.shape
    tokens = row_band * columns
    width = features // spaces
    heads = width // HEAD_DIM
    scalars = (flags, widths)
    sizes = (spaces, frames, columns, row_band, features)
    q, k, v = (x.reshape(tokens, features) for x in (queries, keys, values))
    half = heads - heads // 2
    chunks = [(0, half), (half, heads - half)]
    offsets = range(1, spaces)

    def along_space(x, offset):
        return lax.ppermute(x, "space", [(s, (s + offset) % spaces) for s in range(spaces)])

    def swap(x, slot, brought=0):
        pairs = []
        for f in range(frames):
            side = 1 if (f + slot) % 2 == 0 else -1
            if 0 <= f + side < frames and 0 <= f - side * brought < frames:
                pairs.append((f, f + side))
        return lax.ppermute(x, "frame", pairs)

    def swap_both(xs, brought=0):
        second = swap(xs[1], 1, brought)
        return [swap(xs[0], 0, brought), second]

    def blocks_of(chunk, which):
        return [(offset, chunk[0] * HEAD_DIM, chunk[1] * HEAD_DIM) for offset in which]

    large = heads - heads // 3
    cuts = [(0, large), (large, heads - large)]
    *sends, source = pack(
        (k, v), blocks_of(chunks[0], offsets) + blocks_of(cuts[0], (0,)), (), spaces, True
    )
    partners = [[along_space(x, offset) for x, offset in zip(sends, offsets)]]
    firsts, own = [swap_both([source, source])], [source]
    *sends, source, rest = pack(
        (k, v),
        blocks_of(chunks[1], offsets) + blocks_of(cuts[1], (0,)) + blocks_of(chunks[1], (0,)),
        partners[0], spaces, False,
    )
    partners.append([along_space(x, offset) for x, offset in zip(sends, offsets)])
    firsts.append(swap_both([source, source]))
    own.append(rest)
    sends = pack((q,), [(offset, 0, width) for offset in offsets], partners[1], spaces, False)
    query_parts = [q] + [along_space(x, offset) for x, offset in zip(sends, offsets)]
    partners[1] = list(tie(partners[1], sends))

    last = frames - 2
    behind = 2 * len(offsets)

    def own_band(message, hops):
        return [(slot, hops, [(x, x.shape[0] - 2, 0)]) for slot, x in enumerate(message)]

    def partner_bands(message, hops):
        return [
            (slot, hops, [(x, 2 * (o - 1), o) for o in offsets]) for slot, x in enumerate(message)
        ]

    seconds, states = [], []
    for c, chunk in enumerate(chunks):
        begin, end = chunk[0], sum(chunk)
        arrays, here = list(partners[c]), []
        for (first, number), pair in zip(cuts, firsts):
            low, high = max(begin, first), min(end, first + number)
            if low < high:
                here.append((len(arrays), low - first, high - low, low - begin))
                arrays += pair
        outs_copies = []
        for slot in range(2):
            copies = [(n, 0, chunk[1] * HEAD_DIM, 2 * n, 0) for n in range(len(offsets))]
            copies += [
                (n + 1 - slot, lane * HEAD_DIM, number * HEAD_DIM, behind, to * HEAD_DIM)
                for n, lane, number, to in here
            ]
            outs_copies.append(tuple(copies))
        ready = join(arrays, tuple(outs_copies), behind + 2, chunk[1] * HEAD_DIM)
        seconds.append(swap_both(ready))
        pieces = [(own[c], 0, 0)] + [(x, 0, o) for x, o in zip(partners[c], offsets)]
        groups = [(0, 0, pieces)] + own_band(ready[::-1], 1)
        states.append(attend(scalars, query_parts, groups, None, False, chunk, sizes))

    messages = seconds
    for hops in range(2, frames - 1):
        following = []
        for c, chunk in enumerate(chunks):
            came = messages[c]
            came = list(tie(came[::-1], [state[1] for state in states]))[::-1]
            rows = behind if hops == last else behind + 2
            sent = [came[1 - slot][:rows] for slot in range(2)]
            following.append(swap_both(sent, hops - 1))
            groups = partner_bands(came, hops - 1) + own_band(came, hops)
            states[c] = attend(scalars, query_parts, groups, states[c], False, chunk, sizes)
        messages = following
    ends = []
    for message in messages:
        came = list(tie(message, [state[1] for state in states]))
        ends.append(partner_bands(came, last))

    own, returned = [], []
    for c, chunk in enumerate(chunks):
        kept, *parts = attend(scalars, query_parts, ends[c], states[c], True, chunk, sizes)
        own.append((kept, (0, chunk[0] * HEAD_DIM)))
        for offset, x in zip(offsets, parts):
            returned.append((along_space(x, -offset), (offset, chunk[0] * HEAD_DIM)))
    late = len(returned) - len(offsets)
    result = None
    for batch in (own + returned[:late], returned[late:]):
        pieces, places = zip(*batch)
        result = put(pieces, places, result, q.shape, spaces)
    return result.reshape(queries.shape)


def solution(mesh):
    placed = P(("group", "frame"), "space", None, "head")
    return jax.shard_map(
        functools.partial(shards, mesh.shape["space"], mesh.shape["frame"]),
        mesh=mesh,
        in_specs=(placed, placed, placed, P(), P()),
        out_specs=placed,
        check_vma=False,
    )
```

```python
import functools
import math

import jax
import jax.numpy as jnp
from jax import lax
from jax.experimental import pallas as pl
from jax.experimental.pallas import tpu as pltpu
from jax.sharding import PartitionSpec as P

HEAD_DIM = 128
NEG_FILL = -1e30
VMEM_LIMIT = 16 * 1024 * 1024
SMALL_LIMIT = 2 * 1024 * 1024
STAGED_LIMIT = 60 * 1024 * 1024
ROW_GROUPS = 2
NT = (((1,), (1,)), ((), ()))
TN = (((0,), (0,)), ((), ()))


def pack_kernel(spaces, jobs, staged, *refs):
    refs = list(refs)
    halfway = refs[len(refs) - len(jobs) - 1 : -1] if staged else []
    sems = refs[-1]
    here = lax.axis_index("space")
    tokens = refs[0].shape[0]
    groups = ROW_GROUPS if staged else 1
    first_copies, second_copies = [], []
    for n, (source, offset, first, width, target, row) in enumerate(jobs):
        share = refs[source].shape[-1] // spaces
        column = pl.multiple_of(lax.rem(here + offset, spaces) * share + first, HEAD_DIM)
        out = refs[target] if row is None else refs[target].at[row]
        for g in range(groups):
            rows = pl.ds(g * (tokens // groups), tokens // groups)
            origin = refs[source].at[rows, pl.ds(column, width)]
            stop = halfway[n].at[rows] if staged else out.at[rows]
            copy = pltpu.make_async_copy(origin, stop, sems.at[0, n * groups + g])
            copy.start()
            first_copies.append(copy)
            if staged:
                second_copies.append(
                    pltpu.make_async_copy(stop, out.at[rows], sems.at[1, n * groups + g])
                )
    for n, copy in enumerate(first_copies):
        copy.wait()
        if staged:
            second_copies[n].start()
    for copy in second_copies:
        copy.wait()


def pack(sources, blocks, after, spaces, staged):
    tokens = sources[0].shape[0]
    several = len(sources) > 1
    jobs, shapes = [], []
    first_out = len(sources) + len(after)
    for n, (offset, first, width) in enumerate(blocks):
        lead = (len(sources),) if several else ()
        shapes.append(jax.ShapeDtypeStruct(lead + (tokens, width), sources[0].dtype))
        for row in range(len(sources)):
            jobs.append((row, offset, first, width, first_out + n, row if several else None))
    halfway = [pltpu.VMEM((tokens, job[3]), sources[0].dtype) for job in jobs]
    space = pl.ANY if staged else pltpu.VMEM
    return pl.pallas_call(
        functools.partial(pack_kernel, spaces, tuple(jobs), staged),
        in_specs=[pl.BlockSpec(memory_space=pl.ANY)] * first_out,
        out_specs=[pl.BlockSpec(memory_space=space)] * len(shapes),
        out_shape=shapes,
        scratch_shapes=(halfway if staged else [])
        + [pltpu.SemaphoreType.DMA((2, ROW_GROUPS * len(jobs)))],
        compiler_params=pltpu.CompilerParams(
            vmem_limit_bytes=STAGED_LIMIT if staged else SMALL_LIMIT
        ),
        name="pack",
    )(*sources, *after)


def tie(arrays, after):
    return pl.pallas_call(
        lambda *refs: None,
        in_specs=[pl.BlockSpec(memory_space=pl.ANY)] * (len(arrays) + len(after)),
        out_specs=[pl.BlockSpec(memory_space=pl.ANY)] * len(arrays),
        out_shape=[jax.ShapeDtypeStruct(x.shape, x.dtype) for x in arrays],
        input_output_aliases={n: n for n in range(len(arrays))},
        compiler_params=pltpu.CompilerParams(vmem_limit_bytes=SMALL_LIMIT),
        name="tie",
    )(*arrays, *after)


def attend_kernel(
    spaces, frames, columns, row_band, heads, together, groups, query_skip, fresh, final,
    flags_ref, widths_ref, *refs,
):
    refs = list(refs)
    queries = [refs.pop(0) for unused in range(spaces)]
    arrays = 1 + max(piece[0] for group in groups for piece in group[2])
    keyvals = [refs.pop(0) for unused in range(arrays)]
    state_in = None if fresh else (refs.pop(0), refs.pop(0))
    outs = [refs.pop(0) for unused in range(spaces if final else 2)]
    query_ref, key_ref = refs[:2]
    acc_ref, stat_ref = refs[2:] if final else outs
    tokens = queries[0].shape[0]
    frame_now, space_now = lax.axis_index("frame"), lax.axis_index("space")
    scale = math.log2(math.e) / math.sqrt(HEAD_DIM)
    own_column = space_now * (queries[0].shape[-1] // spaces)

    def first_row(offset):
        return lax.rem(space_now - offset + spaces, spaces) * row_band

    def asked_of(group):
        slot, hops = group[:2]
        side = 1 - 2 * lax.rem(frame_now + slot, 2)
        key_frame = frame_now + side * hops
        safe = jnp.clip(key_frame, 0, frames - 1)
        known = (key_frame >= 0) & (key_frame < frames)
        return known & (flags_ref[frame_now, safe] > 0)

    token = lax.broadcasted_iota(jnp.int32, (tokens, HEAD_DIM), 0)
    row = lax.broadcasted_iota(jnp.int32, (tokens, HEAD_DIM), 1)
    starts = [(row - first_row(offset)) * columns for offset in range(spaces)]
    for offset, start in enumerate(starts):
        hit = (token >= start) & (token < start + columns)
        mark = jnp.where(hit, 1.0, 0.0).astype(query_ref.dtype)
        for t in range(together):
            query_ref[t, pl.ds(offset * tokens, tokens), HEAD_DIM:] = mark
    for n, group in enumerate(groups):
        if group[1] > 0:

            @pl.when(asked_of(group))
            def _(n=n, group=group):
                reach = widths_ref[group[1]] * columns
                for m, (unused, unused, offset) in enumerate(group[2]):
                    start = starts[offset]
                    near = (token >= start - reach) & (token < start + columns + reach)
                    fill = jnp.where(near, 0.0, NEG_FILL).astype(key_ref.dtype)
                    for t in range(together):
                        key_ref[n, t, pl.ds(m * tokens, tokens), HEAD_DIM:] = fill

    def attend_heads(turn, carry):
        head = turn * together
        slot_of = (lambda t: t) if final else (lambda t: head + t)

        def lanes(t, skip=0):
            return pl.ds(pl.multiple_of((head + t) * HEAD_DIM + skip, HEAD_DIM), HEAD_DIM)

        def step(t, scores, pieces, old):
            h = slot_of(t)
            top = jnp.max(scores, axis=0, keepdims=True) * scale
            if old:
                before = stat_ref[h, 0:1, :]
                top = jnp.maximum(top, before)
            weights = jnp.exp2(scores * scale - top)
            total = jnp.sum(weights, axis=0, keepdims=True)
            values = jnp.concatenate(
                [keyvals[i][r + 1, :, lanes(t)] for i, r, o in pieces], axis=0
            )
            acc = lax.dot_general(
                values, weights.astype(jnp.bfloat16), TN, preferred_element_type=jnp.float32
            )
            if old:
                fade = jnp.exp2(before - top)
                total = total + stat_ref[h, 1:2, :] * fade
                acc = acc + acc_ref[h] * fade
            stat_ref[h, 0:1, :] = top
            stat_ref[h, 1:2, :] = total
            acc_ref[h] = acc

        for t in range(together):
            for offset in range(spaces):
                skip = query_skip + (own_column if offset == 0 else 0)
                query_ref[t, pl.ds(offset * tokens, tokens), :HEAD_DIM] = queries[offset][
                    :, lanes(t, skip)
                ]
            if not fresh:
                acc_ref[slot_of(t)] = state_in[0][head + t]
                stat_ref[slot_of(t)] = state_in[1][head + t]

        for n, (slot, hops, pieces) in enumerate(groups):
            if hops == 0:
                scores = []
                for t in range(together):
                    keys = jnp.concatenate(
                        [keyvals[i][r, :, lanes(t)] for i, r, o in pieces], axis=0
                    )
                    scores.append(
                        lax.dot_general(
                            keys, query_ref[t, :, :HEAD_DIM], NT,
                            preferred_element_type=jnp.float32,
                        )
                    )
                for t in range(together):
                    step(t, scores[t], pieces, False)
                continue

            @pl.when(asked_of(groups[n]))
            def _(n=n, pieces=pieces):
                many = pl.ds(0, len(pieces) * tokens)
                for t in range(together):
                    for m, (i, r, unused) in enumerate(pieces):
                        key_ref[n, t, pl.ds(m * tokens, tokens), :HEAD_DIM] = keyvals[i][
                            r, :, lanes(t)
                        ]
                scores = [
                    lax.dot_general(
                        key_ref[n, t, many], query_ref[t], NT, preferred_element_type=jnp.float32
                    )
                    for t in range(together)
                ]
                for t in range(together):
                    step(t, scores[t], pieces, True)

        if final:
            for t in range(together):
                result = jnp.transpose(acc_ref[t] * (1.0 / stat_ref[t, 1:2, :]))
                for offset in range(spaces):
                    part = result[offset * tokens : (offset + 1) * tokens]
                    outs[offset][:, lanes(t)] = part.astype(outs[offset].dtype)
        return carry

    lax.fori_loop(0, heads // together, attend_heads, 0)


def attend(scalars, queries, groups, state, final, chunk, sizes):
    spaces, frames, columns, row_band, features = sizes
    first, heads = chunk
    tokens = queries[0].shape[0]
    count = spaces * tokens
    together = next(n for n in (3, 2, 1) if heads % n == 0)
    arrays, numbered = [], []
    for slot, hops, pieces in groups:
        listed = []
        for array, row, offset in pieces:
            known = [n for n, x in enumerate(arrays) if x is array]
            if not known:
                known = [len(arrays)]
                arrays.append(array)
            listed.append((known[0], row, offset))
        numbered.append((slot, hops, tuple(listed)))
    operands = list(queries) + arrays + (list(state) if state is not None else [])
    state_shape = [(heads, HEAD_DIM, count), (heads, 8, count)]
    if final:
        out_shape = [jax.ShapeDtypeStruct((tokens, heads * HEAD_DIM), jnp.bfloat16)] * spaces
    else:
        out_shape = [jax.ShapeDtypeStruct(shape, jnp.float32) for shape in state_shape]
    scratch = [
        pltpu.VMEM((together, count, 2 * HEAD_DIM), jnp.bfloat16),
        pltpu.VMEM((len(groups), together, count, 2 * HEAD_DIM), jnp.bfloat16),
    ]
    if final:
        scratch += [pltpu.VMEM((together,) + shape[1:], jnp.float32) for shape in state_shape]
    pairs = heads * count * tokens * sum(len(pieces) for slot, hops, pieces in groups)
    return pl.pallas_call(
        functools.partial(
            attend_kernel, spaces, frames, columns, row_band, heads, together,
            tuple(numbered), first * HEAD_DIM, state is None, final,
        ),
        in_specs=[pl.BlockSpec(memory_space=pltpu.SMEM)] * 2
        + [pl.BlockSpec(memory_space=pltpu.VMEM)] * len(operands),
        out_specs=[pl.BlockSpec(memory_space=pltpu.VMEM)] * len(out_shape),
        out_shape=out_shape,
        scratch_shapes=scratch,
        compiler_params=pltpu.CompilerParams(vmem_limit_bytes=VMEM_LIMIT),
        cost_estimate=pl.CostEstimate(
            flops=4 * pairs * HEAD_DIM,
            bytes_accessed=8 * count * heads * HEAD_DIM,
            transcendentals=pairs,
        ),
        name="attend_final" if final else "attend",
    )(*scalars, *operands)


def join_kernel(outs_copies, *refs):
    arrays, outs = refs[: -len(outs_copies)], refs[-len(outs_copies) :]
    for out_ref, copies in zip(outs, outs_copies):
        for n, lane, width, row, column in copies:
            rows = pl.ds(row, arrays[n].shape[0])
            out_ref[rows, :, pl.ds(column, width)] = arrays[n][:, :, pl.ds(lane, width)]


def join(arrays, outs_copies, rows, width):
    shape = jax.ShapeDtypeStruct((rows, arrays[0].shape[1], width), arrays[0].dtype)
    return pl.pallas_call(
        functools.partial(join_kernel, outs_copies),
        in_specs=[pl.BlockSpec(memory_space=pltpu.VMEM)] * len(arrays),
        out_specs=[pl.BlockSpec(memory_space=pltpu.VMEM)] * len(outs_copies),
        out_shape=[shape] * len(outs_copies),
        compiler_params=pltpu.CompilerParams(vmem_limit_bytes=SMALL_LIMIT),
        name="join",
    )(*arrays)


def put_kernel(spaces, places, *refs):
    pieces, out_ref, sems = refs[: len(places)], refs[-2], refs[-1]
    share = out_ref.shape[-1] // spaces
    here = lax.axis_index("space")
    copies = []
    for n, (offset, first) in enumerate(places):
        column = pl.multiple_of(lax.rem(here + offset, spaces) * share + first, HEAD_DIM)
        width = pieces[n].shape[-1]
        copy = pltpu.make_async_copy(pieces[n], out_ref.at[:, pl.ds(column, width)], sems.at[n])
        copy.start()
        copies.append(copy)
    for copy in copies:
        copy.wait()


def put(pieces, places, whole, shape, spaces):
    kept = [] if whole is None else [whole]
    return pl.pallas_call(
        functools.partial(put_kernel, spaces, tuple(places)),
        in_specs=[pl.BlockSpec(memory_space=pltpu.VMEM)] * len(pieces)
        + [pl.BlockSpec(memory_space=pl.ANY)] * len(kept),
        out_specs=pl.BlockSpec(memory_space=pl.ANY),
        out_shape=jax.ShapeDtypeStruct(shape, pieces[0].dtype),
        scratch_shapes=[pltpu.SemaphoreType.DMA((len(pieces),))],
        input_output_aliases={len(pieces): 0} if kept else {},
        compiler_params=pltpu.CompilerParams(vmem_limit_bytes=SMALL_LIMIT),
        name="put",
    )(*pieces, *kept)


def shards(spaces, frames, queries, keys, values, flags, widths):
    unused, row_band, columns, features = queries.shape
    tokens = row_band * columns
    width = features // spaces
    heads = width // HEAD_DIM
    scalars = (flags, widths)
    sizes = (spaces, frames, columns, row_band, features)
    q, k, v = (x.reshape(tokens, features) for x in (queries, keys, values))
    half = heads - heads // 2
    chunks = [(0, half), (half, heads - half)]
    offsets = range(1, spaces)

    def along_space(x, offset):
        return lax.ppermute(x, "space", [(s, (s + offset) % spaces) for s in range(spaces)])

    def swap(x, slot, brought=0):
        pairs = []
        for f in range(frames):
            side = 1 if (f + slot) % 2 == 0 else -1
            if 0 <= f + side < frames and 0 <= f - side * brought < frames:
                pairs.append((f, f + side))
        return lax.ppermute(x, "frame", pairs)

    def swap_both(xs, brought=0):
        second = swap(xs[1], 1, brought)
        return [swap(xs[0], 0, brought), second]

    def blocks_of(chunk, which):
        return [(offset, chunk[0] * HEAD_DIM, chunk[1] * HEAD_DIM) for offset in which]

    large = heads - heads // 3
    cuts = [(0, large), (large, heads - large)]
    *sends, source = pack(
        (k, v), blocks_of(chunks[0], offsets) + blocks_of(cuts[0], (0,)), (), spaces, True
    )
    partners = [[along_space(x, offset) for x, offset in zip(sends, offsets)]]
    firsts, own = [swap_both([source, source])], [source]
    *sends, source, rest = pack(
        (k, v),
        blocks_of(chunks[1], offsets) + blocks_of(cuts[1], (0,)) + blocks_of(chunks[1], (0,)),
        partners[0], spaces, False,
    )
    partners.append([along_space(x, offset) for x, offset in zip(sends, offsets)])
    firsts.append(swap_both([source, source]))
    own.append(rest)
    sends = pack((q,), [(offset, 0, width) for offset in offsets], partners[1], spaces, False)
    query_parts = [q] + [along_space(x, offset) for x, offset in zip(sends, offsets)]
    partners[1] = list(tie(partners[1], sends))

    last = frames - 2
    behind = 2 * len(offsets)

    def own_band(message, hops):
        return [(slot, hops, [(x, x.shape[0] - 2, 0)]) for slot, x in enumerate(message)]

    def partner_bands(message, hops):
        return [
            (slot, hops, [(x, 2 * (o - 1), o) for o in offsets]) for slot, x in enumerate(message)
        ]

    seconds, states = [], []
    for c, chunk in enumerate(chunks):
        begin, end = chunk[0], sum(chunk)
        arrays, here = list(partners[c]), []
        for (first, number), pair in zip(cuts, firsts):
            low, high = max(begin, first), min(end, first + number)
            if low < high:
                here.append((len(arrays), low - first, high - low, low - begin))
                arrays += pair
        outs_copies = []
        for slot in range(2):
            copies = [(n, 0, chunk[1] * HEAD_DIM, 2 * n, 0) for n in range(len(offsets))]
            copies += [
                (n + 1 - slot, lane * HEAD_DIM, number * HEAD_DIM, behind, to * HEAD_DIM)
                for n, lane, number, to in here
            ]
            outs_copies.append(tuple(copies))
        ready = join(arrays, tuple(outs_copies), behind + 2, chunk[1] * HEAD_DIM)
        seconds.append(swap_both(ready))
        pieces = [(own[c], 0, 0)] + [(x, 0, o) for x, o in zip(partners[c], offsets)]
        groups = [(0, 0, pieces)] + own_band(ready[::-1], 1)
        states.append(attend(scalars, query_parts, groups, None, False, chunk, sizes))

    messages = seconds
    for hops in range(2, frames - 1):
        following = []
        for c, chunk in enumerate(chunks):
            came = messages[c]
            came = list(tie(came[::-1], [state[1] for state in states]))[::-1]
            rows = behind if hops == last else behind + 2
            sent = [came[1 - slot][:rows] for slot in range(2)]
            following.append(swap_both(sent, hops - 1))
            groups = partner_bands(came, hops - 1) + own_band(came, hops)
            states[c] = attend(scalars, query_parts, groups, states[c], False, chunk, sizes)
        messages = following
    ends = []
    for c, message in enumerate(messages):
        turn = -1 if c == 0 else 1
        came = list(tie(message[::turn], [state[1] for state in states]))[::turn]
        ends.append(partner_bands(came, last))

    own, returned = [], []
    for c, chunk in enumerate(chunks):
        kept, *parts = attend(scalars, query_parts, ends[c], states[c], True, chunk, sizes)
        own.append((kept, (0, chunk[0] * HEAD_DIM)))
        for offset, x in zip(offsets, parts):
            returned.append((along_space(x, -offset), (offset, chunk[0] * HEAD_DIM)))
    late = len(returned) - len(offsets)
    result = None
    for batch in (own + returned[:late], returned[late:]):
        pieces, places = zip(*batch)
        result = put(pieces, places, result, q.shape, spaces)
    return result.reshape(queries.shape)


def solution(mesh):
    placed = P(("group", "frame"), "space", None, "head")
    return jax.shard_map(
        functools.partial(shards, mesh.shape["space"], mesh.shape["frame"]),
        mesh=mesh,
        in_specs=(placed, placed, placed, P(), P()),
        out_specs=placed,
        check_vma=False,
    )
```
